256 devices in a mesh: gx: 4 (over y), gy: 8 (over x, z_hi), gz: 8 (over z_lo, core).
Axes of the slice: x: 4, y: 4, z: 8 (z_hi: 2, z_lo: 4; z = z_hi * 4 + z_lo), core: 2. Of those that a mesh axis runs over, the one named last changes fastest.
Arguments:
- charges: float32 [262144], P(('gx', 'gy', 'gz')), may hold values from -6 to 6
- mesh_start: int32 [3, 262144], P(None, ('gx', 'gy', 'gz')), may hold values from 0 to 319, as said below
- mesh_frac: float32 [3, 262144], P(None, ('gx', 'gy', 'gz')), may hold values from 0 to 1
- influence: float32 [320, 320, 320], P(('gx', 'gz'), 'gy'), may hold values from 4 to 400, as said below
Outputs:
- potential: float32 [262144], P(('gx', 'gy', 'gz'))
- forces: float32 [3, 262144], P(None, ('gx', 'gy', 'gz'))
The draws below stay inside these ranges and needn't reach their ends.
Inputs may be any that keep to these rules, and one draw needn't show every extreme that they name: `mesh_start`: A device at position p along gx+gz (joined in that order) and position q along gy holds sites whose start along x lies in p * 10 to p * 10 + 9 and whose start along y lies in q * 40 to q * 40 + 39; starts along z take any value. influence[kz, kx, ky] equals influence[(-kz) mod 320, (-kx) mod 320, (-ky) mod 320].
All inputs are finite; a program needn't handle non-finite values.
Results may differ from the reference program's by a relative error of at most 0.00017.
Values sent between devices are 32-bit elements; how exact they have to be, the bound alone decides.
No kernel may reach another device: no remote copies, remote signals or barrier semaphores. Data moves between devices by JAX's collectives and lax.ppermute only.
A program may use at most 128 MiB of HBM per device.

```python
import jax
import jax.numpy as jnp

M = 320
SITES_DEV = 1024
SITES = 262144
PX = 10
PY = 40
N_GY = 8
N_GZ = 8


def draw_mesh_start(key, part):
    key = jax.random.fold_in(key, 11)
    key_x, key_y, key_z = jax.random.split(key, 3)
    owner_block = jnp.arange(SITES, dtype=jnp.int32) // SITES_DEV
    row_index = owner_block // (N_GY * N_GZ)
    column_index = owner_block // N_GZ % N_GY
    slab_index = owner_block % N_GZ
    pencil_index = row_index * N_GZ + slab_index
    start_x = pencil_index * PX + jax.random.randint(key_x, (SITES,), 0, PX, dtype=jnp.int32)
    start_y = column_index * PY + jax.random.randint(key_y, (SITES,), 0, PY, dtype=jnp.int32)
    start_z = jax.random.randint(key_z, (SITES,), 0, M, dtype=jnp.int32)
    return jnp.stack([start_x, start_y, start_z]).astype(jnp.int32)


def draw_influence(key, part):
    key = jax.random.fold_in(key, 7)
    level = jax.random.uniform(key, (M, M, M), jnp.float32, jnp.log(4.0), jnp.log(400.0))
    base = jnp.exp(level)
    mirrored = jnp.roll(jnp.flip(base, (0, 1, 2)), 1, (0, 1, 2))
    return jnp.clip(0.5 * (base + mirrored), 4.0, 400.0).astype(jnp.float32)


def shard_levels(rng, dims, shards, smallest, high):
    def one(position, shards_of):
        draws = jax.random.uniform(jax.random.fold_in(jax.random.fold_in(rng, 6), position), (shards_of,), jnp.float32, smallest / len(shards), high / len(shards))
        return jnp.repeat(jnp.exp(draws), dims[position] // shards_of).reshape((-1,) + (1,) * (len(dims) - position - 1))

    level = one(*shards[0])
    for cut in shards[1:]:
        level = level * one(*cut)
    return level


def scatter_about(key, shape, spread, reach, cuts=(), held_as=jnp.bfloat16):
    drawn = jax.random.normal(key, shape, jnp.float32) * spread
    if len(cuts) > 0:
        drawn = shard_levels(key, shape, cuts, -0.22, 0.18) * drawn
    return jnp.clip(drawn, min=-reach, max=reach).astype(held_as)


def setup_inputs(seed: int = 0) -> dict:
    key_of = jax.random.split(jax.random.key(seed), 5)
    return {
        "charges": scatter_about(key_of[0], (SITES,), 1.0, 6.0, ((0, 256),), jnp.float32),
        "mesh_start": draw_mesh_start(jax.random.fold_in(key_of[4], 71), 0),
        "mesh_frac": jnp.clip(1.0 * jax.random.uniform(key_of[2], (3, SITES), jnp.float32) ** shard_levels(key_of[2], (3, SITES), ((1, 256),), -0.2, 0.2), 0.0, 1.0),
        "influence": draw_influence(jax.random.fold_in(key_of[4], 71), 0),
    }


def spline_weights(fraction):
    values = [1.0 - fraction, fraction] + [jnp.zeros_like(fraction) for unused in range(4)]
    for order in range(3, 6):
        factor = 1.0 / (order - 1)
        values[order - 1] = factor * fraction * values[order - 2]
        for offset in range(1, order - 1):
            values[order - offset - 1] = factor * ((fraction + offset) * values[order - offset - 2] + (order - offset - fraction) * values[order - offset - 1])
        values[0] = factor * (1.0 - fraction) * values[0]
    slopes = [-values[0]] + [values[offset - 1] - values[offset] for offset in range(1, 6)]
    factor = 1.0 / 5.0
    values[5] = factor * fraction * values[4]
    for offset in range(1, 5):
        values[5 - offset] = factor * ((fraction + offset) * values[4 - offset] + (6 - offset - fraction) * values[5 - offset])
    values[0] = factor * (1.0 - fraction) * values[0]
    return values, slopes


def reference(charges, mesh_start, mesh_frac, influence):
    values, slopes = spline_weights(mesh_frac)
    extent = M
    mesh_flat = jnp.zeros((extent * extent * extent,), charges.dtype)
    for along_x in range(6):
        indices = []
        amounts = []
        for along_y in range(6):
            for along_z in range(6):
                linear = ((mesh_start[0] + along_x) % extent) * extent * extent + ((mesh_start[1] + along_y) % extent) * extent + (mesh_start[2] + along_z) % extent
                indices.append(linear.astype(jnp.int32))
                amounts.append(charges * values[along_x][0] * values[along_y][1] * values[along_z][2])
        mesh_flat = mesh_flat.at[jnp.concatenate(indices)].add(jnp.concatenate(amounts))
    charge_mesh = mesh_flat.reshape(extent, extent, extent)
    spectrum = jnp.fft.fftn(charge_mesh) * jnp.transpose(influence, (1, 2, 0))
    mesh_potential = jnp.real(jnp.fft.ifftn(spectrum)).astype(charges.dtype).reshape(-1)
    potential = jnp.zeros_like(charges)
    grad_x = jnp.zeros_like(charges)
    grad_y = jnp.zeros_like(charges)
    grad_z = jnp.zeros_like(charges)
    for along_x in range(6):
        for along_y in range(6):
            for along_z in range(6):
                linear = ((mesh_start[0] + along_x) % extent) * extent * extent + ((mesh_start[1] + along_y) % extent) * extent + (mesh_start[2] + along_z) % extent
                cell_value = mesh_potential[linear.astype(jnp.int32)]
                weight_x = values[along_x][0]
                weight_y = values[along_y][1]
                weight_z = values[along_z][2]
                potential = potential + weight_x * weight_y * weight_z * cell_value
                grad_x = grad_x + slopes[along_x][0] * weight_y * weight_z * cell_value
                grad_y = grad_y + weight_x * slopes[along_y][1] * weight_z * cell_value
                grad_z = grad_z + weight_x * weight_y * slopes[along_z][2] * cell_value
    forces = jnp.stack([-charges * grad_x, -charges * grad_y, -charges * grad_z])
    return potential, forces
```

```python
import functools
import math

import jax
import jax.numpy as jnp
import ml_dtypes
import numpy as np
from jax import lax
from jax.experimental import pallas as pl
from jax.experimental.pallas import tpu as pltpu
from jax.sharding import PartitionSpec as P

M = 320
PX = 10
PY = 40
GX, GY, GZ = 4, 8, 8
PENCILS = GX * GZ
SLOTS = 6
CHUNK = 12
ROWS = GX * GY * GZ * CHUNK
WIDE_X = 15
GROUPS_Y = 6
STEP_Y = 8
LANES = 128
BF16 = jnp.bfloat16
F32 = jnp.float32
NT = (((1,), (1,)), ((), ()))


def halves(table):
    high = table.astype(ml_dtypes.bfloat16)
    low = (table - high.astype(np.float64)).astype(ml_dtypes.bfloat16)
    return high, low


def left_table(table):
    high, low = halves(table)
    return np.concatenate([high, high, low], axis=1)


def right_table(table):
    high, low = halves(table)
    return np.concatenate([high, high, low], axis=0)


def angles(rows, columns, period):
    phase = np.mod(np.outer(rows, columns), period)
    return phase * (2.0 * math.pi / period)


def complex_left(angle):
    c, s = np.cos(angle), np.sin(angle)
    return np.block([[c, s], [-s, c]])


def lane_table(outer, inner, period, inner_first):
    c = np.cos(angles(np.arange(inner[0]), np.arange(inner[1]), period))
    s = np.sin(angles(np.arange(inner[0]), np.arange(inner[1]), period))
    eye = np.eye(outer)
    if inner_first:
        c, s = np.kron(c, eye), np.kron(s, eye)
    else:
        c, s = np.kron(eye, c), np.kron(eye, s)
    pad = [(0, LANES - c.shape[0]), (0, LANES - c.shape[1])]
    c, s = np.pad(c, pad), np.pad(s, pad)
    return np.block([[c, -s], [s, c]])


def wave_slots():
    waves = np.zeros((GX, SLOTS, GZ), np.int64)
    fold = np.zeros((GX, SLOTS, GZ))
    for gx in range(GX):
        for gz in range(GZ):
            p = gx * GZ + gz
            first = 10 * p + (0 if p < PENCILS // 2 else 1)
            for j in range(5):
                waves[gx, j, gz] = first + j
                fold[gx, j, gz] = 1.0 if first + j == 0 else 2.0
            if p == PENCILS // 2:
                waves[gx, 5, gz] = M // 2
                fold[gx, 5, gz] = 1.0
    return waves.reshape(-1), fold.reshape(-1)


@functools.lru_cache(maxsize=None)
def tables():
    waves, fold = wave_slots()
    angle = angles(waves, np.arange(M), M)
    live = (fold > 0)[:, None]
    front = np.concatenate([np.cos(angle) * live, -np.sin(angle) * live])
    scale = fold[:, None] / float(M * M * M)
    back = np.concatenate([np.cos(angle) * scale, -np.sin(angle) * scale]).T
    back = np.pad(back, [(0, 384 - M), (0, 0)])
    left_x = complex_left(angles(np.arange(32), np.arange(32), 32))
    left_y = complex_left(angles(np.arange(40), np.arange(40), 40))
    lanes_x = lane_table(STEP_Y, (WIDE_X, 10), 10, True)
    lanes_y = lane_table(10, (STEP_Y, 8), 8, False)
    lane = np.arange(LANES)
    turn_x = angles(np.arange(32), np.where(lane < 120, lane // 8, 0), M)
    turn_y = angles(np.arange(40), lane % 8, M)
    return dict(
        front=left_table(front),
        back=left_table(back),
        left_x=left_table(left_x),
        left_y=left_table(left_y),
        left_xh=left_table(left_x.T),
        left_yh=left_table(left_y.T),
        lanes_x=right_table(lanes_x),
        lanes_y=right_table(lanes_y),
        lanes_xh=right_table(lanes_x.T),
        lanes_yh=right_table(lanes_y.T),
        turn_x=np.stack([np.cos(turn_x), -np.sin(turn_x)]).astype(np.float32),
        turn_y=np.stack([np.cos(turn_y), -np.sin(turn_y)]).astype(np.float32),
    )


def split(value):
    high = value.astype(BF16)
    low = (value - high.astype(F32)).astype(BF16)
    return high, low


def split_rows(value):
    high, low = split(value)
    return jnp.concatenate([high, low, high], axis=0)


def split_lanes(value):
    high, low = split(value)
    return jnp.concatenate([high, low, high], axis=1)


def dot(left, right):
    return jnp.dot(left, right, preferred_element_type=F32)


def spline_weights(fraction):
    values = [1.0 - fraction, fraction] + [jnp.zeros_like(fraction) for unused in range(4)]
    for order in range(3, 6):
        factor = 1.0 / (order - 1)
        values[order - 1] = factor * fraction * values[order - 2]
        for offset in range(1, order - 1):
            values[order - offset - 1] = factor * (
                (fraction + offset) * values[order - offset - 2]
                + (order - offset - fraction) * values[order - offset - 1]
            )
        values[0] = factor * (1.0 - fraction) * values[0]
    slopes = [-values[0]] + [values[offset - 1] - values[offset] for offset in range(1, 6)]
    factor = 1.0 / 5.0
    values[5] = factor * fraction * values[4]
    for offset in range(1, 5):
        values[5 - offset] = factor * (
            (fraction + offset) * values[4 - offset] + (6 - offset - fraction) * values[5 - offset]
        )
    values[0] = factor * (1.0 - fraction) * values[0]
    return values, slopes


def place(coefficients, dimension, offset):
    result = jnp.zeros(offset.shape, F32)
    for j in range(6):
        result = jnp.where(offset == j, coefficients[j][dimension : dimension + 1], result)
    return result


def rows_below(start, length):
    return lax.broadcasted_iota(jnp.int32, (length, start.shape[1]), 0) - start


def z_offset(start, first, length):
    offset = rows_below(start, length) + first
    return jnp.where(offset < 0, offset + M, offset)


def spread_kernel(charge_ref, start_ref, frac_ref, front_ref, out_ref, wz_ref, plane_ref):
    sites = charge_ref.shape[1]
    values, unused = spline_weights(frac_ref[...])
    weight_x = place(values, 0, rows_below(lax.rem(start_ref[0:1], PX), 16)) * charge_ref[...]
    weight_y = place(values, 1, rows_below(lax.rem(start_ref[1:2], PY), GROUPS_Y * STEP_Y))
    start_z = start_ref[2:3]
    for block in range(0, M, 16):
        high, low = split(place(values, 2, z_offset(start_z, block, 16)))
        wz_ref[0, block : block + 16] = high
        wz_ref[1, block : block + 16] = low
    for g in range(GROUPS_Y):
        near = weight_y[g * STEP_Y : (g + 1) * STEP_Y]
        for x in range(0, 16, 2):
            pair = [near * jnp.broadcast_to(weight_x[x + i : x + i + 1], near.shape) for i in range(2)]
            high, low = split(jnp.concatenate(pair, axis=0))
            plane_ref[0, g * LANES + x * 8 : g * LANES + x * 8 + 16] = high
            plane_ref[1, g * LANES + x * 8 : g * LANES + x * 8 + 16] = low
    mesh = lax.dot_general(wz_ref[0], plane_ref[0], NT, preferred_element_type=F32)
    mesh = mesh + lax.dot_general(wz_ref[0], plane_ref[1], NT, preferred_element_type=F32)
    mesh = mesh + lax.dot_general(wz_ref[1], plane_ref[0], NT, preferred_element_type=F32)
    waves = dot(front_ref[...], split_rows(mesh))
    span = SLOTS * GZ
    for gx in range(GX):
        first = gx * GY * GZ * CHUNK
        for part in range(2):
            rows = waves[(part * GX + gx) * span : (part * GX + gx + 1) * span]
            for g in range(GROUPS_Y):
                out_ref[pl.ds(first + part * GROUPS_Y + g, span, stride=CHUNK), :] = rows[
                    :, g * LANES : (g + 1) * LANES
                ]
        out_ref[first + span * CHUNK : first + GY * GZ * CHUNK] = jnp.zeros(((GY * GZ - span) * CHUNK, LANES), F32)


def turn(real, imag, cos, sin):
    return real * cos - imag * sin, real * sin + imag * cos


def plane_kernel(
    in_ref,
    influence_ref,
    left_x_ref,
    left_y_ref,
    left_xh_ref,
    left_yh_ref,
    lanes_x_ref,
    lanes_y_ref,
    lanes_xh_ref,
    lanes_yh_ref,
    turn_x_ref,
    turn_y_ref,
    out_ref,
    real_ref,
    imag_ref,
):
    cos_x, sin_x = turn_x_ref[0], turn_x_ref[1]
    cos_y, sin_y = turn_y_ref[0], turn_y_ref[1]

    def lane(value, k):
        return value[:, k * LANES : (k + 1) * LANES]

    def chunk_rows(gx, q, part, g):
        return pl.ds((gx * GY + q) * GZ * CHUNK + part * GROUPS_Y + g, GZ, stride=CHUNK)

    spill = None
    for q in range(GY):
        rows = [
            jnp.concatenate([in_ref[chunk_rows(gx, q, part, g), :] for g in range(GROUPS_Y)], axis=1)
            for part in range(2)
            for gx in range(GX)
        ]
        mixed = dot(left_x_ref[...], split_rows(jnp.concatenate(rows, axis=0)))
        turned = [
            jnp.concatenate(turn(lane(mixed[:32], g), lane(mixed[32:], g), cos_x, sin_x), axis=1)
            for g in range(GROUPS_Y)
        ]
        done = dot(split_lanes(jnp.concatenate(turned, axis=0)), lanes_x_ref[...])
        first = q * 5 * 32
        head = done[:32] if spill is None else done[:32] + spill
        real_ref[first : first + 32] = lane(head, 0)
        imag_ref[first : first + 32] = lane(head, 1)
        real_ref[first + 32 : first + 160] = lane(done[32:160], 0)
        imag_ref[first + 32 : first + 160] = lane(done[32:160], 1)
        spill = done[160:192]
    real_ref[0:32] += lane(spill, 0)
    imag_ref[0:32] += lane(spill, 1)

    batch = 4
    for k in range(0, 32, batch):
        picks = [pl.ds(k + i, 40, stride=32) for i in range(batch)]
        real = jnp.concatenate([real_ref[pick, :] for pick in picks], axis=1)
        imag = jnp.concatenate([imag_ref[pick, :] for pick in picks], axis=1)
        mixed = dot(left_y_ref[...], split_rows(jnp.concatenate([real, imag], axis=0)))
        turned = [
            jnp.concatenate(turn(lane(mixed[:40], i), lane(mixed[40:], i), cos_y, sin_y), axis=1)
            for i in range(batch)
        ]
        spectrum = dot(split_lanes(jnp.concatenate(turned, axis=0)), lanes_y_ref[...])
        influence = influence_ref[k * 40 : (k + batch) * 40]
        spectrum = spectrum * jnp.concatenate([influence, influence], axis=1)
        back = dot(split_lanes(spectrum), lanes_yh_ref[...])
        pieces = [
            turn(lane(back[i * 40 : (i + 1) * 40], 0), lane(back[i * 40 : (i + 1) * 40], 1), cos_y, -sin_y)
            for i in range(batch)
        ]
        stacked = jnp.concatenate(
            [jnp.concatenate([piece[part] for piece in pieces], axis=1) for part in range(2)], axis=0
        )
        inverse = dot(left_yh_ref[...], split_rows(stacked))
        for i in range(batch):
            real_ref[picks[i], :] = lane(inverse[:40], i)
            imag_ref[picks[i], :] = lane(inverse[40:], i)

    for q in range(GY):
        first = q * 5 * 32
        rows = jnp.concatenate([real_ref[first : first + 160], imag_ref[first : first + 160]], axis=1)
        back = dot(split_lanes(rows), lanes_xh_ref[...])
        pieces = [
            turn(lane(back[g * 32 : (g + 1) * 32], 0), lane(back[g * 32 : (g + 1) * 32], 1), cos_x, -sin_x)
            for g in range(5)
        ]
        stacked = jnp.concatenate(
            [jnp.concatenate([piece[part] for piece in pieces], axis=1) for part in range(2)], axis=0
        )
        inverse = dot(left_xh_ref[...], split_rows(stacked))
        for part in range(2):
            for gx in range(GX):
                tile = inverse[(part * GX + gx) * GZ : (part * GX + gx + 1) * GZ]
                for g in range(5):
                    out_ref[chunk_rows(gx, q, part, g), :] = lane(tile, g)
                out_ref[chunk_rows(gx, (q + GY - 1) % GY, part, 5), :] = lane(tile, 0)


def gather_kernel(in_ref, charge_ref, start_ref, frac_ref, back_ref, potential_ref, forces_ref, wz_ref, mesh_ref):
    sites = charge_ref.shape[1]
    values, slopes = spline_weights(frac_ref[...])
    offset_x = rows_below(lax.rem(start_ref[0:1], PX), 16)
    offset_y = rows_below(lax.rem(start_ref[1:2], PY), GROUPS_Y * STEP_Y)
    weight_x, slope_x = place(values, 0, offset_x), place(slopes, 0, offset_x)
    weight_y, slope_y = place(values, 1, offset_y), place(slopes, 1, offset_y)
    start_z = start_ref[2:3]
    for block in range(0, 384, 16):
        if block < M:
            offset = z_offset(start_z, block, 16)
            pairs = [split(place(values, 2, offset)), split(place(slopes, 2, offset))]
        else:
            nothing = jnp.zeros((16, sites), BF16)
            pairs = [(nothing, nothing)] * 2
        for kind in range(2):
            wz_ref[kind, block : block + 16] = pairs[kind][0]
            wz_ref[kind, 384 + block : 384 + block + 16] = pairs[kind][0]
            wz_ref[kind, 768 + block : 768 + block + 16] = pairs[kind][1]
    span = SLOTS * GZ
    rows = [
        jnp.concatenate(
            [
                in_ref[pl.ds(gx * GY * GZ * CHUNK + part * GROUPS_Y + g, span, stride=CHUNK), :]
                for g in range(GROUPS_Y)
            ],
            axis=1,
        )
        for part in range(2)
        for gx in range(GX)
    ]
    mesh = dot(back_ref[...], split_rows(jnp.concatenate(rows, axis=0)))
    mesh_ref[...] = split_lanes(jnp.transpose(mesh))
    width = 256
    for first in range(0, sites, width):
        lanes = slice(first, first + width)
        near = dot(mesh_ref[...], wz_ref[0, :, lanes])
        near_slope = dot(mesh_ref[...], wz_ref[1, :, lanes])
        sums = [jnp.zeros((STEP_Y, width), F32) for unused in range(4)]
        for g in range(GROUPS_Y):
            wy = weight_y[g * STEP_Y : (g + 1) * STEP_Y, lanes]
            sy = slope_y[g * STEP_Y : (g + 1) * STEP_Y, lanes]
            for x in range(WIDE_X):
                row = g * LANES + x * STEP_Y
                value = near[row : row + STEP_Y]
                weighted = wy * value
                wx = weight_x[x : x + 1, lanes]
                sums[0] = sums[0] + wx * weighted
                sums[1] = sums[1] + slope_x[x : x + 1, lanes] * weighted
                sums[2] = sums[2] + wx * (sy * value)
                sums[3] = sums[3] + wx * (wy * near_slope[row : row + STEP_Y])
        totals = [jnp.sum(part, axis=0, keepdims=True) for part in sums]
        potential_ref[:, lanes] = totals[0]
        charge = charge_ref[:, lanes]
        for d in range(3):
            forces_ref[d : d + 1, lanes] = -charge * totals[d + 1]


LIMIT = pltpu.CompilerParams(vmem_limit_bytes=56 * 1024 * 1024)


def exchange(chunks):
    flat = chunks.reshape(GX * GY * GZ, 1, CHUNK * LANES)
    return lax.all_to_all(flat, ("gx", "gy", "gz"), 0, 0, tiled=True).reshape(ROWS, LANES)


def body(charges, mesh_start, mesh_frac, influence):
    table = {name: jnp.asarray(value) for name, value in tables().items()}
    sites = charges.shape[0]
    charge = charges.reshape(1, sites)
    pencil = lax.axis_index(("gx", "gz"))
    first = jnp.where(pencil < PENCILS // 2, 0, 1)
    five = lax.dynamic_slice_in_dim(influence, first, 5, axis=0)
    planes = jnp.concatenate([five, influence[:1], influence[:2]], axis=0)
    planes = lax.all_to_all(planes, "gy", 0, 0, tiled=True)
    planes = planes.reshape(10, 32, 8, 40).transpose(1, 3, 0, 2).reshape(1280, 80)
    planes = jnp.pad(planes, [(0, 0), (0, LANES - 80)])
    chunks = pl.pallas_call(
        spread_kernel,
        out_shape=jax.ShapeDtypeStruct((ROWS, LANES), F32),
        scratch_shapes=[pltpu.VMEM((2, M, sites), BF16), pltpu.VMEM((2, GROUPS_Y * LANES, sites), BF16)],
        compiler_params=LIMIT,
        name="spread",
    )(charge, mesh_start, mesh_frac, table["front"])
    chunks = exchange(chunks)
    chunks = pl.pallas_call(
        plane_kernel,
        out_shape=jax.ShapeDtypeStruct((ROWS, LANES), F32),
        scratch_shapes=[pltpu.VMEM((1280, LANES), F32), pltpu.VMEM((1280, LANES), F32)],
        compiler_params=LIMIT,
        name="plane",
    )(
        chunks,
        planes,
        table["left_x"],
        table["left_y"],
        table["left_xh"],
        table["left_yh"],
        table["lanes_x"],
        table["lanes_y"],
        table["lanes_xh"],
        table["lanes_yh"],
        table["turn_x"],
        table["turn_y"],
    )
    chunks = exchange(chunks)
    potential, forces = pl.pallas_call(
        gather_kernel,
        out_shape=(jax.ShapeDtypeStruct((1, sites), F32), jax.ShapeDtypeStruct((3, sites), F32)),
        scratch_shapes=[pltpu.VMEM((2, 1152, sites), BF16), pltpu.VMEM((GROUPS_Y * LANES, 1152), BF16)],
        compiler_params=LIMIT,
        name="gather",
    )(chunks, charge, mesh_start, mesh_frac, table["back"])
    return potential.reshape(sites), forces


def solution(mesh):
    return jax.shard_map(
        body,
        mesh=mesh,
        in_specs=(
            P(("gx", "gy", "gz")),
            P(None, ("gx", "gy", "gz")),
            P(None, ("gx", "gy", "gz")),
            P(("gx", "gz"), "gy", None),
        ),
        out_specs=(P(("gx", "gy", "gz")), P(None, ("gx", "gy", "gz"))),
        check_vma=False,
    )
```

```python
import functools
import math

import jax
import jax.numpy as jnp
import ml_dtypes
import numpy as np
from jax import lax
from jax.experimental import pallas as pl
from jax.experimental.pallas import tpu as pltpu
from jax.sharding import PartitionSpec as P

M = 320
PX = 10
PY = 40
GX, GY, GZ = 4, 8, 8
PENCILS = GX * GZ
SLOTS = 6
CHUNK = 8
HALF = CHUNK // 2
ROWS = GX * GY * GZ * CHUNK
GROUPS_Y = 6
STEP_Y = 8
LANES = 128
WIDE = HALF * LANES
CELLS = GROUPS_Y * PX * STEP_Y
DEEP = 384
SPANS = tuple(
    tuple(range(row * LANES // (PX * STEP_Y), min((row * LANES + LANES - 1) // (PX * STEP_Y), GROUPS_Y - 1) + 1))
    for row in range(HALF)
)
BF16 = jnp.bfloat16
F32 = jnp.float32
NT = (((1,), (1,)), ((), ()))


def halves(table):
    high = table.astype(ml_dtypes.bfloat16)
    low = (table - high.astype(np.float64)).astype(ml_dtypes.bfloat16)
    return high, low


def left_table(table):
    high, low = halves(table)
    return np.concatenate([high, high, low], axis=1)


def right_table(table):
    high, low = halves(table)
    return np.concatenate([high, high, low], axis=0)


def angles(rows, columns, period):
    phase = np.mod(np.outer(rows, columns), period)
    return phase * (2.0 * math.pi / period)


def complex_left(angle):
    c, s = np.cos(angle), np.sin(angle)
    return np.block([[c, s], [-s, c]])


def lanes_complex(angle, live):
    c, s = np.cos(angle) * live, np.sin(angle) * live
    return np.block([[c, -s], [s, c]])


def lanes_x_table(row, group):
    cell = row * LANES + np.arange(LANES)
    x, y = cell // STEP_Y % PX, cell % STEP_Y
    lane = np.arange(LANES)
    k2, y2 = lane // STEP_Y, lane % STEP_Y
    live = (cell < CELLS)[:, None] & (cell // (PX * STEP_Y) == group)[:, None]
    live = live & (y[:, None] == y2[None, :]) & (lane < 80)[None, :]
    return lanes_complex(angles(x, k2, 10), live)


def lanes_y_table():
    lane = np.arange(LANES)
    live = (lane[:, None] // 8 == lane[None, :] // 8) & (lane < 80)[:, None]
    return lanes_complex(angles(lane % 8, lane % 8, 8), live)


def wave_slots():
    waves = np.zeros((GX, SLOTS, GZ), np.int64)
    fold = np.zeros((GX, SLOTS, GZ))
    for gx in range(GX):
        for gz in range(GZ):
            p = gx * GZ + gz
            first = 10 * p + (0 if p < PENCILS // 2 else 1)
            for j in range(5):
                waves[gx, j, gz] = first + j
                fold[gx, j, gz] = 1.0 if first + j == 0 else 2.0
            if p == PENCILS // 2:
                waves[gx, 5, gz] = M // 2
                fold[gx, 5, gz] = 1.0
    return waves.reshape(-1), fold.reshape(-1)


@functools.lru_cache(maxsize=None)
def tables():
    waves, fold = wave_slots()
    angle = angles(waves, np.arange(M), M)
    live = (fold > 0)[:, None]
    front = np.concatenate([np.cos(angle) * live, -np.sin(angle) * live])
    scale = fold[:, None] / float(M * M * M)
    back = np.concatenate([np.cos(angle) * scale, -np.sin(angle) * scale]).T
    back = np.pad(back, [(0, DEEP - M), (0, 0)])
    left_x = complex_left(angles(np.arange(32), np.arange(32), 32))
    order = np.concatenate([5 * np.arange(GY) + g for g in range(5)])
    left_y = complex_left(angles(np.arange(40), order, 40))
    lanes_x = [np.concatenate([lanes_x_table(row, g) for g in SPANS[row]], axis=1) for row in range(HALF)]
    lanes_y = lanes_y_table()
    lane = np.arange(LANES)
    turn_x = angles(np.arange(32), np.arange(WIDE) // STEP_Y % PX, M)
    turn_y = angles(np.arange(40), lane % 8, M)
    return dict(
        front=left_table(front),
        back=left_table(back),
        left_x=left_table(left_x),
        left_y=left_table(left_y),
        left_xh=left_table(left_x.T),
        left_yh=left_table(left_y.T),
        lanes_x=np.concatenate([right_table(table) for table in lanes_x], axis=1),
        lanes_y=right_table(lanes_y),
        lanes_xh=np.concatenate([right_table(table.T) for table in lanes_x], axis=0),
        lanes_yh=right_table(lanes_y.T),
        turn_x=np.stack([np.cos(turn_x), -np.sin(turn_x)]).astype(np.float32),
        turn_y=np.stack([np.cos(turn_y), -np.sin(turn_y)]).astype(np.float32),
    )


def split(value):
    high = value.astype(BF16)
    low = (value - high.astype(F32)).astype(BF16)
    return high, low


def split_rows(value):
    high, low = split(value)
    return jnp.concatenate([high, low, high], axis=0)


def split_lanes(value):
    high, low = split(value)
    return jnp.concatenate([high, low, high], axis=1)


def dot(left, right):
    return jnp.dot(left, right, preferred_element_type=F32)


def spline_weights(fraction):
    values = [1.0 - fraction, fraction] + [jnp.zeros_like(fraction) for unused in range(4)]
    for order in range(3, 6):
        factor = 1.0 / (order - 1)
        values[order - 1] = factor * fraction * values[order - 2]
        for offset in range(1, order - 1):
            values[order - offset - 1] = factor * (
                (fraction + offset) * values[order - offset - 2]
                + (order - offset - fraction) * values[order - offset - 1]
            )
        values[0] = factor * (1.0 - fraction) * values[0]
    slopes = [-values[0]] + [values[offset - 1] - values[offset] for offset in range(1, 6)]
    factor = 1.0 / 5.0
    values[5] = factor * fraction * values[4]
    for offset in range(1, 5):
        values[5 - offset] = factor * (
            (fraction + offset) * values[4 - offset] + (6 - offset - fraction) * values[5 - offset]
        )
    values[0] = factor * (1.0 - fraction) * values[0]
    return values, slopes


def place(coefficients, dimension, offset):
    result = jnp.zeros(offset.shape, F32)
    for j in range(6):
        result = jnp.where(offset == j, coefficients[j][dimension : dimension + 1], result)
    return result


def rows_below(start, length):
    return lax.broadcasted_iota(jnp.int32, (length, start.shape[1]), 0) - start


def z_offset(start, first, length):
    offset = rows_below(start, length) + first
    return jnp.where(offset < 0, offset + M, offset)


def parameters(site_ref):
    whole = site_ref[4:7].astype(jnp.int32)
    return site_ref[0:1], site_ref[1:4], whole[0:1], whole[1:2], whole[2:3]


def spread_kernel(own_ref, near_ref, front_ref, out_ref, wz_ref, plane_ref):
    sites = own_ref.shape[1]
    for source in range(2):
        charge, fraction, start_x, start_y, start_z = parameters((own_ref, near_ref)[source])
        lanes = slice(source * sites, (source + 1) * sites)
        values, unused = spline_weights(fraction)
        weight_x = place(values, 0, rows_below(start_x - source * PX, 16)) * charge
        weight_y = place(values, 1, rows_below(start_y, GROUPS_Y * STEP_Y))
        for block in range(0, M, 16):
            high, low = split(place(values, 2, z_offset(start_z, block, 16)))
            wz_ref[0, block : block + 16, lanes] = high
            wz_ref[1, block : block + 16, lanes] = low
        for cell in range(0, WIDE, 16):
            pair = []
            for first in (cell, cell + STEP_Y):
                if first < CELLS:
                    g, x = first // (PX * STEP_Y), first // STEP_Y % PX
                    near = weight_y[g * STEP_Y : (g + 1) * STEP_Y]
                    pair.append(near * jnp.broadcast_to(weight_x[x : x + 1], near.shape))
                else:
                    pair.append(jnp.zeros((STEP_Y, sites), F32))
            high, low = split(jnp.concatenate(pair, axis=0))
            plane_ref[0, cell : cell + 16, lanes] = high
            plane_ref[1, cell : cell + 16, lanes] = low
    mesh = lax.dot_general(wz_ref[0], plane_ref[0], NT, preferred_element_type=F32)
    mesh = mesh + lax.dot_general(wz_ref[0], plane_ref[1], NT, preferred_element_type=F32)
    mesh = mesh + lax.dot_general(wz_ref[1], plane_ref[0], NT, preferred_element_type=F32)
    waves = dot(front_ref[...], split_rows(mesh))
    span = SLOTS * GZ
    for gx in range(GX):
        first = gx * GY * GZ * CHUNK
        for part in range(2):
            rows = waves[(part * GX + gx) * span : (part * GX + gx + 1) * span]
            for r in range(HALF):
                out_ref[pl.ds(first + part * HALF + r, span, stride=CHUNK), :] = rows[:, r * LANES : (r + 1) * LANES]
        out_ref[first + span * CHUNK : first + GY * GZ * CHUNK] = jnp.zeros(((GY * GZ - span) * CHUNK, LANES), F32)


def turn(real, imag, cos, sin):
    return real * cos - imag * sin, real * sin + imag * cos


def plane_kernel(
    in_ref,
    influence_ref,
    left_x_ref,
    left_y_ref,
    left_xh_ref,
    left_yh_ref,
    lanes_x_ref,
    lanes_y_ref,
    lanes_xh_ref,
    lanes_yh_ref,
    turn_x_ref,
    turn_y_ref,
    out_ref,
    real_ref,
    imag_ref,
):
    cos_x, sin_x = turn_x_ref[0], turn_x_ref[1]
    cos_y, sin_y = turn_y_ref[0], turn_y_ref[1]

    def lane(value, k):
        return value[:, k * LANES : (k + 1) * LANES]

    def chunk_rows(gx, q, part, r):
        return pl.ds((gx * GY + q) * GZ * CHUNK + part * HALF + r, GZ, stride=CHUNK)

    turned = []
    for q in range(GY):
        rows = [
            jnp.concatenate([in_ref[chunk_rows(gx, q, part, r), :] for r in range(HALF)], axis=1)
            for part in range(2)
            for gx in range(GX)
        ]
        mixed = dot(left_x_ref[...], split_rows(jnp.concatenate(rows, axis=0)))
        turned.append(turn(mixed[:32], mixed[32:], cos_x, sin_x))
    groups = [None] * GROUPS_Y
    column = 0
    for r in range(HALF):
        rows = jnp.concatenate([jnp.concatenate([lane(re, r), lane(im, r)], axis=1) for re, im in turned], axis=0)
        width = 2 * LANES * len(SPANS[r])
        done = dot(split_lanes(rows), lanes_x_ref[:, column : column + width])
        column += width
        for i, g in enumerate(SPANS[r]):
            piece = done[:, i * 2 * LANES : (i + 1) * 2 * LANES]
            groups[g] = piece if groups[g] is None else groups[g] + piece
    spill = groups[5]
    groups[0] = groups[0] + jnp.concatenate([spill[7 * 32 :], spill[: 7 * 32]], axis=0)
    for g in range(5):
        real_ref[g * 256 : (g + 1) * 256] = lane(groups[g], 0)
        imag_ref[g * 256 : (g + 1) * 256] = lane(groups[g], 1)

    batch = 4
    for k in range(0, 32, batch):
        picks = [pl.ds(k + i, 40, stride=32) for i in range(batch)]
        real = jnp.concatenate([real_ref[pick, :] for pick in picks], axis=1)
        imag = jnp.concatenate([imag_ref[pick, :] for pick in picks], axis=1)
        mixed = dot(left_y_ref[...], split_rows(jnp.concatenate([real, imag], axis=0)))
        turned = [
            jnp.concatenate(turn(lane(mixed[:40], i), lane(mixed[40:], i), cos_y, sin_y), axis=1)
            for i in range(batch)
        ]
        spectrum = dot(split_lanes(jnp.concatenate(turned, axis=0)), lanes_y_ref[...])
        influence = influence_ref[k * 40 : (k + batch) * 40]
        spectrum = spectrum * jnp.concatenate([influence, influence], axis=1)
        back = dot(split_lanes(spectrum), lanes_yh_ref[...])
        pieces = [
            turn(lane(back[i * 40 : (i + 1) * 40], 0), lane(back[i * 40 : (i + 1) * 40], 1), cos_y, -sin_y)
            for i in range(batch)
        ]
        stacked = jnp.concatenate(
            [jnp.concatenate([piece[part] for piece in pieces], axis=1) for part in range(2)], axis=0
        )
        inverse = dot(left_yh_ref[...], split_rows(stacked))
        for i in range(batch):
            real_ref[picks[i], :] = lane(inverse[:40], i)
            imag_ref[picks[i], :] = lane(inverse[40:], i)

    groups = [
        split(jnp.concatenate([real_ref[g * 256 : (g + 1) * 256], imag_ref[g * 256 : (g + 1) * 256]], axis=1))
        for g in range(5)
    ]
    groups.append([jnp.concatenate([half[32:], half[:32]], axis=0) for half in groups[0]])
    pieces = []
    row = 0
    for r in range(HALF):
        high = [groups[g][0] for g in SPANS[r]]
        low = [groups[g][1] for g in SPANS[r]]
        depth = 3 * 2 * LANES * len(SPANS[r])
        back = dot(jnp.concatenate(high + low + high, axis=1), lanes_xh_ref[row : row + depth])
        row += depth
        pieces.append(back)
    for q in range(GY):
        picked = [back[q * 32 : (q + 1) * 32] for back in pieces]
        real = jnp.concatenate([lane(back, 0) for back in picked], axis=1)
        imag = jnp.concatenate([lane(back, 1) for back in picked], axis=1)
        stacked = jnp.concatenate(turn(real, imag, cos_x, -sin_x), axis=0)
        inverse = dot(left_xh_ref[...], split_rows(stacked))
        for part in range(2):
            for gx in range(GX):
                tile = inverse[(part * GX + gx) * GZ : (part * GX + gx + 1) * GZ]
                for r in range(HALF):
                    out_ref[chunk_rows(gx, q, part, r), :] = lane(tile, r)


def gather_sites(site_ref, shift, columns, mesh, wz_ref, finish):
    sites = site_ref.shape[1]
    unused, fraction, start_x, start_y, start_z = parameters(site_ref)
    values, slopes = spline_weights(fraction)
    offset_x = rows_below(start_x - shift, 16)
    offset_y = rows_below(start_y, GROUPS_Y * STEP_Y)
    weight_x, slope_x = place(values, 0, offset_x), place(slopes, 0, offset_x)
    weight_y, slope_y = place(values, 1, offset_y), place(slopes, 1, offset_y)
    for block in range(0, DEEP, 16):
        if block < M:
            offset = z_offset(start_z, block, 16)
            pairs = [split(place(values, 2, offset)), split(place(slopes, 2, offset))]
        else:
            nothing = jnp.zeros((16, sites), BF16)
            pairs = [(nothing, nothing)] * 2
        for kind in range(2):
            wz_ref[kind, block : block + 16] = pairs[kind][0]
            wz_ref[kind, DEEP + block : DEEP + block + 16] = pairs[kind][0]
            wz_ref[kind, 2 * DEEP + block : 2 * DEEP + block + 16] = pairs[kind][1]
    width = 256
    for first in range(0, sites, width):
        lanes = slice(first, first + width)
        near = dot(mesh, wz_ref[0, :, lanes])
        near_slope = dot(mesh, wz_ref[1, :, lanes])
        sums = [jnp.zeros((STEP_Y, width), F32) for unused in range(4)]
        for g in range(GROUPS_Y):
            wy = weight_y[g * STEP_Y : (g + 1) * STEP_Y, lanes]
            sy = slope_y[g * STEP_Y : (g + 1) * STEP_Y, lanes]
            for x in range(columns):
                row = (g * columns + x) * STEP_Y
                value = near[row : row + STEP_Y]
                weighted = wy * value
                wx = weight_x[x : x + 1, lanes]
                sums[0] = sums[0] + wx * weighted
                sums[1] = sums[1] + slope_x[x : x + 1, lanes] * weighted
                sums[2] = sums[2] + wx * (sy * value)
                sums[3] = sums[3] + wx * (wy * near_slope[row : row + STEP_Y])
        finish(lanes, [jnp.sum(part, axis=0, keepdims=True) for part in sums])


def near_kernel(in_ref, near_ref, back_ref, mesh_ref, part_ref, wz_ref):
    span = SLOTS * GZ
    rows = [
        jnp.concatenate(
            [in_ref[pl.ds(gx * GY * GZ * CHUNK + part * HALF + r, span, stride=CHUNK), :] for r in range(HALF)],
            axis=1,
        )
        for part in range(2)
        for gx in range(GX)
    ]
    mesh = dot(back_ref[...], split_rows(jnp.concatenate(rows, axis=0)))
    mesh = jnp.transpose(mesh)[:CELLS]
    mesh_ref[...] = split_lanes(mesh)
    edge = [mesh[g * PX * STEP_Y : g * PX * STEP_Y + 5 * STEP_Y] for g in range(GROUPS_Y)]
    edge = split_lanes(jnp.concatenate(edge, axis=0))

    def finish(lanes, totals):
        for i in range(4):
            part_ref[i : i + 1, lanes] = totals[i]

    gather_sites(near_ref, PX, 5, edge, wz_ref, finish)


def own_kernel(mesh_ref, own_ref, part_ref, wz_ref):
    def finish(lanes, totals):
        for i in range(4):
            part_ref[i : i + 1, lanes] = totals[i]

    gather_sites(own_ref, 0, PX, mesh_ref[...], wz_ref, finish)


LIMIT = pltpu.CompilerParams(vmem_limit_bytes=56 * 1024 * 1024)


def exchange(chunks):
    flat = chunks.reshape(GX * GY * GZ, 1, CHUNK * LANES)
    return lax.all_to_all(flat, ("gx", "gy", "gz"), 0, 0, tiled=True).reshape(ROWS, LANES)


def body(charges, mesh_start, mesh_frac, influence):
    table = {name: jnp.asarray(value) for name, value in tables().items()}
    sites = charges.shape[0]
    start_x = lax.rem(mesh_start[0:1], PX)
    start_y = lax.rem(mesh_start[1:2], PY)
    whole = jnp.concatenate([start_x, start_y, mesh_start[2:3]], axis=0).astype(F32)
    own = jnp.concatenate([charges.reshape(1, sites), mesh_frac, whole, jnp.zeros((1, sites), F32)], axis=0)
    near = lax.ppermute(own, ("gx", "gz"), [(p, (p + 1) % PENCILS) for p in range(PENCILS)])
    pencil = lax.axis_index(("gx", "gz"))
    first = jnp.where(pencil < PENCILS // 2, 0, 1)
    five = lax.dynamic_slice_in_dim(influence, first, 5, axis=0)
    planes = jnp.concatenate([five, influence[:1], influence[:2]], axis=0)
    planes = lax.all_to_all(planes, "gy", 0, 0, tiled=True)
    planes = planes.reshape(10, 32, 8, 40).transpose(1, 3, 0, 2).reshape(1280, 80)
    planes = jnp.pad(planes, [(0, 0), (0, LANES - 80)])
    chunks = pl.pallas_call(
        spread_kernel,
        out_shape=jax.ShapeDtypeStruct((ROWS, LANES), F32),
        scratch_shapes=[pltpu.VMEM((2, M, 2 * sites), BF16), pltpu.VMEM((2, WIDE, 2 * sites), BF16)],
        compiler_params=LIMIT,
        name="spread",
    )(own, near, table["front"])
    chunks = exchange(chunks)
    chunks = pl.pallas_call(
        plane_kernel,
        out_shape=jax.ShapeDtypeStruct((ROWS, LANES), F32),
        scratch_shapes=[pltpu.VMEM((1280, LANES), F32), pltpu.VMEM((1280, LANES), F32)],
        compiler_params=LIMIT,
        name="plane",
    )(
        chunks,
        planes,
        table["left_x"],
        table["left_y"],
        table["left_xh"],
        table["left_yh"],
        table["lanes_x"],
        table["lanes_y"],
        table["lanes_xh"],
        table["lanes_yh"],
        table["turn_x"],
        table["turn_y"],
    )
    chunks = exchange(chunks)
    mesh, edge = pl.pallas_call(
        near_kernel,
        out_shape=(jax.ShapeDtypeStruct((CELLS, 3 * DEEP), BF16), jax.ShapeDtypeStruct((4, sites), F32)),
        scratch_shapes=[pltpu.VMEM((2, 3 * DEEP, sites), BF16)],
        compiler_params=LIMIT,
        name="near",
    )(chunks, near, table["back"])
    edge = lax.ppermute(edge, ("gx", "gz"), [(p, (p - 1) % PENCILS) for p in range(PENCILS)])
    inner = pl.pallas_call(
        own_kernel,
        out_shape=jax.ShapeDtypeStruct((4, sites), F32),
        scratch_shapes=[pltpu.VMEM((2, 3 * DEEP, sites), BF16)],
        compiler_params=LIMIT,
        name="own",
    )(mesh, own)
    total = inner + edge
    return total[0], -charges[None, :] * total[1:]


def solution(mesh):
    return jax.shard_map(
        body,
        mesh=mesh,
        in_specs=(
            P(("gx", "gy", "gz")),
            P(None, ("gx", "gy", "gz")),
            P(None, ("gx", "gy", "gz")),
            P(("gx", "gz"), "gy", None),
        ),
        out_specs=(P(("gx", "gy", "gz")), P(None, ("gx", "gy", "gz"))),
        check_vma=False,
    )
```

```python
import functools
import math

import jax
import jax.numpy as jnp
import ml_dtypes
import numpy as np
from jax import lax
from jax.experimental import pallas as pl
from jax.experimental.pallas import tpu as pltpu
from jax.sharding import PartitionSpec as P

M = 320
PX = 10
PY = 40
GX, GY, GZ = 4, 8, 8
PENCILS = GX * GZ
SLOTS = 6
CHUNK = 8
HALF = CHUNK // 2
ROWS = GX * GY * GZ * CHUNK
GROUPS_Y = 6
STEP_Y = 8
LANES = 128
WIDE = HALF * LANES
CELLS = GROUPS_Y * PX * STEP_Y
DEEP = 384
STRIDE = 40
BF16 = jnp.bfloat16
F32 = jnp.float32
NT = (((1,), (1,)), ((), ()))


def halves(table):
    high = table.astype(ml_dtypes.bfloat16)
    low = (table - high.astype(np.float64)).astype(ml_dtypes.bfloat16)
    return high, low


def left_table(table):
    high, low = halves(table)
    return np.concatenate([high, high, low], axis=1)


def angles(rows, columns, period):
    phase = np.mod(np.outer(rows, columns), period)
    return phase * (2.0 * math.pi / period)


def complex_left(angle):
    c, s = np.cos(angle), np.sin(angle)
    return np.block([[c, s], [-s, c]])


def lanes_complex(angle, live):
    c, s = np.cos(angle) * live, np.sin(angle) * live
    return np.block([[c, -s], [s, c]])


def lanes_x_table(group):
    slot = np.arange(LANES) // STEP_Y
    x = (slot - PX * group) % (LANES // STEP_Y)
    y = np.arange(LANES) % STEP_Y
    live = (x < PX)[:, None] & (y[:, None] == y[None, :]) & (slot < 10)[None, :]
    return lanes_complex(angles(x, slot, 10), live)


def lanes_y_table():
    lane = np.arange(LANES)
    live = (lane[:, None] // 8 == lane[None, :] // 8) & (lane < 80)[:, None]
    return lanes_complex(angles(lane % 8, lane % 8, 8), live)


def wave_slots():
    waves = np.zeros((GX, SLOTS, GZ), np.int64)
    fold = np.zeros((GX, SLOTS, GZ))
    for gx in range(GX):
        for gz in range(GZ):
            p = gx * GZ + gz
            upper = p >= PENCILS // 2
            for j in range(SLOTS):
                wave = 10 * p + j
                if (j < 5 and not upper) or (j > 0 and upper) or wave == M // 2:
                    waves[gx, j, gz] = wave
                    fold[gx, j, gz] = 1.0 if wave in (0, M // 2) else 2.0
    return waves.reshape(-1), fold.reshape(-1)


@functools.lru_cache(maxsize=None)
def tables():
    waves, fold = wave_slots()
    angle = angles(waves, np.arange(M), M)
    live = (fold > 0)[:, None]
    front = np.concatenate([np.cos(angle) * live, -np.sin(angle) * live])
    scale = fold[:, None] / float(M * M * M)
    back = np.concatenate([np.cos(angle) * scale, -np.sin(angle) * scale]).T
    back = np.pad(back, [(0, DEEP - M), (0, 0)])
    left_x = complex_left(angles(np.arange(32), np.arange(32), 32))
    order = np.concatenate([5 * np.arange(GY) + g for g in range(5)])
    left_y = complex_left(angles(np.arange(40), order, 40))
    lanes_x = [lanes_x_table(g) for g in range(GROUPS_Y)]
    lanes_y = lanes_y_table()
    lane = np.arange(LANES)
    turn_x = angles(np.arange(32), np.arange(WIDE) // STEP_Y % PX, M)
    turn_y = angles(np.arange(40), lane % 8, M)
    parts = [part for table in lanes_x + [lanes_y] for part in halves(table)]
    for table in (left_x, left_x.T, left_y, left_y.T):
        left = left_table(table)
        parts.append(np.pad(left, [(0, 0), (0, 256 - left.shape[1])]))
    turns = [np.cos(turn_x), -np.sin(turn_x), np.cos(turn_y), -np.sin(turn_y)]
    turns = [part[:, i : i + LANES] for part in turns for i in range(0, part.shape[1], LANES)]
    return dict(
        front=left_table(front),
        back=left_table(back),
        mixes=np.concatenate(parts, axis=0),
        turns=np.concatenate(turns, axis=0).astype(np.float32),
    )


def split(value):
    high = value.astype(BF16)
    low = (value - high.astype(F32)).astype(BF16)
    return high, low


def split_rows(value):
    high, low = split(value)
    return jnp.concatenate([high, low, high], axis=0)


def split_lanes(value):
    high, low = split(value)
    return jnp.concatenate([high, low, high], axis=1)


def dot(left, right):
    return jnp.dot(left, right, preferred_element_type=F32)


def dot_nt(left, right):
    return lax.dot_general(left, right, NT, preferred_element_type=F32)


def dot_lanes(form, value, high_table, low_table):
    high, low = split(value)
    return form(high, high_table) + form(low, high_table) + form(high, low_table)


def spline_weights(fraction):
    values = [1.0 - fraction, fraction] + [jnp.zeros_like(fraction) for unused in range(4)]
    for order in range(3, 6):
        factor = 1.0 / (order - 1)
        values[order - 1] = factor * fraction * values[order - 2]
        for offset in range(1, order - 1):
            values[order - offset - 1] = factor * (
                (fraction + offset) * values[order - offset - 2]
                + (order - offset - fraction) * values[order - offset - 1]
            )
        values[0] = factor * (1.0 - fraction) * values[0]
    slopes = [-values[0]] + [values[offset - 1] - values[offset] for offset in range(1, 6)]
    factor = 1.0 / 5.0
    values[5] = factor * fraction * values[4]
    for offset in range(1, 5):
        values[5 - offset] = factor * (
            (fraction + offset) * values[4 - offset] + (6 - offset - fraction) * values[5 - offset]
        )
    values[0] = factor * (1.0 - fraction) * values[0]
    return values, slopes


def place(coefficients, dimension, offset):
    result = jnp.zeros(offset.shape, F32)
    for j in range(6):
        result = jnp.where(offset == j, coefficients[j][dimension : dimension + 1], result)
    return result


def rows_below(start, length):
    return lax.broadcasted_iota(jnp.int32, (length, start.shape[1]), 0) - start


def z_offset(start, first, length):
    offset = rows_below(start, length) + first
    return jnp.where(offset < 0, offset + M, offset)


def parameters(site_ref):
    whole = site_ref[4:7].astype(jnp.int32)
    return site_ref[0:1], site_ref[1:4], whole[0:1], whole[1:2], whole[2:3]


def pack_kernel(charge_ref, start_ref, frac_ref, out_ref):
    out_ref[0:1] = charge_ref[...]
    out_ref[1:4] = frac_ref[...]
    out_ref[4:5] = lax.rem(start_ref[0:1], PX).astype(F32)
    out_ref[5:6] = lax.rem(start_ref[1:2], PY).astype(F32)
    out_ref[6:7] = start_ref[2:3].astype(F32)
    out_ref[7:8] = jnp.zeros(charge_ref.shape, F32)


def finish_kernel(own_ref, edge_ref, inner_ref, potential_ref, forces_ref):
    total = inner_ref[...] + edge_ref[...]
    potential_ref[...] = total[0:1]
    forces_ref[...] = -own_ref[0:1] * total[1:4]


def spread_kernel(own_ref, near_ref, front_ref, out_ref, wz_ref, plane_ref):
    sites = own_ref.shape[1]
    for source in range(2):
        charge, fraction, start_x, start_y, start_z = parameters((own_ref, near_ref)[source])
        lanes = slice(source * sites, (source + 1) * sites)
        values, unused = spline_weights(fraction)
        weight_x = place(values, 0, rows_below(start_x - source * PX, 16)) * charge
        weight_y = place(values, 1, rows_below(start_y, GROUPS_Y * STEP_Y))
        for block in range(0, M, 16):
            high, low = split(place(values, 2, z_offset(start_z, block, 16)))
            wz_ref[0, block : block + 16, lanes] = high
            wz_ref[1, block : block + 16, lanes] = low
        for cell in range(0, WIDE, 16):
            pair = []
            for first in (cell, cell + STEP_Y):
                if first < CELLS:
                    g, x = first // (PX * STEP_Y), first // STEP_Y % PX
                    near = weight_y[g * STEP_Y : (g + 1) * STEP_Y]
                    pair.append(near * jnp.broadcast_to(weight_x[x : x + 1], near.shape))
                else:
                    pair.append(jnp.zeros((STEP_Y, sites), F32))
            high, low = split(jnp.concatenate(pair, axis=0))
            plane_ref[0, cell : cell + 16, lanes] = high
            plane_ref[1, cell : cell + 16, lanes] = low
    mesh = lax.dot_general(wz_ref[0], plane_ref[0], NT, preferred_element_type=F32)
    mesh = mesh + lax.dot_general(wz_ref[0], plane_ref[1], NT, preferred_element_type=F32)
    mesh = mesh + lax.dot_general(wz_ref[1], plane_ref[0], NT, preferred_element_type=F32)
    waves = dot(front_ref[...], split_rows(mesh))
    span = SLOTS * GZ
    for gx in range(GX):
        first = gx * GY * GZ * CHUNK
        for part in range(2):
            rows = waves[(part * GX + gx) * span : (part * GX + gx + 1) * span]
            for r in range(HALF):
                out_ref[pl.ds(first + part * HALF + r, span, stride=CHUNK), :] = rows[:, r * LANES : (r + 1) * LANES]
        out_ref[first + span * CHUNK : first + GY * GZ * CHUNK] = jnp.zeros(((GY * GZ - span) * CHUNK, LANES), F32)


def turn(real, imag, cos, sin):
    return real * cos - imag * sin, real * sin + imag * cos


def plane_kernel(in_ref, influence_ref, mixes_ref, turns_ref, out_ref, real_ref, imag_ref, real_back_ref, imag_back_ref):
    def lanes_table(index):
        first = index * 512
        return mixes_ref[first : first + 256], mixes_ref[first + 256 : first + 512]

    first = (GROUPS_Y + 1) * 512
    left_x, left_xh = mixes_ref[first : first + 64, :192], mixes_ref[first + 64 : first + 128, :192]
    left_y, left_yh = mixes_ref[first + 128 : first + 208, :240], mixes_ref[first + 208 : first + 288, :240]
    cos_x, sin_x = [
        jnp.concatenate([turns_ref[(i * HALF + r) * 32 : (i * HALF + r + 1) * 32] for r in range(HALF)], axis=1)
        for i in range(2)
    ]
    cos_y, sin_y = turns_ref[256:296], turns_ref[296:336]

    def lane(value, k):
        return value[:, k * LANES : (k + 1) * LANES]

    def chunk_rows(gx, q, part, r):
        return pl.ds((gx * GY + q) * GZ * CHUNK + part * HALF + r, GZ, stride=CHUNK)

    turned = []
    for q in range(GY):
        rows = [
            jnp.concatenate([in_ref[chunk_rows(gx, q, part, r), :] for r in range(HALF)], axis=1)
            for part in range(2)
            for gx in range(GX)
        ]
        mixed = dot(left_x, split_rows(jnp.concatenate(rows, axis=0)))
        turned.append(turn(mixed[:32], mixed[32:], cos_x, sin_x))
    lanes = lax.broadcasted_iota(jnp.int32, (1, 2 * LANES), 1) % LANES

    def placed(group, rows):
        first = group * PX * STEP_Y
        row = first // LANES
        if first % LANES + PX * STEP_Y <= LANES:
            return rows[row]
        return jnp.where(lanes >= first % LANES, rows[row], rows[row + 1])

    rows = [
        jnp.concatenate([jnp.concatenate([lane(re, r), lane(im, r)], axis=1) for re, im in turned], axis=0)
        for r in range(HALF)
    ]
    groups = [
        dot_lanes(dot, placed(g, rows), *lanes_table(g)) for g in range(GROUPS_Y)
    ]
    spill = groups[5]
    groups[0] = groups[0] + jnp.concatenate([spill[7 * 32 :], spill[: 7 * 32]], axis=0)
    for g in range(5):
        for q in range(GY):
            first = (g * GY + q) * STRIDE
            real_ref[first : first + 32] = lane(groups[g][q * 32 : (q + 1) * 32], 0)
            imag_ref[first : first + 32] = lane(groups[g][q * 32 : (q + 1) * 32], 1)

    batch = 32
    for k in range(0, 32, batch):
        picks = [pl.ds(k + i, 40, stride=STRIDE) for i in range(batch)]
        real = jnp.concatenate([real_ref[pick, :] for pick in picks], axis=1)
        imag = jnp.concatenate([imag_ref[pick, :] for pick in picks], axis=1)
        mixed = dot(left_y, split_rows(jnp.concatenate([real, imag], axis=0)))
        turned = [
            jnp.concatenate(turn(lane(mixed[:40], i), lane(mixed[40:], i), cos_y, sin_y), axis=1)
            for i in range(batch)
        ]
        spectrum = dot_lanes(dot, jnp.concatenate(turned, axis=0), *lanes_table(GROUPS_Y))
        influence = influence_ref[k * 40 : (k + batch) * 40]
        spectrum = spectrum * jnp.concatenate([influence, influence], axis=1)
        back = dot_lanes(dot_nt, spectrum, *lanes_table(GROUPS_Y))
        pieces = [
            turn(lane(back[i * 40 : (i + 1) * 40], 0), lane(back[i * 40 : (i + 1) * 40], 1), cos_y, -sin_y)
            for i in range(batch)
        ]
        stacked = jnp.concatenate(
            [jnp.concatenate([piece[part] for piece in pieces], axis=1) for part in range(2)], axis=0
        )
        inverse = dot(left_yh, split_rows(stacked))
        for i in range(batch):
            real_back_ref[picks[i], :] = lane(inverse[:40], i)
            imag_back_ref[picks[i], :] = lane(inverse[40:], i)

    groups = [
        jnp.concatenate(
            [
                jnp.concatenate(
                    [ref[(g * GY + q) * STRIDE : (g * GY + q) * STRIDE + 32] for q in range(GY)], axis=0
                )
                for ref in (real_back_ref, imag_back_ref)
            ],
            axis=1,
        )
        for g in range(5)
    ]
    groups.append(jnp.concatenate([groups[0][32:], groups[0][:32]], axis=0))
    pieces = [None] * HALF
    for g in range(GROUPS_Y):
        back = dot_lanes(dot_nt, groups[g], *lanes_table(g))
        first = g * PX * STEP_Y
        row = first // LANES
        pieces[row] = back if pieces[row] is None else jnp.where(lanes >= first % LANES, back, pieces[row])
        if first % LANES + PX * STEP_Y > LANES:
            pieces[row + 1] = back
    for q in range(GY):
        picked = [back[q * 32 : (q + 1) * 32] for back in pieces]
        real = jnp.concatenate([lane(back, 0) for back in picked], axis=1)
        imag = jnp.concatenate([lane(back, 1) for back in picked], axis=1)
        stacked = jnp.concatenate(turn(real, imag, cos_x, -sin_x), axis=0)
        inverse = dot(left_xh, split_rows(stacked))
        for part in range(2):
            for gx in range(GX):
                tile = inverse[(part * GX + gx) * GZ : (part * GX + gx + 1) * GZ]
                for r in range(HALF):
                    out_ref[chunk_rows(gx, q, part, r), :] = lane(tile, r)


def gather_sites(site_ref, shift, columns, mesh, wz_ref, finish):
    sites = site_ref.shape[1]
    unused, fraction, start_x, start_y, start_z = parameters(site_ref)
    values, slopes = spline_weights(fraction)
    offset_x = rows_below(start_x - shift, 16)
    offset_y = rows_below(start_y, GROUPS_Y * STEP_Y)
    weight_x, slope_x = place(values, 0, offset_x), place(slopes, 0, offset_x)
    weight_y, slope_y = place(values, 1, offset_y), place(slopes, 1, offset_y)
    for block in range(0, DEEP, 16):
        if block < M:
            offset = z_offset(start_z, block, 16)
            pairs = [split(place(values, 2, offset)), split(place(slopes, 2, offset))]
        else:
            nothing = jnp.zeros((16, sites), BF16)
            pairs = [(nothing, nothing)] * 2
        for kind in range(2):
            wz_ref[kind, block : block + 16] = pairs[kind][0]
            wz_ref[kind, DEEP + block : DEEP + block + 16] = pairs[kind][0]
            wz_ref[kind, 2 * DEEP + block : 2 * DEEP + block + 16] = pairs[kind][1]
    width = 256
    for first in range(0, sites, width):
        lanes = slice(first, first + width)
        near = dot(mesh, wz_ref[0, :, lanes])
        near_slope = dot(mesh, wz_ref[1, :, lanes])
        sums = [jnp.zeros((STEP_Y, width), F32) for unused in range(4)]
        for g in range(GROUPS_Y):
            wy = weight_y[g * STEP_Y : (g + 1) * STEP_Y, lanes]
            sy = slope_y[g * STEP_Y : (g + 1) * STEP_Y, lanes]
            for x in range(columns):
                row = (g * columns + x) * STEP_Y
                value = near[row : row + STEP_Y]
                weighted = wy * value
                wx = weight_x[x : x + 1, lanes]
                sums[0] = sums[0] + wx * weighted
                sums[1] = sums[1] + slope_x[x : x + 1, lanes] * weighted
                sums[2] = sums[2] + wx * (sy * value)
                sums[3] = sums[3] + wx * (wy * near_slope[row : row + STEP_Y])
        finish(lanes, [jnp.sum(part, axis=0, keepdims=True) for part in sums])


def near_kernel(in_ref, near_ref, back_ref, mesh_ref, part_ref, wz_ref):
    span = SLOTS * GZ
    rows = [
        jnp.concatenate(
            [in_ref[pl.ds(gx * GY * GZ * CHUNK + part * HALF + r, span, stride=CHUNK), :] for r in range(HALF)],
            axis=1,
        )
        for part in range(2)
        for gx in range(GX)
    ]
    mesh = dot(back_ref[...], split_rows(jnp.concatenate(rows, axis=0)))
    mesh = jnp.transpose(mesh)[:CELLS]
    mesh_ref[...] = split_lanes(mesh)
    edge = [mesh[g * PX * STEP_Y : g * PX * STEP_Y + 5 * STEP_Y] for g in range(GROUPS_Y)]
    edge = split_lanes(jnp.concatenate(edge, axis=0))

    def finish(lanes, totals):
        for i in range(4):
            part_ref[i : i + 1, lanes] = totals[i]

    gather_sites(near_ref, PX, 5, edge, wz_ref, finish)


def own_kernel(mesh_ref, own_ref, part_ref, wz_ref):
    def finish(lanes, totals):
        for i in range(4):
            part_ref[i : i + 1, lanes] = totals[i]

    gather_sites(own_ref, 0, PX, mesh_ref[...], wz_ref, finish)


PLANE_SCRATCH = [pltpu.VMEM((40 * STRIDE, LANES), F32) for unused in range(4)]
LIMIT = pltpu.CompilerParams(vmem_limit_bytes=24 * 1024 * 1024)


def exchange(chunks):
    flat = chunks.reshape(GX * GY * GZ, 1, CHUNK * LANES)
    return lax.all_to_all(flat, ("gx", "gy", "gz"), 0, 0, tiled=True).reshape(ROWS, LANES)


def body(charges, mesh_start, mesh_frac, influence):
    table = {name: jnp.asarray(value) for name, value in tables().items()}
    sites = charges.shape[0]
    own = pl.pallas_call(
        pack_kernel,
        out_shape=jax.ShapeDtypeStruct((8, sites), F32),
        compiler_params=LIMIT,
        name="pack",
    )(charges.reshape(1, sites), mesh_start, mesh_frac)
    near = lax.ppermute(own, ("gx", "gz"), [(p, (p + 1) % PENCILS) for p in range(PENCILS)])
    planes, near = lax.optimization_barrier((influence[:GY], near))
    planes = lax.all_to_all(planes, "gy", 0, 0, tiled=True)
    planes = planes.reshape(10, 32, 8, 40).transpose(1, 3, 0, 2).reshape(1280, 80)
    planes = jnp.pad(planes, [(0, 0), (0, LANES - 80)])
    chunks = pl.pallas_call(
        spread_kernel,
        out_shape=jax.ShapeDtypeStruct((ROWS, LANES), F32),
        scratch_shapes=[pltpu.VMEM((2, M, 2 * sites), BF16), pltpu.VMEM((2, WIDE, 2 * sites), BF16)],
        compiler_params=LIMIT,
        name="spread",
    )(own, near, table["front"])
    chunks = exchange(chunks)
    chunks = pl.pallas_call(
        plane_kernel,
        out_shape=jax.ShapeDtypeStruct((ROWS, LANES), F32),
        scratch_shapes=PLANE_SCRATCH,
        compiler_params=LIMIT,
        name="plane",
    )(
        chunks,
        planes,
        table["mixes"],
        table["turns"],
    )
    chunks = exchange(chunks)
    mesh, edge = pl.pallas_call(
        near_kernel,
        out_shape=(jax.ShapeDtypeStruct((CELLS, 3 * DEEP), BF16), jax.ShapeDtypeStruct((4, sites), F32)),
        scratch_shapes=[pltpu.VMEM((2, 3 * DEEP, sites), BF16)],
        compiler_params=LIMIT,
        name="near",
    )(chunks, near, table["back"])
    edge = lax.ppermute(edge, ("gx", "gz"), [(p, (p - 1) % PENCILS) for p in range(PENCILS)])
    inner = pl.pallas_call(
        own_kernel,
        out_shape=jax.ShapeDtypeStruct((4, sites), F32),
        scratch_shapes=[pltpu.VMEM((2, 3 * DEEP, sites), BF16)],
        compiler_params=LIMIT,
        name="own",
    )(mesh, own)
    potential, forces = pl.pallas_call(
        finish_kernel,
        out_shape=(jax.ShapeDtypeStruct((1, sites), F32), jax.ShapeDtypeStruct((3, sites), F32)),
        compiler_params=LIMIT,
        name="finish",
    )(own, edge, inner)
    return potential.reshape(sites), forces


def solution(mesh):
    return jax.shard_map(
        body,
        mesh=mesh,
        in_specs=(
            P(("gx", "gy", "gz")),
            P(None, ("gx", "gy", "gz")),
            P(None, ("gx", "gy", "gz")),
            P(("gx", "gz"), "gy", None),
        ),
        out_specs=(P(("gx", "gy", "gz")), P(None, ("gx", "gy", "gz"))),
        check_vma=False,
    )
```

```python
import functools
import math

import jax
import jax.numpy as jnp
import ml_dtypes
import numpy as np
from jax import lax
from jax.experimental import pallas as pl
from jax.experimental.pallas import tpu as pltpu
from jax.sharding import PartitionSpec as P

M = 320
PX = 10
PY = 40
GX, GY, GZ = 4, 8, 8
PENCILS = GX * GZ
SLOTS = 6
CHUNK = 8
HALF = CHUNK // 2
ROWS = GX * GY * GZ * CHUNK
GROUPS_Y = 6
STEP_Y = 8
LANES = 128
WIDE = HALF * LANES
CELLS = GROUPS_Y * PX * STEP_Y
DEEP = 1024
STRIDE = 40
BF16 = jnp.bfloat16
F32 = jnp.float32
NT = (((1,), (1,)), ((), ()))


def halves(table):
    high = table.astype(ml_dtypes.bfloat16)
    low = (table - high.astype(np.float64)).astype(ml_dtypes.bfloat16)
    return high, low


def left_table(table):
    high, low = halves(table)
    return np.concatenate([high, high, low], axis=1)


def angles(rows, columns, period):
    phase = np.mod(np.outer(rows, columns), period)
    return phase * (2.0 * math.pi / period)


def complex_left(angle):
    c, s = np.cos(angle), np.sin(angle)
    return np.block([[c, s], [-s, c]])


def lanes_complex(angle, live):
    c, s = np.cos(angle) * live, np.sin(angle) * live
    return np.block([[c, -s], [s, c]])


def lanes_x_table():
    slot = np.arange(LANES) // STEP_Y
    y = np.arange(LANES) % STEP_Y
    live = (slot < PX)[:, None] & (y[:, None] == y[None, :]) & (slot < 10)[None, :]
    return lanes_complex(angles(slot, slot, 10), live)


def lanes_y_table():
    lane = np.arange(LANES)
    live = (lane[:, None] // 8 == lane[None, :] // 8) & (lane < 80)[:, None]
    return lanes_complex(angles(lane % 8, lane % 8, 8), live)


def wave_slots():
    waves = np.zeros((GX, SLOTS, GZ), np.int64)
    fold = np.zeros((GX, SLOTS, GZ))
    for gx in range(GX):
        for gz in range(GZ):
            p = gx * GZ + gz
            upper = p >= PENCILS // 2
            for j in range(SLOTS):
                wave = 10 * p + j
                if (j < 5 and not upper) or (j > 0 and upper) or wave == M // 2:
                    waves[gx, j, gz] = wave
                    fold[gx, j, gz] = 1.0 if wave in (0, M // 2) else 2.0
    return waves.reshape(-1), fold.reshape(-1)


@functools.lru_cache(maxsize=None)
def tables():
    waves, fold = wave_slots()
    angle = angles(waves, np.arange(M), M)
    live = (fold > 0)[:, None]
    front = np.concatenate([np.cos(angle) * live, -np.sin(angle) * live])
    scale = fold[:, None] / float(M * M * M)
    back = np.concatenate([np.cos(angle) * scale, -np.sin(angle) * scale]).T
    back = np.pad(back, [(0, 384 - M), (0, 0)])
    left_x = complex_left(angles(np.arange(32), np.arange(32), 32))
    order = np.concatenate([5 * np.arange(GY) + g for g in range(5)])
    left_y = complex_left(angles(np.arange(40), order, 40))
    lanes_x = lanes_x_table()
    lanes_y = lanes_y_table()
    lane = np.arange(LANES)
    turn_x = angles(np.arange(32), np.arange(WIDE) // STEP_Y % PX, M)
    turn_y = angles(np.arange(40), lane % 8, M)
    parts = [part for table in (lanes_x, lanes_y) for part in halves(table)]
    for table in (left_x, left_x.T, left_y, left_y.T):
        left = left_table(table)
        parts.append(np.pad(left, [(0, 0), (0, 256 - left.shape[1])]))
    turns = [np.cos(turn_x), -np.sin(turn_x), np.cos(turn_y), -np.sin(turn_y)]
    turns = [part[:, i : i + LANES] for part in turns for i in range(0, part.shape[1], LANES)]
    return dict(
        front=left_table(front),
        back=left_table(back),
        mixes=np.concatenate(parts, axis=0),
        turns=np.concatenate(turns, axis=0).astype(np.float32),
    )


def split(value):
    high = value.astype(BF16)
    low = (value - high.astype(F32)).astype(BF16)
    return high, low


def split_rows(value):
    high, low = split(value)
    return jnp.concatenate([high, low, high], axis=0)


def split_lanes(value):
    high, low = split(value)
    return jnp.concatenate([high, low, high], axis=1)


def dot(left, right):
    return jnp.dot(left, right, preferred_element_type=F32)


def dot_nt(left, right):
    return lax.dot_general(left, right, NT, preferred_element_type=F32)


def dot_lanes(form, value, high_table, low_table):
    high, low = split(value)
    return form(high, high_table) + form(low, high_table) + form(high, low_table)


def spline_weights(fraction):
    values = [1.0 - fraction, fraction] + [jnp.zeros_like(fraction) for unused in range(4)]
    for order in range(3, 6):
        factor = 1.0 / (order - 1)
        values[order - 1] = factor * fraction * values[order - 2]
        for offset in range(1, order - 1):
            values[order - offset - 1] = factor * (
                (fraction + offset) * values[order - offset - 2]
                + (order - offset - fraction) * values[order - offset - 1]
            )
        values[0] = factor * (1.0 - fraction) * values[0]
    slopes = [-values[0]] + [values[offset - 1] - values[offset] for offset in range(1, 6)]
    factor = 1.0 / 5.0
    values[5] = factor * fraction * values[4]
    for offset in range(1, 5):
        values[5 - offset] = factor * (
            (fraction + offset) * values[4 - offset] + (6 - offset - fraction) * values[5 - offset]
        )
    values[0] = factor * (1.0 - fraction) * values[0]
    return values, slopes


def place(coefficients, dimension, offset):
    result = jnp.zeros(offset.shape, F32)
    for j in range(6):
        result = jnp.where(offset == j, coefficients[j][dimension : dimension + 1], result)
    return result


def rows_below(start, length):
    return lax.broadcasted_iota(jnp.int32, (length, start.shape[1]), 0) - start


def z_offset(start, first, length):
    offset = rows_below(start, length) + first
    return jnp.where(offset < 0, offset + M, offset)


def parameters(site_ref):
    whole = site_ref[4:7].astype(jnp.int32)
    return site_ref[0:1], site_ref[1:4], whole[0:1], whole[1:2], whole[2:3]


def pack_kernel(charge_in, start_in, frac_in, influence_in, out_ref, planes_ref, charge_ref, start_ref, frac_ref, sems):
    copies = [
        pltpu.make_async_copy(start_in, start_ref, sems.at[0]),
        pltpu.make_async_copy(frac_in, frac_ref, sems.at[1]),
        pltpu.make_async_copy(charge_in, charge_ref, sems.at[2]),
        pltpu.make_async_copy(influence_in.at[0:GY], planes_ref, sems.at[3]),
    ]
    for copy in copies:
        copy.start()
    for copy in copies[:3]:
        copy.wait()
    out_ref[0:1] = charge_ref[...]
    out_ref[1:4] = frac_ref[...]
    out_ref[4:5] = lax.rem(start_ref[0:1], PX).astype(F32)
    out_ref[5:6] = lax.rem(start_ref[1:2], PY).astype(F32)
    out_ref[6:7] = start_ref[2:3].astype(F32)
    out_ref[7:8] = jnp.zeros(charge_ref.shape, F32)
    copies[3].wait()


def finish_kernel(own_ref, edge_ref, inner_ref, potential_ref, forces_ref):
    total = inner_ref[...] + edge_ref[...]
    potential_ref[...] = total[0:1]
    forces_ref[...] = -own_ref[0:1] * total[1:4]


def spread_kernel(own_ref, near_ref, front_ref, out_ref, wz_ref, plane_ref):
    sites = own_ref.shape[1]
    for source in range(2):
        charge, fraction, start_x, start_y, start_z = parameters((own_ref, near_ref)[source])
        lanes = slice(source * sites, (source + 1) * sites)
        values, unused = spline_weights(fraction)
        weight_x = place(values, 0, rows_below(start_x - source * PX, 16)) * charge
        weight_y = place(values, 1, rows_below(start_y, GROUPS_Y * STEP_Y))
        for block in range(0, M, 16):
            high, low = split(place(values, 2, z_offset(start_z, block, 16)))
            wz_ref[0, block : block + 16, lanes] = high
            wz_ref[1, block : block + 16, lanes] = low
        for cell in range(0, WIDE, 16):
            pair = []
            for first in (cell, cell + STEP_Y):
                if first < CELLS:
                    g, x = first // (PX * STEP_Y), first // STEP_Y % PX
                    near = weight_y[g * STEP_Y : (g + 1) * STEP_Y]
                    pair.append(near * jnp.broadcast_to(weight_x[x : x + 1], near.shape))
                else:
                    pair.append(jnp.zeros((STEP_Y, sites), F32))
            high, low = split(jnp.concatenate(pair, axis=0))
            plane_ref[0, cell : cell + 16, lanes] = high
            plane_ref[1, cell : cell + 16, lanes] = low
    mesh = lax.dot_general(wz_ref[0], plane_ref[0], NT, preferred_element_type=F32)
    mesh = mesh + lax.dot_general(wz_ref[0], plane_ref[1], NT, preferred_element_type=F32)
    mesh = mesh + lax.dot_general(wz_ref[1], plane_ref[0], NT, preferred_element_type=F32)
    waves = dot(front_ref[...], split_rows(mesh))
    span = SLOTS * GZ
    for gx in range(GX):
        first = gx * GY * GZ * CHUNK
        for part in range(2):
            rows = waves[(part * GX + gx) * span : (part * GX + gx + 1) * span]
            for r in range(HALF):
                out_ref[pl.ds(first + part * HALF + r, span, stride=CHUNK), :] = rows[:, r * LANES : (r + 1) * LANES]
        out_ref[first + span * CHUNK : first + GY * GZ * CHUNK] = jnp.zeros(((GY * GZ - span) * CHUNK, LANES), F32)


def turn(real, imag, cos, sin):
    return real * cos - imag * sin, real * sin + imag * cos


def plane_kernel(in_ref, influence_ref, mixes_ref, turns_ref, out_ref, real_ref, imag_ref, real_back_ref, imag_back_ref):
    def lanes_x_table(group):
        shift = group * PX * STEP_Y % LANES
        pieces = []
        for first in range(0, 512, LANES):
            if shift:
                pieces.append(mixes_ref[first + LANES - shift : first + LANES])
            pieces.append(mixes_ref[first : first + LANES - shift])
        table = jnp.concatenate(pieces, axis=0)
        return table[:256], table[256:]

    lanes_y_table = mixes_ref[512:768], mixes_ref[768:1024]
    first = 1024
    left_x, left_xh = mixes_ref[first : first + 64, :192], mixes_ref[first + 64 : first + 128, :192]
    left_y, left_yh = mixes_ref[first + 128 : first + 208, :240], mixes_ref[first + 208 : first + 288, :240]
    cos_x, sin_x = [
        jnp.concatenate([turns_ref[(i * HALF + r) * 32 : (i * HALF + r + 1) * 32] for r in range(HALF)], axis=1)
        for i in range(2)
    ]
    cos_y, sin_y = turns_ref[256:296], turns_ref[296:336]

    def lane(value, k):
        return value[:, k * LANES : (k + 1) * LANES]

    def chunk_rows(gx, q, part, r):
        return pl.ds((gx * GY + q) * GZ * CHUNK + part * HALF + r, GZ, stride=CHUNK)

    turned = []
    for q in range(GY):
        rows = [
            jnp.concatenate([in_ref[chunk_rows(gx, q, part, r), :] for r in range(HALF)], axis=1)
            for part in range(2)
            for gx in range(GX)
        ]
        mixed = dot(left_x, split_rows(jnp.concatenate(rows, axis=0)))
        turned.append(turn(mixed[:32], mixed[32:], cos_x, sin_x))
    lanes = lax.broadcasted_iota(jnp.int32, (1, 2 * LANES), 1) % LANES

    def placed(group, rows):
        first = group * PX * STEP_Y
        row = first // LANES
        if first % LANES + PX * STEP_Y <= LANES:
            return rows[row]
        return jnp.where(lanes >= first % LANES, rows[row], rows[row + 1])

    rows = [
        jnp.concatenate([jnp.concatenate([lane(re, r), lane(im, r)], axis=1) for re, im in turned], axis=0)
        for r in range(HALF)
    ]
    groups = [
        dot_lanes(dot, placed(g, rows), *lanes_x_table(g)) for g in range(GROUPS_Y)
    ]
    spill = groups[5]
    groups[0] = groups[0] + jnp.concatenate([spill[7 * 32 :], spill[: 7 * 32]], axis=0)
    for g in range(5):
        for q in range(GY):
            first = (g * GY + q) * STRIDE
            real_ref[first : first + 32] = lane(groups[g][q * 32 : (q + 1) * 32], 0)
            imag_ref[first : first + 32] = lane(groups[g][q * 32 : (q + 1) * 32], 1)

    batch = 32
    for k in range(0, 32, batch):
        picks = [pl.ds(k + i, 40, stride=STRIDE) for i in range(batch)]
        real = jnp.concatenate([real_ref[pick, :] for pick in picks], axis=1)
        imag = jnp.concatenate([imag_ref[pick, :] for pick in picks], axis=1)
        mixed = dot(left_y, split_rows(jnp.concatenate([real, imag], axis=0)))
        turned = [
            jnp.concatenate(turn(lane(mixed[:40], i), lane(mixed[40:], i), cos_y, sin_y), axis=1)
            for i in range(batch)
        ]
        spectrum = dot_lanes(dot, jnp.concatenate(turned, axis=0), *lanes_y_table)
        influence = influence_ref[k * 40 : (k + batch) * 40]
        spectrum = spectrum * jnp.concatenate([influence, influence], axis=1)
        back = dot_lanes(dot_nt, spectrum, *lanes_y_table)
        pieces = [
            turn(lane(back[i * 40 : (i + 1) * 40], 0), lane(back[i * 40 : (i + 1) * 40], 1), cos_y, -sin_y)
            for i in range(batch)
        ]
        stacked = jnp.concatenate(
            [jnp.concatenate([piece[part] for piece in pieces], axis=1) for part in range(2)], axis=0
        )
        inverse = dot(left_yh, split_rows(stacked))
        for i in range(batch):
            real_back_ref[picks[i], :] = lane(inverse[:40], i)
            imag_back_ref[picks[i], :] = lane(inverse[40:], i)

    groups = [
        jnp.concatenate(
            [
                jnp.concatenate(
                    [ref[(g * GY + q) * STRIDE : (g * GY + q) * STRIDE + 32] for q in range(GY)], axis=0
                )
                for ref in (real_back_ref, imag_back_ref)
            ],
            axis=1,
        )
        for g in range(5)
    ]
    groups.append(jnp.concatenate([groups[0][32:], groups[0][:32]], axis=0))
    pieces = [None] * HALF
    for g in range(GROUPS_Y):
        back = dot_lanes(dot_nt, groups[g], *lanes_x_table(g))
        first = g * PX * STEP_Y
        row = first // LANES
        pieces[row] = back if pieces[row] is None else jnp.where(lanes >= first % LANES, back, pieces[row])
        if first % LANES + PX * STEP_Y > LANES:
            pieces[row + 1] = back
    for q in range(GY):
        picked = [back[q * 32 : (q + 1) * 32] for back in pieces]
        real = jnp.concatenate([lane(back, 0) for back in picked], axis=1)
        imag = jnp.concatenate([lane(back, 1) for back in picked], axis=1)
        stacked = jnp.concatenate(turn(real, imag, cos_x, -sin_x), axis=0)
        inverse = dot(left_xh, split_rows(stacked))
        for part in range(2):
            for gx in range(GX):
                tile = inverse[(part * GX + gx) * GZ : (part * GX + gx + 1) * GZ]
                for r in range(HALF):
                    out_ref[chunk_rows(gx, q, part, r), :] = lane(tile, r)


def gather_sites(site_ref, shift, columns, mesh, wz_ref, finish):
    sites = site_ref.shape[1]
    unused, fraction, start_x, start_y, start_z = parameters(site_ref)
    values, slopes = spline_weights(fraction)
    offset_x = rows_below(start_x - shift, 16)
    offset_y = rows_below(start_y, GROUPS_Y * STEP_Y)
    weight_x, slope_x = place(values, 0, offset_x), place(slopes, 0, offset_x)
    weight_y, slope_y = place(values, 1, offset_y), place(slopes, 1, offset_y)
    for block in range(0, M, 16):
        offset = z_offset(start_z, block, 16)
        for kind, coefficients in ((0, values), (1, slopes)):
            high, low = split(place(coefficients, 2, offset))
            for term, part in enumerate((high, high, low)):
                row = term * 256 + block if block < 256 else 768 + term * 64 + block - 256
                wz_ref[kind, row : row + 16] = part
    for kind in range(2):
        wz_ref[kind, 960:DEEP] = jnp.zeros((64, sites), BF16)
    width = 256
    for first in range(0, sites, width):
        lanes = slice(first, first + width)
        near = dot(mesh, wz_ref[0, :, lanes])
        near_slope = dot(mesh, wz_ref[1, :, lanes])
        sums = [jnp.zeros((STEP_Y, width), F32) for unused in range(4)]
        for g in range(GROUPS_Y):
            wy = weight_y[g * STEP_Y : (g + 1) * STEP_Y, lanes]
            sy = slope_y[g * STEP_Y : (g + 1) * STEP_Y, lanes]
            for x in range(columns):
                row = (g * columns + x) * STEP_Y
                value = near[row : row + STEP_Y]
                weighted = wy * value
                wx = weight_x[x : x + 1, lanes]
                sums[0] = sums[0] + wx * weighted
                sums[1] = sums[1] + slope_x[x : x + 1, lanes] * weighted
                sums[2] = sums[2] + wx * (sy * value)
                sums[3] = sums[3] + wx * (wy * near_slope[row : row + STEP_Y])
        finish(lanes, [jnp.sum(part, axis=0, keepdims=True) for part in sums])


def deep_lanes(mesh):
    high, low = split(mesh)
    tail = jnp.concatenate([high[:, 256:M], low[:, 256:M], high[:, 256:M], jnp.zeros((mesh.shape[0], 64), BF16)], axis=1)
    return jnp.concatenate([high[:, :256], low[:, :256], high[:, :256], tail], axis=1)


def near_kernel(in_ref, near_ref, back_ref, mesh_ref, part_ref, wz_ref):
    span = SLOTS * GZ
    rows = [
        jnp.concatenate(
            [in_ref[pl.ds(gx * GY * GZ * CHUNK + part * HALF + r, span, stride=CHUNK), :] for r in range(HALF)],
            axis=1,
        )
        for part in range(2)
        for gx in range(GX)
    ]
    mesh = dot(back_ref[...], split_rows(jnp.concatenate(rows, axis=0)))
    mesh = jnp.transpose(mesh)[:CELLS]
    mesh_ref[...] = deep_lanes(mesh)
    edge = [mesh[g * PX * STEP_Y : g * PX * STEP_Y + 5 * STEP_Y] for g in range(GROUPS_Y)]
    edge = deep_lanes(jnp.concatenate(edge, axis=0))

    def finish(lanes, totals):
        for i in range(4):
            part_ref[i : i + 1, lanes] = totals[i]

    gather_sites(near_ref, PX, 5, edge, wz_ref, finish)


def own_kernel(mesh_ref, own_ref, part_ref, wz_ref):
    def finish(lanes, totals):
        for i in range(4):
            part_ref[i : i + 1, lanes] = totals[i]

    gather_sites(own_ref, 0, PX, mesh_ref[...], wz_ref, finish)


PLANE_SCRATCH = [pltpu.VMEM((40 * STRIDE, LANES), F32) for unused in range(4)]
LIMIT = pltpu.CompilerParams(vmem_limit_bytes=24 * 1024 * 1024)


def exchange(chunks):
    flat = chunks.reshape(GX * GY * GZ, 1, CHUNK * LANES)
    return lax.all_to_all(flat, ("gx", "gy", "gz"), 0, 0, tiled=True).reshape(ROWS, LANES)


def body(charges, mesh_start, mesh_frac, influence):
    table = {name: jnp.asarray(value) for name, value in tables().items()}
    sites = charges.shape[0]
    own, planes = pl.pallas_call(
        pack_kernel,
        out_shape=(
            jax.ShapeDtypeStruct((8, sites), F32),
            jax.ShapeDtypeStruct((GY,) + influence.shape[1:], F32),
        ),
        in_specs=[pl.BlockSpec(memory_space=pl.ANY)] * 4,
        scratch_shapes=[
            pltpu.VMEM((1, sites), F32),
            pltpu.VMEM((3, sites), jnp.int32),
            pltpu.VMEM((3, sites), F32),
            pltpu.SemaphoreType.DMA((4,)),
        ],
        compiler_params=pltpu.CompilerParams(vmem_limit_bytes=60 * 1024 * 1024),
        name="pack",
    )(charges.reshape(1, sites), mesh_start, mesh_frac, influence)
    near = lax.ppermute(own, ("gx", "gz"), [(p, (p + 1) % PENCILS) for p in range(PENCILS)])
    planes = lax.all_to_all(planes, "gy", 0, 0, tiled=True)
    planes = planes.reshape(10, 32, 8, 40).transpose(1, 3, 0, 2).reshape(1280, 80)
    planes = jnp.pad(planes, [(0, 0), (0, LANES - 80)])
    chunks = pl.pallas_call(
        spread_kernel,
        out_shape=jax.ShapeDtypeStruct((ROWS, LANES), F32),
        scratch_shapes=[pltpu.VMEM((2, M, 2 * sites), BF16), pltpu.VMEM((2, WIDE, 2 * sites), BF16)],
        compiler_params=LIMIT,
        cost_estimate=pl.CostEstimate(flops=40000000000, bytes_accessed=10000000, transcendentals=0),
        name="spread",
    )(own, near, table["front"])
    chunks = exchange(chunks)
    chunks = pl.pallas_call(
        plane_kernel,
        out_shape=jax.ShapeDtypeStruct((ROWS, LANES), F32),
        scratch_shapes=PLANE_SCRATCH,
        compiler_params=LIMIT,
        name="plane",
    )(
        chunks,
        planes,
        table["mixes"],
        table["turns"],
    )
    chunks = exchange(chunks)
    mesh, edge = pl.pallas_call(
        near_kernel,
        out_shape=(jax.ShapeDtypeStruct((CELLS, DEEP), BF16), jax.ShapeDtypeStruct((4, sites), F32)),
        scratch_shapes=[pltpu.VMEM((2, DEEP, sites), BF16)],
        compiler_params=LIMIT,
        name="near",
    )(chunks, near, table["back"])
    edge = lax.ppermute(edge, ("gx", "gz"), [(p, (p - 1) % PENCILS) for p in range(PENCILS)])
    inner = pl.pallas_call(
        own_kernel,
        out_shape=jax.ShapeDtypeStruct((4, sites), F32),
        scratch_shapes=[pltpu.VMEM((2, DEEP, sites), BF16)],
        compiler_params=LIMIT,
        name="own",
    )(mesh, own)
    potential, forces = pl.pallas_call(
        finish_kernel,
        out_shape=(jax.ShapeDtypeStruct((1, sites), F32), jax.ShapeDtypeStruct((3, sites), F32)),
        compiler_params=LIMIT,
        name="finish",
    )(own, edge, inner)
    return potential.reshape(sites), forces


def solution(mesh):
    return jax.shard_map(
        body,
        mesh=mesh,
        in_specs=(
            P(("gx", "gy", "gz")),
            P(None, ("gx", "gy", "gz")),
            P(None, ("gx", "gy", "gz")),
            P(("gx", "gz"), "gy", None),
        ),
        out_specs=(P(("gx", "gy", "gz")), P(None, ("gx", "gy", "gz"))),
        check_vma=False,
    )
```

```python
import functools
import math

import jax
import jax.numpy as jnp
import ml_dtypes
import numpy as np
from jax import lax
from jax.experimental import pallas as pl
from jax.experimental.pallas import tpu as pltpu
from jax.sharding import PartitionSpec as P

M = 320
PX = 10
PY = 40
GX, GY, GZ = 4, 8, 8
PENCILS = GX * GZ
SLOTS = 6
CHUNK = 8
HALF = CHUNK // 2
ROWS = GX * GY * GZ * CHUNK
GROUPS_Y = 6
STEP_Y = 8
LANES = 128
WIDE = HALF * LANES
CELLS = GROUPS_Y * PX * STEP_Y
DEEP = 1024
STRIDE = 40
PLANE_ROWS = 104
BF16 = jnp.bfloat16
F32 = jnp.float32
NT = (((1,), (1,)), ((), ()))


def halves(table):
    high = table.astype(ml_dtypes.bfloat16)
    low = (table - high.astype(np.float64)).astype(ml_dtypes.bfloat16)
    return high, low


def left_table(table):
    high, low = halves(table)
    return np.concatenate([high, high, low], axis=1)


def angles(rows, columns, period):
    phase = np.mod(np.outer(rows, columns), period)
    return phase * (2.0 * math.pi / period)


def complex_left(angle):
    c, s = np.cos(angle), np.sin(angle)
    return np.block([[c, s], [-s, c]])


def lanes_complex(angle, live):
    c, s = np.cos(angle) * live, np.sin(angle) * live
    return np.block([[c, -s], [s, c]])


def lanes_x_table():
    slot = np.arange(LANES) // STEP_Y
    y = np.arange(LANES) % STEP_Y
    live = (slot < PX)[:, None] & (y[:, None] == y[None, :]) & (slot < 10)[None, :]
    return lanes_complex(angles(slot, slot, 10), live)


def lanes_y_table():
    lane = np.arange(LANES)
    live = (lane[:, None] // 8 == lane[None, :] // 8) & (lane < 80)[:, None]
    return lanes_complex(angles(lane % 8, lane % 8, 8), live)


def wave_slots():
    waves = np.zeros((GX, SLOTS, GZ), np.int64)
    fold = np.zeros((GX, SLOTS, GZ))
    for gx in range(GX):
        for gz in range(GZ):
            p = gx * GZ + gz
            upper = p >= PENCILS // 2
            for j in range(SLOTS):
                wave = 10 * p + j
                if (j < 5 and not upper) or (j > 0 and upper) or wave == M // 2:
                    waves[gx, j, gz] = wave
                    fold[gx, j, gz] = 1.0 if wave in (0, M // 2) else 2.0
    return waves.reshape(-1), fold.reshape(-1)


@functools.lru_cache(maxsize=None)
def tables():
    waves, fold = wave_slots()
    angle = angles(waves, np.arange(M), M)
    live = (fold > 0)[:, None]
    front = np.concatenate([np.cos(angle) * live, -np.sin(angle) * live])
    scale = fold[:, None] / float(M * M * M)
    back = np.concatenate([np.cos(angle) * scale, -np.sin(angle) * scale]).T
    back = np.pad(back, [(0, 384 - M), (0, 0)])
    left_x = complex_left(angles(np.arange(32), np.arange(32), 32))
    order = np.concatenate([5 * np.arange(GY) + g for g in range(5)])
    left_y = complex_left(angles(np.arange(40), order, 40))
    lanes_x = lanes_x_table()
    lanes_y = lanes_y_table()
    lane = np.arange(LANES)
    turn_x = angles(np.arange(32), np.arange(WIDE) // STEP_Y % PX, M)
    turn_y = angles(np.arange(40), lane % 8, M)
    parts = [part for table in (lanes_x, lanes_y) for part in halves(table)]
    for table in (left_x, left_x.T, left_y, left_y.T):
        left = left_table(table)
        parts.append(np.pad(left, [(0, 0), (0, 256 - left.shape[1])]))
    turns = [np.cos(turn_x), -np.sin(turn_x), np.cos(turn_y), -np.sin(turn_y)]
    turns = [part[:, i : i + LANES] for part in turns for i in range(0, part.shape[1], LANES)]
    return dict(
        front=left_table(front),
        back=left_table(back),
        mixes=np.concatenate(parts, axis=0),
        turns=np.concatenate(turns, axis=0).astype(np.float32),
    )


def split(value):
    high = value.astype(BF16)
    low = (value - high.astype(F32)).astype(BF16)
    return high, low


def split_rows(value):
    high, low = split(value)
    return jnp.concatenate([high, low, high], axis=0)


def split_lanes(value):
    high, low = split(value)
    return jnp.concatenate([high, low, high], axis=1)


def dot(left, right):
    return jnp.dot(left, right, preferred_element_type=F32)


def dot_nt(left, right):
    return lax.dot_general(left, right, NT, preferred_element_type=F32)


def dot_lanes(form, value, high_table, low_table):
    high, low = split(value)
    return form(high, high_table) + form(low, high_table) + form(high, low_table)


def spline_weights(fraction):
    values = [1.0 - fraction, fraction] + [jnp.zeros_like(fraction) for unused in range(4)]
    for order in range(3, 6):
        factor = 1.0 / (order - 1)
        values[order - 1] = factor * fraction * values[order - 2]
        for offset in range(1, order - 1):
            values[order - offset - 1] = factor * (
                (fraction + offset) * values[order - offset - 2]
                + (order - offset - fraction) * values[order - offset - 1]
            )
        values[0] = factor * (1.0 - fraction) * values[0]
    slopes = [-values[0]] + [values[offset - 1] - values[offset] for offset in range(1, 6)]
    factor = 1.0 / 5.0
    values[5] = factor * fraction * values[4]
    for offset in range(1, 5):
        values[5 - offset] = factor * (
            (fraction + offset) * values[4 - offset] + (6 - offset - fraction) * values[5 - offset]
        )
    values[0] = factor * (1.0 - fraction) * values[0]
    return values, slopes


def place(coefficients, dimension, offset):
    result = jnp.zeros(offset.shape, F32)
    for j in range(6):
        result = jnp.where(offset == j, coefficients[j][dimension : dimension + 1], result)
    return result


def rows_below(start, length):
    return lax.broadcasted_iota(jnp.int32, (length, start.shape[1]), 0) - start


def z_offset(start, first, length):
    offset = rows_below(start, length) + first
    return jnp.where(offset < 0, offset + M, offset)


def parameters(site_ref):
    whole = site_ref[4:7].astype(jnp.int32)
    return site_ref[0:1], site_ref[1:4], whole[0:1], whole[1:2], whole[2:3]


def pack_kernel(
    charge_in, start_in, frac_in, influence_in, out_ref, planes_ref, charge_ref, start_ref, frac_ref, slab_ref, sems
):
    copies = [
        pltpu.make_async_copy(start_in, start_ref, sems.at[0]),
        pltpu.make_async_copy(frac_in, frac_ref, sems.at[1]),
        pltpu.make_async_copy(charge_in, charge_ref, sems.at[2]),
        pltpu.make_async_copy(influence_in.at[0:SLOTS], slab_ref, sems.at[3]),
    ]
    for copy in copies:
        copy.start()
    for copy in copies[:3]:
        copy.wait()
    out_ref[0:1] = charge_ref[...]
    out_ref[1:4] = frac_ref[...]
    out_ref[4:5] = lax.rem(start_ref[0:1], PX).astype(F32)
    out_ref[5:6] = lax.rem(start_ref[1:2], PY).astype(F32)
    out_ref[6:7] = start_ref[2:3].astype(F32)
    out_ref[7:8] = jnp.zeros(charge_ref.shape, F32)
    copies[3].wait()
    half = PY // 2
    for j in range(SLOTS):
        first = j * PLANE_ROWS
        tail = slab_ref[j, :, 2 * LANES : M]
        planes_ref[first : first + PY] = slab_ref[j, :, :LANES]
        planes_ref[first + PY : first + 2 * PY] = slab_ref[j, :, LANES : 2 * LANES]
        planes_ref[first + 2 * PY : first + 2 * PY + half] = jnp.concatenate([tail[:half], tail[half:]], axis=1)
        planes_ref[first + 2 * PY + half : first + PLANE_ROWS] = jnp.zeros((PLANE_ROWS - 2 * PY - half, LANES), F32)
    planes_ref[SLOTS * PLANE_ROWS :] = jnp.zeros(((GY - SLOTS) * PLANE_ROWS, LANES), F32)


def finish_kernel(own_ref, edge_ref, inner_ref, potential_ref, forces_ref):
    total = inner_ref[...] + edge_ref[...]
    potential_ref[...] = total[0:1]
    forces_ref[...] = -own_ref[0:1] * total[1:4]


def spread_kernel(own_ref, near_ref, front_ref, out_ref, wz_ref, plane_ref):
    sites = own_ref.shape[1]
    for source in range(2):
        charge, fraction, start_x, start_y, start_z = parameters((own_ref, near_ref)[source])
        lanes = slice(source * sites, (source + 1) * sites)
        values, unused = spline_weights(fraction)
        weight_x = place(values, 0, rows_below(start_x - source * PX, 16)) * charge
        weight_y = place(values, 1, rows_below(start_y, GROUPS_Y * STEP_Y))
        for block in range(0, M, 16):
            high, low = split(place(values, 2, z_offset(start_z, block, 16)))
            wz_ref[0, block : block + 16, lanes] = high
            wz_ref[1, block : block + 16, lanes] = low
        for cell in range(0, WIDE, 16):
            pair = []
            for first in (cell, cell + STEP_Y):
                if first < CELLS:
                    g, x = first // (PX * STEP_Y), first // STEP_Y % PX
                    near = weight_y[g * STEP_Y : (g + 1) * STEP_Y]
                    pair.append(near * jnp.broadcast_to(weight_x[x : x + 1], near.shape))
                else:
                    pair.append(jnp.zeros((STEP_Y, sites), F32))
            high, low = split(jnp.concatenate(pair, axis=0))
            plane_ref[0, cell : cell + 16, lanes] = high
            plane_ref[1, cell : cell + 16, lanes] = low
    mesh = lax.dot_general(wz_ref[0], plane_ref[0], NT, preferred_element_type=F32)
    mesh = mesh + lax.dot_general(wz_ref[0], plane_ref[1], NT, preferred_element_type=F32)
    mesh = mesh + lax.dot_general(wz_ref[1], plane_ref[0], NT, preferred_element_type=F32)
    waves = dot(front_ref[...], split_rows(mesh))
    span = SLOTS * GZ
    for gx in range(GX):
        first = gx * GY * GZ * CHUNK
        for part in range(2):
            rows = waves[(part * GX + gx) * span : (part * GX + gx + 1) * span]
            for r in range(HALF):
                out_ref[pl.ds(first + part * HALF + r, span, stride=CHUNK), :] = rows[:, r * LANES : (r + 1) * LANES]
        out_ref[first + span * CHUNK : first + GY * GZ * CHUNK] = jnp.zeros(((GY * GZ - span) * CHUNK, LANES), F32)


def turn(real, imag, cos, sin):
    return real * cos - imag * sin, real * sin + imag * cos


def plane_kernel(in_ref, influence_ref, mixes_ref, turns_ref, out_ref, real_ref, imag_ref, real_back_ref, imag_back_ref):
    def lanes_x_table(group):
        shift = group * PX * STEP_Y % LANES
        pieces = []
        for first in range(0, 512, LANES):
            if shift:
                pieces.append(mixes_ref[first + LANES - shift : first + LANES])
            pieces.append(mixes_ref[first : first + LANES - shift])
        table = jnp.concatenate(pieces, axis=0)
        return table[:256], table[256:]

    lanes_y_table = mixes_ref[512:768], mixes_ref[768:1024]
    first = 1024
    left_x, left_xh = mixes_ref[first : first + 64, :192], mixes_ref[first + 64 : first + 128, :192]
    left_y, left_yh = mixes_ref[first + 128 : first + 208, :240], mixes_ref[first + 208 : first + 288, :240]
    cos_x, sin_x = [
        jnp.concatenate([turns_ref[(i * HALF + r) * 32 : (i * HALF + r + 1) * 32] for r in range(HALF)], axis=1)
        for i in range(2)
    ]
    cos_y, sin_y = turns_ref[256:296], turns_ref[296:336]

    def lane(value, k):
        return value[:, k * LANES : (k + 1) * LANES]

    def chunk_rows(gx, q, part, r):
        return pl.ds((gx * GY + q) * GZ * CHUNK + part * HALF + r, GZ, stride=CHUNK)

    turned = []
    for q in range(GY):
        rows = [
            jnp.concatenate([in_ref[chunk_rows(gx, q, part, r), :] for r in range(HALF)], axis=1)
            for part in range(2)
            for gx in range(GX)
        ]
        mixed = dot(left_x, split_rows(jnp.concatenate(rows, axis=0)))
        turned.append(turn(mixed[:32], mixed[32:], cos_x, sin_x))
    lanes = lax.broadcasted_iota(jnp.int32, (1, 2 * LANES), 1) % LANES

    def placed(group, rows):
        first = group * PX * STEP_Y
        row = first // LANES
        if first % LANES + PX * STEP_Y <= LANES:
            return rows[row]
        return jnp.where(lanes >= first % LANES, rows[row], rows[row + 1])

    rows = [
        jnp.concatenate([jnp.concatenate([lane(re, r), lane(im, r)], axis=1) for re, im in turned], axis=0)
        for r in range(HALF)
    ]
    groups = [
        dot_lanes(dot, placed(g, rows), *lanes_x_table(g)) for g in range(GROUPS_Y)
    ]
    spill = groups[5]
    groups[0] = groups[0] + jnp.concatenate([spill[7 * 32 :], spill[: 7 * 32]], axis=0)
    for g in range(5):
        for q in range(GY):
            first = (g * GY + q) * STRIDE
            real_ref[first : first + 32] = lane(groups[g][q * 32 : (q + 1) * 32], 0)
            imag_ref[first : first + 32] = lane(groups[g][q * 32 : (q + 1) * 32], 1)

    batch = 32
    for k in range(0, 32, batch):
        picks = [pl.ds(k + i, 40, stride=STRIDE) for i in range(batch)]
        real = jnp.concatenate([real_ref[pick, :] for pick in picks], axis=1)
        imag = jnp.concatenate([imag_ref[pick, :] for pick in picks], axis=1)
        mixed = dot(left_y, split_rows(jnp.concatenate([real, imag], axis=0)))
        turned = [
            jnp.concatenate(turn(lane(mixed[:40], i), lane(mixed[40:], i), cos_y, sin_y), axis=1)
            for i in range(batch)
        ]
        spectrum = dot_lanes(dot, jnp.concatenate(turned, axis=0), *lanes_y_table)
        influence = influence_ref[k * 40 : (k + batch) * 40]
        spectrum = spectrum * jnp.concatenate([influence, influence], axis=1)
        back = dot_lanes(dot_nt, spectrum, *lanes_y_table)
        pieces = [
            turn(lane(back[i * 40 : (i + 1) * 40], 0), lane(back[i * 40 : (i + 1) * 40], 1), cos_y, -sin_y)
            for i in range(batch)
        ]
        stacked = jnp.concatenate(
            [jnp.concatenate([piece[part] for piece in pieces], axis=1) for part in range(2)], axis=0
        )
        inverse = dot(left_yh, split_rows(stacked))
        for i in range(batch):
            real_back_ref[picks[i], :] = lane(inverse[:40], i)
            imag_back_ref[picks[i], :] = lane(inverse[40:], i)

    groups = [
        jnp.concatenate(
            [
                jnp.concatenate(
                    [ref[(g * GY + q) * STRIDE : (g * GY + q) * STRIDE + 32] for q in range(GY)], axis=0
                )
                for ref in (real_back_ref, imag_back_ref)
            ],
            axis=1,
        )
        for g in range(5)
    ]
    groups.append(jnp.concatenate([groups[0][32:], groups[0][:32]], axis=0))
    pieces = [None] * HALF
    for g in range(GROUPS_Y):
        back = dot_lanes(dot_nt, groups[g], *lanes_x_table(g))
        first = g * PX * STEP_Y
        row = first // LANES
        pieces[row] = back if pieces[row] is None else jnp.where(lanes >= first % LANES, back, pieces[row])
        if first % LANES + PX * STEP_Y > LANES:
            pieces[row + 1] = back
    for q in range(GY):
        picked = [back[q * 32 : (q + 1) * 32] for back in pieces]
        real = jnp.concatenate([lane(back, 0) for back in picked], axis=1)
        imag = jnp.concatenate([lane(back, 1) for back in picked], axis=1)
        stacked = jnp.concatenate(turn(real, imag, cos_x, -sin_x), axis=0)
        inverse = dot(left_xh, split_rows(stacked))
        for part in range(2):
            for gx in range(GX):
                tile = inverse[(part * GX + gx) * GZ : (part * GX + gx + 1) * GZ]
                for r in range(HALF):
                    out_ref[chunk_rows(gx, q, part, r), :] = lane(tile, r)


def gather_sites(site_ref, shift, columns, mesh, wz_ref, finish):
    sites = site_ref.shape[1]
    unused, fraction, start_x, start_y, start_z = parameters(site_ref)
    values, slopes = spline_weights(fraction)
    offset_x = rows_below(start_x - shift, 16)
    offset_y = rows_below(start_y, GROUPS_Y * STEP_Y)
    weight_x, slope_x = place(values, 0, offset_x), place(slopes, 0, offset_x)
    weight_y, slope_y = place(values, 1, offset_y), place(slopes, 1, offset_y)
    for block in range(0, M, 16):
        offset = z_offset(start_z, block, 16)
        for kind, coefficients in ((0, values), (1, slopes)):
            high, low = split(place(coefficients, 2, offset))
            for term, part in enumerate((high, high, low)):
                row = term * 256 + block if block < 256 else 768 + term * 64 + block - 256
                wz_ref[kind, row : row + 16] = part
    for kind in range(2):
        wz_ref[kind, 960:DEEP] = jnp.zeros((64, sites), BF16)
    width = 256
    for first in range(0, sites, width):
        lanes = slice(first, first + width)
        near = dot(mesh, wz_ref[0, :, lanes])
        near_slope = dot(mesh, wz_ref[1, :, lanes])
        sums = [jnp.zeros((STEP_Y, width), F32) for unused in range(4)]
        for g in range(GROUPS_Y):
            wy = weight_y[g * STEP_Y : (g + 1) * STEP_Y, lanes]
            sy = slope_y[g * STEP_Y : (g + 1) * STEP_Y, lanes]
            for x in range(columns):
                row = (g * columns + x) * STEP_Y
                value = near[row : row + STEP_Y]
                weighted = wy * value
                wx = weight_x[x : x + 1, lanes]
                sums[0] = sums[0] + wx * weighted
                sums[1] = sums[1] + slope_x[x : x + 1, lanes] * weighted
                sums[2] = sums[2] + wx * (sy * value)
                sums[3] = sums[3] + wx * (wy * near_slope[row : row + STEP_Y])
        finish(lanes, [jnp.sum(part, axis=0, keepdims=True) for part in sums])


def deep_lanes(mesh):
    high, low = split(mesh)
    tail = jnp.concatenate([high[:, 256:M], low[:, 256:M], high[:, 256:M], jnp.zeros((mesh.shape[0], 64), BF16)], axis=1)
    return jnp.concatenate([high[:, :256], low[:, :256], high[:, :256], tail], axis=1)


def near_kernel(in_ref, near_ref, back_ref, mesh_ref, part_ref, wz_ref):
    span = SLOTS * GZ
    rows = [
        jnp.concatenate(
            [in_ref[pl.ds(gx * GY * GZ * CHUNK + part * HALF + r, span, stride=CHUNK), :] for r in range(HALF)],
            axis=1,
        )
        for part in range(2)
        for gx in range(GX)
    ]
    mesh = dot(back_ref[...], split_rows(jnp.concatenate(rows, axis=0)))
    mesh = jnp.transpose(mesh)[:CELLS]
    mesh_ref[...] = deep_lanes(mesh)
    edge = [mesh[g * PX * STEP_Y : g * PX * STEP_Y + 5 * STEP_Y] for g in range(GROUPS_Y)]
    edge = deep_lanes(jnp.concatenate(edge, axis=0))

    def finish(lanes, totals):
        for i in range(4):
            part_ref[i : i + 1, lanes] = totals[i]

    gather_sites(near_ref, PX, 5, edge, wz_ref, finish)


def own_kernel(mesh_ref, own_ref, part_ref, wz_ref):
    def finish(lanes, totals):
        for i in range(4):
            part_ref[i : i + 1, lanes] = totals[i]

    gather_sites(own_ref, 0, PX, mesh_ref[...], wz_ref, finish)


PLANE_SCRATCH = [pltpu.VMEM((40 * STRIDE, LANES), F32) for unused in range(4)]
LIMIT = pltpu.CompilerParams(vmem_limit_bytes=24 * 1024 * 1024)


def exchange(chunks):
    flat = chunks.reshape(GX * GY * GZ, 1, CHUNK * LANES)
    return lax.all_to_all(flat, ("gx", "gy", "gz"), 0, 0, tiled=True).reshape(ROWS, LANES)


def body(charges, mesh_start, mesh_frac, influence):
    table = {name: jnp.asarray(value) for name, value in tables().items()}
    sites = charges.shape[0]
    own, planes = pl.pallas_call(
        pack_kernel,
        out_shape=(
            jax.ShapeDtypeStruct((8, sites), F32),
            jax.ShapeDtypeStruct((GY * PLANE_ROWS, LANES), F32),
        ),
        in_specs=[pl.BlockSpec(memory_space=pl.ANY)] * 4,
        scratch_shapes=[
            pltpu.VMEM((1, sites), F32),
            pltpu.VMEM((3, sites), jnp.int32),
            pltpu.VMEM((3, sites), F32),
            pltpu.VMEM((SLOTS, PY, M), F32),
            pltpu.SemaphoreType.DMA((4,)),
        ],
        compiler_params=pltpu.CompilerParams(vmem_limit_bytes=60 * 1024 * 1024),
        name="pack",
    )(charges.reshape(1, sites), mesh_start, mesh_frac, influence)
    near = lax.ppermute(own, ("gx", "gz"), [(p, (p + 1) % PENCILS) for p in range(PENCILS)])
    planes = lax.all_to_all(planes.reshape(GY, 1, PLANE_ROWS * LANES), "gy", 0, 0, tiled=True)
    planes = planes.reshape(GY, PLANE_ROWS, LANES)
    tail = planes[:, 2 * PY : 2 * PY + PY // 2]
    tail = jnp.concatenate([tail[:, :, : LANES // 2], tail[:, :, LANES // 2 :]], axis=1)
    planes = jnp.concatenate([planes[:, :PY], planes[:, PY : 2 * PY], tail], axis=2)
    planes = planes.reshape(10, 32, 8, 40).transpose(1, 3, 0, 2).reshape(1280, 80)
    planes = jnp.pad(planes, [(0, 0), (0, LANES - 80)])
    chunks = pl.pallas_call(
        spread_kernel,
        out_shape=jax.ShapeDtypeStruct((ROWS, LANES), F32),
        scratch_shapes=[pltpu.VMEM((2, M, 2 * sites), BF16), pltpu.VMEM((2, WIDE, 2 * sites), BF16)],
        compiler_params=LIMIT,
        cost_estimate=pl.CostEstimate(flops=40000000000, bytes_accessed=10000000, transcendentals=0),
        name="spread",
    )(own, near, table["front"])
    chunks = exchange(chunks)
    chunks = pl.pallas_call(
        plane_kernel,
        out_shape=jax.ShapeDtypeStruct((ROWS, LANES), F32),
        scratch_shapes=PLANE_SCRATCH,
        compiler_params=LIMIT,
        name="plane",
    )(
        chunks,
        planes,
        table["mixes"],
        table["turns"],
    )
    chunks = exchange(chunks)
    mesh, edge = pl.pallas_call(
        near_kernel,
        out_shape=(jax.ShapeDtypeStruct((CELLS, DEEP), BF16), jax.ShapeDtypeStruct((4, sites), F32)),
        scratch_shapes=[pltpu.VMEM((2, DEEP, sites), BF16)],
        compiler_params=LIMIT,
        name="near",
    )(chunks, near, table["back"])
    edge = lax.ppermute(edge, ("gx", "gz"), [(p, (p - 1) % PENCILS) for p in range(PENCILS)])
    inner = pl.pallas_call(
        own_kernel,
        out_shape=jax.ShapeDtypeStruct((4, sites), F32),
        scratch_shapes=[pltpu.VMEM((2, DEEP, sites), BF16)],
        compiler_params=LIMIT,
        name="own",
    )(mesh, own)
    potential, forces = pl.pallas_call(
        finish_kernel,
        out_shape=(jax.ShapeDtypeStruct((1, sites), F32), jax.ShapeDtypeStruct((3, sites), F32)),
        compiler_params=LIMIT,
        name="finish",
    )(own, edge, inner)
    return potential.reshape(sites), forces


def solution(mesh):
    return jax.shard_map(
        body,
        mesh=mesh,
        in_specs=(
            P(("gx", "gy", "gz")),
            P(None, ("gx", "gy", "gz")),
            P(None, ("gx", "gy", "gz")),
            P(("gx", "gz"), "gy", None),
        ),
        out_specs=(P(("gx", "gy", "gz")), P(None, ("gx", "gy", "gz"))),
        check_vma=False,
    )
```

```python
import functools
import math

import jax
import jax.numpy as jnp
import ml_dtypes
import numpy as np
from jax import lax
from jax.experimental import pallas as pl
from jax.experimental.pallas import tpu as pltpu
from jax.sharding import PartitionSpec as P

M = 320
PX = 10
PY = 40
GX, GY, GZ = 4, 8, 8
PENCILS = GX * GZ
SLOTS = 6
CHUNK = 8
HALF = CHUNK // 2
ROWS = GX * GY * GZ * CHUNK
GROUPS_Y = 6
STEP_Y = 8
LANES = 128
WIDE = HALF * LANES
CELLS = GROUPS_Y * PX * STEP_Y
DEEP = 1024
STRIDE = 40
PLANE_ROWS = 104
BF16 = jnp.bfloat16
F32 = jnp.float32
NT = (((1,), (1,)), ((), ()))


def halves(table):
    high = table.astype(ml_dtypes.bfloat16)
    low = (table - high.astype(np.float64)).astype(ml_dtypes.bfloat16)
    return high, low


def left_table(table):
    high, low = halves(table)
    return np.concatenate([high, high, low], axis=1)


def angles(rows, columns, period):
    phase = np.mod(np.outer(rows, columns), period)
    return phase * (2.0 * math.pi / period)


def complex_left(angle):
    c, s = np.cos(angle), np.sin(angle)
    return np.block([[c, s], [-s, c]])


def lanes_complex(angle, live):
    c, s = np.cos(angle) * live, np.sin(angle) * live
    return np.block([[c, -s], [s, c]])


def lanes_x_table():
    slot = np.arange(LANES) // STEP_Y
    y = np.arange(LANES) % STEP_Y
    live = (slot < PX)[:, None] & (y[:, None] == y[None, :]) & (slot < 10)[None, :]
    return lanes_complex(angles(slot, slot, 10), live)


def lanes_y_table():
    lane = np.arange(LANES)
    live = (lane[:, None] // 8 == lane[None, :] // 8) & (lane < 80)[:, None]
    return lanes_complex(angles(lane % 8, lane % 8, 8), live)


def wave_slots():
    waves = np.zeros((GX, SLOTS, GZ), np.int64)
    fold = np.zeros((GX, SLOTS, GZ))
    for gx in range(GX):
        for gz in range(GZ):
            p = gx * GZ + gz
            upper = p >= PENCILS // 2
            for j in range(SLOTS):
                wave = 10 * p + j
                if (j < 5 and not upper) or (j > 0 and upper) or wave == M // 2:
                    waves[gx, j, gz] = wave
                    fold[gx, j, gz] = 1.0 if wave in (0, M // 2) else 2.0
    return waves.reshape(-1), fold.reshape(-1)


@functools.lru_cache(maxsize=None)
def tables():
    waves, fold = wave_slots()
    angle = angles(waves, np.arange(M), M)
    live = (fold > 0)[:, None]
    front = np.concatenate([np.cos(angle) * live, -np.sin(angle) * live])
    scale = fold[:, None] / float(M * M * M)
    back = np.concatenate([np.cos(angle) * scale, -np.sin(angle) * scale]).T
    back = np.pad(back, [(0, 384 - M), (0, 0)])
    left_x = complex_left(angles(np.arange(32), np.arange(32), 32))
    order = np.concatenate([5 * np.arange(GY) + g for g in range(5)])
    left_y = complex_left(angles(np.arange(40), order, 40))
    lanes_x = lanes_x_table()
    lanes_y = lanes_y_table()
    lane = np.arange(LANES)
    turn_x = angles(np.arange(32), np.arange(WIDE) // STEP_Y % PX, M)
    turn_y = angles(np.arange(40), lane % 8, M)
    parts = [part for table in (lanes_x, lanes_y) for part in halves(table)]
    for table in (left_x, left_x.T, left_y, left_y.T):
        left = left_table(table)
        parts.append(np.pad(left, [(0, 0), (0, 256 - left.shape[1])]))
    turns = [np.cos(turn_x), -np.sin(turn_x), np.cos(turn_y), -np.sin(turn_y)]
    turns = [part[:, i : i + LANES] for part in turns for i in range(0, part.shape[1], LANES)]
    return dict(
        front=left_table(front),
        back=left_table(back),
        mixes=np.concatenate(parts, axis=0),
        turns=np.concatenate(turns, axis=0).astype(np.float32),
    )


def split(value):
    high = value.astype(BF16)
    low = (value - high.astype(F32)).astype(BF16)
    return high, low


def split_rows(value):
    high, low = split(value)
    return jnp.concatenate([high, low, high], axis=0)


def split_lanes(value):
    high, low = split(value)
    return jnp.concatenate([high, low, high], axis=1)


def dot(left, right):
    return jnp.dot(left, right, preferred_element_type=F32)


def dot_nt(left, right):
    return lax.dot_general(left, right, NT, preferred_element_type=F32)


def dot_lanes(form, value, high_table, low_table):
    high, low = split(value)
    return form(high, high_table) + form(low, high_table) + form(high, low_table)


def spline_weights(fraction):
    values = [1.0 - fraction, fraction] + [jnp.zeros_like(fraction) for unused in range(4)]
    for order in range(3, 6):
        factor = 1.0 / (order - 1)
        values[order - 1] = factor * fraction * values[order - 2]
        for offset in range(1, order - 1):
            values[order - offset - 1] = factor * (
                (fraction + offset) * values[order - offset - 2]
                + (order - offset - fraction) * values[order - offset - 1]
            )
        values[0] = factor * (1.0 - fraction) * values[0]
    slopes = [-values[0]] + [values[offset - 1] - values[offset] for offset in range(1, 6)]
    factor = 1.0 / 5.0
    values[5] = factor * fraction * values[4]
    for offset in range(1, 5):
        values[5 - offset] = factor * (
            (fraction + offset) * values[4 - offset] + (6 - offset - fraction) * values[5 - offset]
        )
    values[0] = factor * (1.0 - fraction) * values[0]
    return values, slopes


def place(coefficients, dimension, offset):
    result = jnp.zeros(offset.shape, F32)
    for j in range(6):
        result = jnp.where(offset == j, coefficients[j][dimension : dimension + 1], result)
    return result


def rows_below(start, length):
    return lax.broadcasted_iota(jnp.int32, (length, start.shape[1]), 0) - start


def z_offset(start, first, length):
    offset = rows_below(start, length) + first
    return jnp.where(offset < 0, offset + M, offset)


def parameters(site_ref):
    whole = site_ref[4:7].astype(jnp.int32)
    return site_ref[0:1], site_ref[1:4], whole[0:1], whole[1:2], whole[2:3]


def pack_kernel(
    charge_in, start_in, frac_in, influence_in, out_ref, planes_ref, charge_ref, start_ref, frac_ref, slab_ref, sems
):
    copies = [
        pltpu.make_async_copy(start_in, start_ref, sems.at[0]),
        pltpu.make_async_copy(frac_in, frac_ref, sems.at[1]),
        pltpu.make_async_copy(charge_in, charge_ref, sems.at[2]),
        pltpu.make_async_copy(influence_in.at[0:SLOTS], slab_ref, sems.at[3]),
    ]
    for copy in copies:
        copy.start()
    for copy in copies[:3]:
        copy.wait()
    out_ref[0:1] = charge_ref[...]
    out_ref[1:4] = frac_ref[...]
    out_ref[4:5] = lax.rem(start_ref[0:1], PX).astype(F32)
    out_ref[5:6] = lax.rem(start_ref[1:2], PY).astype(F32)
    out_ref[6:7] = start_ref[2:3].astype(F32)
    out_ref[7:8] = jnp.zeros(charge_ref.shape, F32)
    copies[3].wait()
    half = PY // 2
    for j in range(SLOTS):
        first = j * PLANE_ROWS
        tail = slab_ref[j, :, 2 * LANES : M]
        planes_ref[first : first + PY] = slab_ref[j, :, :LANES]
        planes_ref[first + PY : first + 2 * PY] = slab_ref[j, :, LANES : 2 * LANES]
        planes_ref[first + 2 * PY : first + 2 * PY + half] = jnp.concatenate([tail[:half], tail[half:]], axis=1)
        planes_ref[first + 2 * PY + half : first + PLANE_ROWS] = jnp.zeros((PLANE_ROWS - 2 * PY - half, LANES), F32)
    planes_ref[SLOTS * PLANE_ROWS :] = jnp.zeros(((GY - SLOTS) * PLANE_ROWS, LANES), F32)


def finish_kernel(own_ref, edge_ref, inner_ref, potential_ref, forces_ref):
    total = inner_ref[...] + edge_ref[...]
    potential_ref[...] = total[0:1]
    forces_ref[...] = -own_ref[0:1] * total[1:4]


def spread_kernel(own_ref, near_ref, front_ref, out_ref, wz_ref, plane_ref):
    sites = own_ref.shape[1]
    for source in range(2):
        charge, fraction, start_x, start_y, start_z = parameters((own_ref, near_ref)[source])
        lanes = slice(source * sites, (source + 1) * sites)
        values, unused = spline_weights(fraction)
        weight_x = place(values, 0, rows_below(start_x - source * PX, 16)) * charge
        weight_y = place(values, 1, rows_below(start_y, GROUPS_Y * STEP_Y))
        for block in range(0, M, 16):
            high, low = split(place(values, 2, z_offset(start_z, block, 16)))
            wz_ref[0, block : block + 16, lanes] = high
            wz_ref[1, block : block + 16, lanes] = low
        for cell in range(0, WIDE, 16):
            pair = []
            for first in (cell, cell + STEP_Y):
                if first < CELLS:
                    g, x = first // (PX * STEP_Y), first // STEP_Y % PX
                    near = weight_y[g * STEP_Y : (g + 1) * STEP_Y]
                    pair.append(near * jnp.broadcast_to(weight_x[x : x + 1], near.shape))
                else:
                    pair.append(jnp.zeros((STEP_Y, sites), F32))
            high, low = split(jnp.concatenate(pair, axis=0))
            plane_ref[0, cell : cell + 16, lanes] = high
            plane_ref[1, cell : cell + 16, lanes] = low
    mesh = lax.dot_general(wz_ref[0], plane_ref[0], NT, preferred_element_type=F32)
    mesh = mesh + lax.dot_general(wz_ref[0], plane_ref[1], NT, preferred_element_type=F32)
    mesh = mesh + lax.dot_general(wz_ref[1], plane_ref[0], NT, preferred_element_type=F32)
    waves = dot(front_ref[...], split_rows(mesh))
    span = SLOTS * GZ
    for gx in range(GX):
        first = gx * GY * GZ * CHUNK
        for part in range(2):
            rows = waves[(part * GX + gx) * span : (part * GX + gx + 1) * span]
            for r in range(HALF):
                out_ref[pl.ds(first + part * HALF + r, span, stride=CHUNK), :] = rows[:, r * LANES : (r + 1) * LANES]
        out_ref[first + span * CHUNK : first + GY * GZ * CHUNK] = jnp.zeros(((GY * GZ - span) * CHUNK, LANES), F32)


def turn(real, imag, cos, sin):
    return real * cos - imag * sin, real * sin + imag * cos


def plane_kernel(in_ref, influence_ref, mixes_ref, turns_ref, out_ref, real_ref, imag_ref, real_back_ref, imag_back_ref):
    def lanes_x_table(group):
        shift = group * PX * STEP_Y % LANES
        pieces = []
        for first in range(0, 512, LANES):
            if shift:
                pieces.append(mixes_ref[first + LANES - shift : first + LANES])
            pieces.append(mixes_ref[first : first + LANES - shift])
        table = jnp.concatenate(pieces, axis=0)
        return table[:256], table[256:]

    lanes_y_table = mixes_ref[512:768], mixes_ref[768:1024]
    first = 1024
    left_x, left_xh = mixes_ref[first : first + 64, :192], mixes_ref[first + 64 : first + 128, :192]
    left_y, left_yh = mixes_ref[first + 128 : first + 208, :240], mixes_ref[first + 208 : first + 288, :240]
    cos_x, sin_x = [
        jnp.concatenate([turns_ref[(i * HALF + r) * 32 : (i * HALF + r + 1) * 32] for r in range(HALF)], axis=1)
        for i in range(2)
    ]
    cos_y, sin_y = turns_ref[256:296], turns_ref[296:336]

    def lane(value, k):
        return value[:, k * LANES : (k + 1) * LANES]

    def chunk_rows(gx, q, part, r):
        return pl.ds((gx * GY + q) * GZ * CHUNK + part * HALF + r, GZ, stride=CHUNK)

    turned = []
    for q in range(GY):
        rows = [
            jnp.concatenate([in_ref[chunk_rows(gx, q, part, r), :] for r in range(HALF)], axis=1)
            for part in range(2)
            for gx in range(GX)
        ]
        mixed = dot(left_x, split_rows(jnp.concatenate(rows, axis=0)))
        turned.append(turn(mixed[:32], mixed[32:], cos_x, sin_x))
    lanes = lax.broadcasted_iota(jnp.int32, (1, 2 * LANES), 1) % LANES

    def placed(group, rows):
        first = group * PX * STEP_Y
        row = first // LANES
        if first % LANES + PX * STEP_Y <= LANES:
            return rows[row]
        return jnp.where(lanes >= first % LANES, rows[row], rows[row + 1])

    rows = [
        jnp.concatenate([jnp.concatenate([lane(re, r), lane(im, r)], axis=1) for re, im in turned], axis=0)
        for r in range(HALF)
    ]
    groups = [
        dot_lanes(dot, placed(g, rows), *lanes_x_table(g)) for g in range(GROUPS_Y)
    ]
    spill = groups[5]
    groups[0] = groups[0] + jnp.concatenate([spill[7 * 32 :], spill[: 7 * 32]], axis=0)
    for g in range(5):
        for q in range(GY):
            first = (g * GY + q) * STRIDE
            real_ref[first : first + 32] = lane(groups[g][q * 32 : (q + 1) * 32], 0)
            imag_ref[first : first + 32] = lane(groups[g][q * 32 : (q + 1) * 32], 1)

    batch = 32
    for k in range(0, 32, batch):
        picks = [pl.ds(k + i, 40, stride=STRIDE) for i in range(batch)]
        real = jnp.concatenate([real_ref[pick, :] for pick in picks], axis=1)
        imag = jnp.concatenate([imag_ref[pick, :] for pick in picks], axis=1)
        mixed = dot(left_y, split_rows(jnp.concatenate([real, imag], axis=0)))
        turned = [
            jnp.concatenate(turn(lane(mixed[:40], i), lane(mixed[40:], i), cos_y, sin_y), axis=1)
            for i in range(batch)
        ]
        spectrum = dot_lanes(dot, jnp.concatenate(turned, axis=0), *lanes_y_table)
        influence = influence_ref[k * 40 : (k + batch) * 40]
        spectrum = spectrum * jnp.concatenate([influence, influence], axis=1)
        back = dot_lanes(dot_nt, spectrum, *lanes_y_table)
        pieces = [
            turn(lane(back[i * 40 : (i + 1) * 40], 0), lane(back[i * 40 : (i + 1) * 40], 1), cos_y, -sin_y)
            for i in range(batch)
        ]
        stacked = jnp.concatenate(
            [jnp.concatenate([piece[part] for piece in pieces], axis=1) for part in range(2)], axis=0
        )
        inverse = dot(left_yh, split_rows(stacked))
        for i in range(batch):
            real_back_ref[picks[i], :] = lane(inverse[:40], i)
            imag_back_ref[picks[i], :] = lane(inverse[40:], i)

    groups = [
        jnp.concatenate(
            [
                jnp.concatenate(
                    [ref[(g * GY + q) * STRIDE : (g * GY + q) * STRIDE + 32] for q in range(GY)], axis=0
                )
                for ref in (real_back_ref, imag_back_ref)
            ],
            axis=1,
        )
        for g in range(5)
    ]
    groups.append(jnp.concatenate([groups[0][32:], groups[0][:32]], axis=0))
    pieces = [None] * HALF
    for g in range(GROUPS_Y):
        back = dot_lanes(dot_nt, groups[g], *lanes_x_table(g))
        first = g * PX * STEP_Y
        row = first // LANES
        pieces[row] = back if pieces[row] is None else jnp.where(lanes >= first % LANES, back, pieces[row])
        if first % LANES + PX * STEP_Y > LANES:
            pieces[row + 1] = back
    for q in range(GY):
        picked = [back[q * 32 : (q + 1) * 32] for back in pieces]
        real = jnp.concatenate([lane(back, 0) for back in picked], axis=1)
        imag = jnp.concatenate([lane(back, 1) for back in picked], axis=1)
        stacked = jnp.concatenate(turn(real, imag, cos_x, -sin_x), axis=0)
        inverse = dot(left_xh, split_rows(stacked))
        for part in range(2):
            for gx in range(GX):
                tile = inverse[(part * GX + gx) * GZ : (part * GX + gx + 1) * GZ]
                for r in range(HALF):
                    out_ref[chunk_rows(gx, q, part, r), :] = lane(tile, r)


def gather_sites(site_ref, shift, columns, mesh, wz_ref, finish):
    sites = site_ref.shape[1]
    unused, fraction, start_x, start_y, start_z = parameters(site_ref)
    values, slopes = spline_weights(fraction)
    offset_x = rows_below(start_x - shift, 16)
    offset_y = rows_below(start_y, GROUPS_Y * STEP_Y)
    weight_x, slope_x = place(values, 0, offset_x), place(slopes, 0, offset_x)
    weight_y, slope_y = place(values, 1, offset_y), place(slopes, 1, offset_y)
    for block in range(0, M, 16):
        offset = z_offset(start_z, block, 16)
        for kind, coefficients in ((0, values), (1, slopes)):
            high, low = split(place(coefficients, 2, offset))
            for term, part in enumerate((high, high, low)):
                row = term * 256 + block if block < 256 else 768 + term * 64 + block - 256
                wz_ref[kind, row : row + 16] = part
    for kind in range(2):
        wz_ref[kind, 960:DEEP] = jnp.zeros((64, sites), BF16)
    width = 256
    for first in range(0, sites, width):
        lanes = slice(first, first + width)
        near = dot(mesh, wz_ref[0, :, lanes])
        near_slope = dot(mesh, wz_ref[1, :, lanes])
        sums = [jnp.zeros((STEP_Y, width), F32) for unused in range(4)]
        for g in range(GROUPS_Y):
            wy = weight_y[g * STEP_Y : (g + 1) * STEP_Y, lanes]
            sy = slope_y[g * STEP_Y : (g + 1) * STEP_Y, lanes]
            for x in range(columns):
                row = (g * columns + x) * STEP_Y
                value = near[row : row + STEP_Y]
                weighted = wy * value
                wx = weight_x[x : x + 1, lanes]
                sums[0] = sums[0] + wx * weighted
                sums[1] = sums[1] + slope_x[x : x + 1, lanes] * weighted
                sums[2] = sums[2] + wx * (sy * value)
                sums[3] = sums[3] + wx * (wy * near_slope[row : row + STEP_Y])
        finish(lanes, [jnp.sum(part, axis=0, keepdims=True) for part in sums])


def deep_lanes(mesh):
    high, low = split(mesh)
    tail = jnp.concatenate([high[:, 256:M], low[:, 256:M], high[:, 256:M], jnp.zeros((mesh.shape[0], 64), BF16)], axis=1)
    return jnp.concatenate([high[:, :256], low[:, :256], high[:, :256], tail], axis=1)


def near_kernel(in_ref, near_ref, back_ref, mesh_ref, part_ref, wz_ref):
    span = SLOTS * GZ
    rows = [
        jnp.concatenate(
            [in_ref[pl.ds(gx * GY * GZ * CHUNK + part * HALF + r, span, stride=CHUNK), :] for r in range(HALF)],
            axis=1,
        )
        for part in range(2)
        for gx in range(GX)
    ]
    mesh = dot(back_ref[...], split_rows(jnp.concatenate(rows, axis=0)))
    mesh = jnp.transpose(mesh)[:CELLS]
    mesh_ref[...] = deep_lanes(mesh)
    edge = [mesh[g * PX * STEP_Y : g * PX * STEP_Y + 5 * STEP_Y] for g in range(GROUPS_Y)]
    edge = deep_lanes(jnp.concatenate(edge, axis=0))

    def finish(lanes, totals):
        for i in range(4):
            part_ref[i : i + 1, lanes] = totals[i]

    gather_sites(near_ref, PX, 5, edge, wz_ref, finish)


def own_kernel(mesh_ref, own_ref, part_ref, wz_ref):
    def finish(lanes, totals):
        for i in range(4):
            part_ref[i : i + 1, lanes] = totals[i]

    gather_sites(own_ref, 0, PX, mesh_ref[...], wz_ref, finish)


PLANE_SCRATCH = [pltpu.VMEM((40 * STRIDE, LANES), F32) for unused in range(4)]
LIMIT = pltpu.CompilerParams(vmem_limit_bytes=24 * 1024 * 1024)


def exchange(chunks):
    flat = chunks.reshape(GX * GY * GZ, 1, CHUNK * LANES)
    return lax.all_to_all(flat, ("gx", "gy", "gz"), 0, 0, tiled=True).reshape(ROWS, LANES)


def influence_along_x(planes):
    groups = [[2 * x + half for x in range(4)] for half in range(2)]
    flat = planes.reshape(GY // 2, 1, 2 * PLANE_ROWS * LANES)
    planes = lax.all_to_all(flat, "gy", 0, 0, tiled=True, axis_index_groups=groups)
    return planes.reshape(GY // 2, 2, PLANE_ROWS, LANES)


def widen_kernel(in_ref, out_ref):
    out_ref[:, :80] = in_ref[...]
    out_ref[:, 80:] = jnp.zeros((1280, LANES - 80), F32)


def influence_layout(planes):
    half = lax.axis_index("gy") % 2
    kept = lax.dynamic_index_in_dim(planes, half, 1, keepdims=False)
    sent = lax.dynamic_index_in_dim(planes, 1 - half, 1, keepdims=False)
    other = lax.ppermute(sent, "gy", [(s, s ^ 1) for s in range(SLOTS)])
    pair = [jnp.where(half == 0, kept, other), jnp.where(half == 0, other, kept)]
    planes = jnp.stack(pair, axis=1).reshape(GY, PLANE_ROWS, LANES)
    tail = planes[:, 2 * PY : 2 * PY + PY // 2]
    tail = jnp.concatenate([tail[:, :, : LANES // 2], tail[:, :, LANES // 2 :]], axis=1)
    planes = jnp.concatenate([planes[:, :PY], planes[:, PY : 2 * PY], tail], axis=2)
    planes = planes.reshape(10, 32, 8, 40).transpose(1, 3, 0, 2).reshape(1280, 80)
    return pl.pallas_call(
        widen_kernel,
        out_shape=jax.ShapeDtypeStruct((1280, LANES), F32),
        compiler_params=LIMIT,
        cost_estimate=pl.CostEstimate(flops=100000000000, bytes_accessed=1000000, transcendentals=0),
        name="widen",
    )(planes)


def body(charges, mesh_start, mesh_frac, influence):
    table = {name: jnp.asarray(value) for name, value in tables().items()}
    sites = charges.shape[0]
    own, planes = pl.pallas_call(
        pack_kernel,
        out_shape=(
            jax.ShapeDtypeStruct((8, sites), F32),
            jax.ShapeDtypeStruct((GY * PLANE_ROWS, LANES), F32),
        ),
        in_specs=[pl.BlockSpec(memory_space=pl.ANY)] * 4,
        scratch_shapes=[
            pltpu.VMEM((1, sites), F32),
            pltpu.VMEM((3, sites), jnp.int32),
            pltpu.VMEM((3, sites), F32),
            pltpu.VMEM((SLOTS, PY, M), F32),
            pltpu.SemaphoreType.DMA((4,)),
        ],
        compiler_params=pltpu.CompilerParams(vmem_limit_bytes=60 * 1024 * 1024),
        name="pack",
    )(charges.reshape(1, sites), mesh_start, mesh_frac, influence)
    near = lax.ppermute(own, ("gx", "gz"), [(p, (p + 1) % PENCILS) for p in range(PENCILS)])
    planes = influence_along_x(planes)
    chunks = pl.pallas_call(
        spread_kernel,
        out_shape=jax.ShapeDtypeStruct((ROWS, LANES), F32),
        scratch_shapes=[pltpu.VMEM((2, M, 2 * sites), BF16), pltpu.VMEM((2, WIDE, 2 * sites), BF16)],
        compiler_params=LIMIT,
        cost_estimate=pl.CostEstimate(flops=40000000000, bytes_accessed=10000000, transcendentals=0),
        name="spread",
    )(own, near, table["front"])
    planes, chunks = lax.optimization_barrier((planes, chunks))
    planes = influence_layout(planes)
    chunks = exchange(chunks)
    chunks = pl.pallas_call(
        plane_kernel,
        out_shape=jax.ShapeDtypeStruct((ROWS, LANES), F32),
        scratch_shapes=PLANE_SCRATCH,
        compiler_params=LIMIT,
        name="plane",
    )(
        chunks,
        planes,
        table["mixes"],
        table["turns"],
    )
    chunks = exchange(chunks)
    mesh, edge = pl.pallas_call(
        near_kernel,
        out_shape=(jax.ShapeDtypeStruct((CELLS, DEEP), BF16), jax.ShapeDtypeStruct((4, sites), F32)),
        scratch_shapes=[pltpu.VMEM((2, DEEP, sites), BF16)],
        compiler_params=LIMIT,
        name="near",
    )(chunks, near, table["back"])
    edge = lax.ppermute(edge, ("gx", "gz"), [(p, (p - 1) % PENCILS) for p in range(PENCILS)])
    inner = pl.pallas_call(
        own_kernel,
        out_shape=jax.ShapeDtypeStruct((4, sites), F32),
        scratch_shapes=[pltpu.VMEM((2, DEEP, sites), BF16)],
        compiler_params=LIMIT,
        name="own",
    )(mesh, own)
    potential, forces = pl.pallas_call(
        finish_kernel,
        out_shape=(jax.ShapeDtypeStruct((1, sites), F32), jax.ShapeDtypeStruct((3, sites), F32)),
        compiler_params=LIMIT,
        name="finish",
    )(own, edge, inner)
    return potential.reshape(sites), forces


def solution(mesh):
    return jax.shard_map(
        body,
        mesh=mesh,
        in_specs=(
            P(("gx", "gy", "gz")),
            P(None, ("gx", "gy", "gz")),
            P(None, ("gx", "gy", "gz")),
            P(("gx", "gz"), "gy", None),
        ),
        out_specs=(P(("gx", "gy", "gz")), P(None, ("gx", "gy", "gz"))),
        check_vma=False,
    )
```

```python
import functools
import math

import jax
import jax.numpy as jnp
import ml_dtypes
import numpy as np
from jax import lax
from jax.experimental import pallas as pl
from jax.experimental.pallas import tpu as pltpu
from jax.sharding import PartitionSpec as P

M = 320
PX = 10
PY = 40
GX, GY, GZ = 4, 8, 8
PENCILS = GX * GZ
SLOTS = 6
CHUNK = 8
HALF = CHUNK // 2
ROWS = GX * GY * GZ * CHUNK
GROUPS_Y = 6
STEP_Y = 8
LANES = 128
WIDE = HALF * LANES
CELLS = GROUPS_Y * PX * STEP_Y
DEEP = 1024
STRIDE = 40
PLANE_ROWS = 104
BF16 = jnp.bfloat16
F32 = jnp.float32
NT = (((1,), (1,)), ((), ()))


def halves(table):
    high = table.astype(ml_dtypes.bfloat16)
    low = (table - high.astype(np.float64)).astype(ml_dtypes.bfloat16)
    return high, low


def left_table(table):
    high, low = halves(table)
    return np.concatenate([high, high, low], axis=1)


def angles(rows, columns, period):
    phase = np.mod(np.outer(rows, columns), period)
    return phase * (2.0 * math.pi / period)


def complex_left(angle):
    c, s = np.cos(angle), np.sin(angle)
    return np.block([[c, s], [-s, c]])


def lanes_complex(angle, live):
    c, s = np.cos(angle) * live, np.sin(angle) * live
    return np.block([[c, -s], [s, c]])


def lanes_x_table():
    slot = np.arange(LANES) // STEP_Y
    y = np.arange(LANES) % STEP_Y
    live = (slot < PX)[:, None] & (y[:, None] == y[None, :]) & (slot < 10)[None, :]
    return lanes_complex(angles(slot, slot, 10), live)


def lanes_y_table():
    lane = np.arange(LANES)
    live = (lane[:, None] // 8 == lane[None, :] // 8) & (lane < 80)[:, None]
    return lanes_complex(angles(lane % 8, lane % 8, 8), live)


def wave_slots():
    waves = np.zeros((GX, SLOTS, GZ), np.int64)
    fold = np.zeros((GX, SLOTS, GZ))
    for gx in range(GX):
        for gz in range(GZ):
            p = gx * GZ + gz
            upper = p >= PENCILS // 2
            for j in range(SLOTS):
                wave = 10 * p + j
                if (j < 5 and not upper) or (j > 0 and upper) or wave == M // 2:
                    waves[gx, j, gz] = wave
                    fold[gx, j, gz] = 1.0 if wave in (0, M // 2) else 2.0
    return waves.reshape(-1), fold.reshape(-1)


@functools.lru_cache(maxsize=None)
def tables():
    waves, fold = wave_slots()
    angle = angles(waves, np.arange(M), M)
    live = (fold > 0)[:, None]
    front = np.concatenate([np.cos(angle) * live, -np.sin(angle) * live])
    scale = fold[:, None] / float(M * M * M)
    back = np.concatenate([np.cos(angle) * scale, -np.sin(angle) * scale]).T
    back = np.pad(back, [(0, 384 - M), (0, 0)])
    left_x = complex_left(angles(np.arange(32), np.arange(32), 32))
    order = np.concatenate([5 * np.arange(GY) + g for g in range(5)])
    left_y = complex_left(angles(np.arange(40), order, 40))
    lanes_x = lanes_x_table()
    lanes_y = lanes_y_table()
    lane = np.arange(LANES)
    turn_x = angles(np.arange(32), np.arange(WIDE) // STEP_Y % PX, M)
    turn_y = angles(np.arange(40), lane % 8, M)
    parts = [part for table in (lanes_x, lanes_y) for part in halves(table)]
    for table in (left_x, left_x.T, left_y, left_y.T):
        left = left_table(table)
        parts.append(np.pad(left, [(0, 0), (0, 256 - left.shape[1])]))
    turns = [np.cos(turn_x), -np.sin(turn_x), np.cos(turn_y), -np.sin(turn_y)]
    turns = [part[:, i : i + LANES] for part in turns for i in range(0, part.shape[1], LANES)]
    return dict(
        front=left_table(front),
        back=left_table(back),
        mixes=np.concatenate(parts, axis=0),
        turns=np.concatenate(turns, axis=0).astype(np.float32),
    )


def split(value):
    high = value.astype(BF16)
    low = (value - high.astype(F32)).astype(BF16)
    return high, low


def split_rows(value):
    high, low = split(value)
    return jnp.concatenate([high, low, high], axis=0)


def split_lanes(value):
    high, low = split(value)
    return jnp.concatenate([high, low, high], axis=1)


def dot(left, right):
    return jnp.dot(left, right, preferred_element_type=F32)


def dot_nt(left, right):
    return lax.dot_general(left, right, NT, preferred_element_type=F32)


def dot_lanes(form, value, high_table, low_table):
    high, low = split(value)
    return form(high, high_table) + form(low, high_table) + form(high, low_table)


def spline_weights(fraction):
    values = [1.0 - fraction, fraction] + [jnp.zeros_like(fraction) for unused in range(4)]
    for order in range(3, 6):
        factor = 1.0 / (order - 1)
        values[order - 1] = factor * fraction * values[order - 2]
        for offset in range(1, order - 1):
            values[order - offset - 1] = factor * (
                (fraction + offset) * values[order - offset - 2]
                + (order - offset - fraction) * values[order - offset - 1]
            )
        values[0] = factor * (1.0 - fraction) * values[0]
    slopes = [-values[0]] + [values[offset - 1] - values[offset] for offset in range(1, 6)]
    factor = 1.0 / 5.0
    values[5] = factor * fraction * values[4]
    for offset in range(1, 5):
        values[5 - offset] = factor * (
            (fraction + offset) * values[4 - offset] + (6 - offset - fraction) * values[5 - offset]
        )
    values[0] = factor * (1.0 - fraction) * values[0]
    return values, slopes


def place(coefficients, dimension, offset):
    result = jnp.zeros(offset.shape, F32)
    for j in range(6):
        result = jnp.where(offset == j, coefficients[j][dimension : dimension + 1], result)
    return result


def rows_below(start, length):
    return lax.broadcasted_iota(jnp.int32, (length, start.shape[1]), 0) - start


def parameters(site_ref):
    whole = site_ref[4:7].astype(jnp.int32)
    return site_ref[0:1], site_ref[1:4], whole[0:1], whole[1:2], whole[2:3]


def z_offset_short(start, first, length):
    offset = lax.broadcasted_iota(jnp.int16, (length, start.shape[1]), 0) + jnp.int16(first) - start
    return jnp.where(offset < 0, offset + jnp.int16(M), offset)


def place_split(halved, offset):
    results = [jnp.zeros(offset.shape, BF16) for unused in range(2)]
    for j in range(6):
        here = offset == j
        results = [jnp.where(here, halved[j][i], results[i]) for i in range(2)]
    return results


def pack_kernel(
    charge_in, start_in, frac_in, influence_in, out_ref, planes_ref, charge_ref, start_ref, frac_ref, slab_ref, sems
):
    copies = [
        pltpu.make_async_copy(start_in, start_ref, sems.at[0]),
        pltpu.make_async_copy(frac_in, frac_ref, sems.at[1]),
        pltpu.make_async_copy(charge_in, charge_ref, sems.at[2]),
        pltpu.make_async_copy(influence_in.at[0:SLOTS], slab_ref, sems.at[3]),
    ]
    for copy in copies:
        copy.start()
    for copy in copies[:3]:
        copy.wait()
    out_ref[0:1] = charge_ref[...]
    out_ref[1:4] = frac_ref[...]
    out_ref[4:5] = lax.rem(start_ref[0:1], PX).astype(F32)
    out_ref[5:6] = lax.rem(start_ref[1:2], PY).astype(F32)
    out_ref[6:7] = start_ref[2:3].astype(F32)
    out_ref[7:8] = jnp.zeros(charge_ref.shape, F32)
    copies[3].wait()
    half = PY // 2
    for j in range(SLOTS):
        first = j * PLANE_ROWS
        tail = slab_ref[j, :, 2 * LANES : M]
        planes_ref[first : first + PY] = slab_ref[j, :, :LANES]
        planes_ref[first + PY : first + 2 * PY] = slab_ref[j, :, LANES : 2 * LANES]
        planes_ref[first + 2 * PY : first + 2 * PY + half] = jnp.concatenate([tail[:half], tail[half:]], axis=1)
        planes_ref[first + 2 * PY + half : first + PLANE_ROWS] = jnp.zeros((PLANE_ROWS - 2 * PY - half, LANES), F32)
    planes_ref[SLOTS * PLANE_ROWS :] = jnp.zeros(((GY - SLOTS) * PLANE_ROWS, LANES), F32)


def finish_kernel(own_ref, edge_ref, inner_ref, potential_ref, forces_ref):
    total = inner_ref[...] + edge_ref[...]
    potential_ref[...] = total[0:1]
    forces_ref[...] = -own_ref[0:1] * total[1:4]


def spread_kernel(own_ref, near_ref, front_ref, out_ref, wz_ref, plane_ref):
    sites = own_ref.shape[1]
    mesh = None
    for source in range(2):
        charge, fraction, start_x, start_y, start_z = parameters((own_ref, near_ref)[source])
        values, unused = spline_weights(fraction)
        weight_x = place(values, 0, rows_below(start_x - source * PX, 16)) * charge
        weight_y = place(values, 1, rows_below(start_y, GROUPS_Y * STEP_Y))
        for part in range(0, sites, 256):
            picked = slice(part, part + 256)
            lanes = slice(source * sites + part, source * sites + part + 256)
            halved = [split(value[2:3, picked]) for value in values]
            short_z = start_z[:, picked].astype(jnp.int16)
            for block in range(0, M, 16):
                high, low = place_split(halved, z_offset_short(short_z, block, 16))
                wz_ref[0, block : block + 16, lanes] = high
                wz_ref[1, block : block + 16, lanes] = low
            for cell in range(0, WIDE, 16):
                pair = []
                for first in (cell, cell + STEP_Y):
                    if first < CELLS:
                        g, x = first // (PX * STEP_Y), first // STEP_Y % PX
                        near = weight_y[g * STEP_Y : (g + 1) * STEP_Y, picked]
                        pair.append(near * jnp.broadcast_to(weight_x[x : x + 1, picked], near.shape))
                    else:
                        pair.append(jnp.zeros((STEP_Y, 256), F32))
                high, low = split(jnp.concatenate(pair, axis=0))
                plane_ref[0, cell : cell + 16, lanes] = high
                plane_ref[1, cell : cell + 16, lanes] = low
            for i, j in ((0, 0), (0, 1), (1, 0)):
                term = dot_nt(wz_ref[i, :, lanes], plane_ref[j, :, lanes])
                mesh = term if mesh is None else mesh + term
    waves = dot(front_ref[...], split_rows(mesh))
    span = SLOTS * GZ
    for gx in range(GX):
        first = gx * GY * GZ * CHUNK
        for part in range(2):
            rows = waves[(part * GX + gx) * span : (part * GX + gx + 1) * span]
            for r in range(HALF):
                out_ref[pl.ds(first + part * HALF + r, span, stride=CHUNK), :] = rows[:, r * LANES : (r + 1) * LANES]
        out_ref[first + span * CHUNK : first + GY * GZ * CHUNK] = jnp.zeros(((GY * GZ - span) * CHUNK, LANES), F32)


def turn(real, imag, cos, sin):
    return real * cos - imag * sin, real * sin + imag * cos


def plane_kernel(in_ref, influence_ref, mixes_ref, turns_ref, out_ref, real_ref, imag_ref, real_back_ref, imag_back_ref):
    def lanes_x_table(group):
        shift = group * PX * STEP_Y % LANES
        pieces = []
        for first in range(0, 512, LANES):
            if shift:
                pieces.append(mixes_ref[first + LANES - shift : first + LANES])
            pieces.append(mixes_ref[first : first + LANES - shift])
        table = jnp.concatenate(pieces, axis=0)
        return table[:256], table[256:]

    lanes_y_table = mixes_ref[512:768], mixes_ref[768:1024]
    first = 1024
    left_x, left_xh = mixes_ref[first : first + 64, :192], mixes_ref[first + 64 : first + 128, :192]
    left_y, left_yh = mixes_ref[first + 128 : first + 208, :240], mixes_ref[first + 208 : first + 288, :240]
    cos_x, sin_x = [
        jnp.concatenate([turns_ref[(i * HALF + r) * 32 : (i * HALF + r + 1) * 32] for r in range(HALF)], axis=1)
        for i in range(2)
    ]
    cos_y, sin_y = turns_ref[256:296], turns_ref[296:336]

    def lane(value, k):
        return value[:, k * LANES : (k + 1) * LANES]

    def chunk_rows(gx, q, part, r):
        return pl.ds((gx * GY + q) * GZ * CHUNK + part * HALF + r, GZ, stride=CHUNK)

    turned = []
    for q in range(GY):
        rows = [
            jnp.concatenate([in_ref[chunk_rows(gx, q, part, r), :] for r in range(HALF)], axis=1)
            for part in range(2)
            for gx in range(GX)
        ]
        mixed = dot(left_x, split_rows(jnp.concatenate(rows, axis=0)))
        turned.append(turn(mixed[:32], mixed[32:], cos_x, sin_x))
    lanes = lax.broadcasted_iota(jnp.int32, (1, 2 * LANES), 1) % LANES

    def placed(group, rows):
        first = group * PX * STEP_Y
        row = first // LANES
        if first % LANES + PX * STEP_Y <= LANES:
            return rows[row]
        return jnp.where(lanes >= first % LANES, rows[row], rows[row + 1])

    rows = [
        jnp.concatenate([jnp.concatenate([lane(re, r), lane(im, r)], axis=1) for re, im in turned], axis=0)
        for r in range(HALF)
    ]
    groups = [
        dot_lanes(dot, placed(g, rows), *lanes_x_table(g)) for g in range(GROUPS_Y)
    ]
    spill = groups[5]
    groups[0] = groups[0] + jnp.concatenate([spill[7 * 32 :], spill[: 7 * 32]], axis=0)
    for g in range(5):
        for q in range(GY):
            first = (g * GY + q) * STRIDE
            real_ref[first : first + 32] = lane(groups[g][q * 32 : (q + 1) * 32], 0)
            imag_ref[first : first + 32] = lane(groups[g][q * 32 : (q + 1) * 32], 1)

    batch = 32
    for k in range(0, 32, batch):
        picks = [pl.ds(k + i, 40, stride=STRIDE) for i in range(batch)]
        real = jnp.concatenate([real_ref[pick, :] for pick in picks], axis=1)
        imag = jnp.concatenate([imag_ref[pick, :] for pick in picks], axis=1)
        mixed = dot(left_y, split_rows(jnp.concatenate([real, imag], axis=0)))
        turned = [
            jnp.concatenate(turn(lane(mixed[:40], i), lane(mixed[40:], i), cos_y, sin_y), axis=1)
            for i in range(batch)
        ]
        spectrum = dot_lanes(dot, jnp.concatenate(turned, axis=0), *lanes_y_table)
        influence = influence_ref[k * 40 : (k + batch) * 40]
        spectrum = spectrum * jnp.concatenate([influence, influence], axis=1)
        back = dot_lanes(dot_nt, spectrum, *lanes_y_table)
        pieces = [
            turn(lane(back[i * 40 : (i + 1) * 40], 0), lane(back[i * 40 : (i + 1) * 40], 1), cos_y, -sin_y)
            for i in range(batch)
        ]
        stacked = jnp.concatenate(
            [jnp.concatenate([piece[part] for piece in pieces], axis=1) for part in range(2)], axis=0
        )
        inverse = dot(left_yh, split_rows(stacked))
        for i in range(batch):
            real_back_ref[picks[i], :] = lane(inverse[:40], i)
            imag_back_ref[picks[i], :] = lane(inverse[40:], i)

    groups = [
        jnp.concatenate(
            [
                jnp.concatenate(
                    [ref[(g * GY + q) * STRIDE : (g * GY + q) * STRIDE + 32] for q in range(GY)], axis=0
                )
                for ref in (real_back_ref, imag_back_ref)
            ],
            axis=1,
        )
        for g in range(5)
    ]
    groups.append(jnp.concatenate([groups[0][32:], groups[0][:32]], axis=0))
    pieces = [None] * HALF
    for g in range(GROUPS_Y):
        back = dot_lanes(dot_nt, groups[g], *lanes_x_table(g))
        first = g * PX * STEP_Y
        row = first // LANES
        pieces[row] = back if pieces[row] is None else jnp.where(lanes >= first % LANES, back, pieces[row])
        if first % LANES + PX * STEP_Y > LANES:
            pieces[row + 1] = back
    for q in range(GY):
        picked = [back[q * 32 : (q + 1) * 32] for back in pieces]
        real = jnp.concatenate([lane(back, 0) for back in picked], axis=1)
        imag = jnp.concatenate([lane(back, 1) for back in picked], axis=1)
        stacked = jnp.concatenate(turn(real, imag, cos_x, -sin_x), axis=0)
        inverse = dot(left_xh, split_rows(stacked))
        for part in range(2):
            for gx in range(GX):
                tile = inverse[(part * GX + gx) * GZ : (part * GX + gx + 1) * GZ]
                for r in range(HALF):
                    out_ref[chunk_rows(gx, q, part, r), :] = lane(tile, r)


def gather_sites(site_ref, shift, columns, mesh, wz_ref, finish):
    sites = site_ref.shape[1]
    unused, fraction, start_x, start_y, start_z = parameters(site_ref)
    values, slopes = spline_weights(fraction)
    offset_x = rows_below(start_x - shift, 16)
    offset_y = rows_below(start_y, GROUPS_Y * STEP_Y)
    weight_x, slope_x = place(values, 0, offset_x), place(slopes, 0, offset_x)
    weight_y, slope_y = place(values, 1, offset_y), place(slopes, 1, offset_y)
    short_z = start_z.astype(jnp.int16)
    halved = [[split(value[2:3]) for value in coefficients] for coefficients in (values, slopes)]
    for block in range(0, M, 16):
        offset = z_offset_short(short_z, block, 16)
        for kind in range(2):
            high, low = place_split(halved[kind], offset)
            for term, part in enumerate((high, high, low)):
                row = term * 256 + block if block < 256 else 768 + term * 64 + block - 256
                wz_ref[kind, row : row + 16] = part
    for kind in range(2):
        wz_ref[kind, 960:DEEP] = jnp.zeros((64, sites), BF16)
    width = 256
    for first in range(0, sites, width):
        lanes = slice(first, first + width)
        near = dot(mesh, wz_ref[0, :, lanes])
        near_slope = dot(mesh, wz_ref[1, :, lanes])
        sums = [jnp.zeros((STEP_Y, width), F32) for unused in range(4)]
        for g in range(GROUPS_Y):
            wy = weight_y[g * STEP_Y : (g + 1) * STEP_Y, lanes]
            sy = slope_y[g * STEP_Y : (g + 1) * STEP_Y, lanes]
            for x in range(columns):
                row = (g * columns + x) * STEP_Y
                value = near[row : row + STEP_Y]
                weighted = wy * value
                wx = weight_x[x : x + 1, lanes]
                sums[0] = sums[0] + wx * weighted
                sums[1] = sums[1] + slope_x[x : x + 1, lanes] * weighted
                sums[2] = sums[2] + wx * (sy * value)
                sums[3] = sums[3] + wx * (wy * near_slope[row : row + STEP_Y])
        finish(lanes, [jnp.sum(part, axis=0, keepdims=True) for part in sums])


def deep_lanes(mesh):
    high, low = split(mesh)
    tail = jnp.concatenate([high[:, 256:M], low[:, 256:M], high[:, 256:M], jnp.zeros((mesh.shape[0], 64), BF16)], axis=1)
    return jnp.concatenate([high[:, :256], low[:, :256], high[:, :256], tail], axis=1)


def near_kernel(in_ref, near_ref, back_ref, mesh_ref, part_ref, wz_ref):
    span = SLOTS * GZ
    rows = [
        jnp.concatenate(
            [in_ref[pl.ds(gx * GY * GZ * CHUNK + part * HALF + r, span, stride=CHUNK), :] for r in range(HALF)],
            axis=1,
        )
        for part in range(2)
        for gx in range(GX)
    ]
    mesh = dot(back_ref[...], split_rows(jnp.concatenate(rows, axis=0)))
    mesh = jnp.transpose(mesh)[:CELLS]
    mesh_ref[...] = deep_lanes(mesh)
    edge = [mesh[g * PX * STEP_Y : g * PX * STEP_Y + 5 * STEP_Y] for g in range(GROUPS_Y)]
    edge = deep_lanes(jnp.concatenate(edge, axis=0))

    def finish(lanes, totals):
        for i in range(4):
            part_ref[i : i + 1, lanes] = totals[i]

    gather_sites(near_ref, PX, 5, edge, wz_ref, finish)


def own_kernel(mesh_ref, own_ref, part_ref, wz_ref):
    def finish(lanes, totals):
        for i in range(4):
            part_ref[i : i + 1, lanes] = totals[i]

    gather_sites(own_ref, 0, PX, mesh_ref[...], wz_ref, finish)


PLANE_SCRATCH = [pltpu.VMEM((40 * STRIDE, LANES), F32) for unused in range(4)]
LIMIT = pltpu.CompilerParams(vmem_limit_bytes=24 * 1024 * 1024)


def exchange(chunks):
    flat = chunks.reshape(GX * GY * GZ, 1, CHUNK * LANES)
    return lax.all_to_all(flat, ("gx", "gy", "gz"), 0, 0, tiled=True).reshape(ROWS, LANES)


def influence_along_x(planes):
    groups = [[2 * x + half for x in range(4)] for half in range(2)]
    flat = planes.reshape(GY // 2, 1, 2 * PLANE_ROWS * LANES)
    planes = lax.all_to_all(flat, "gy", 0, 0, tiled=True, axis_index_groups=groups)
    return planes.reshape(GY // 2, 2, PLANE_ROWS, LANES)


def widen_kernel(in_ref, out_ref):
    out_ref[:, :80] = in_ref[...]
    out_ref[:, 80:] = jnp.zeros((1280, LANES - 80), F32)


def influence_layout(planes):
    half = lax.axis_index("gy") % 2
    kept = lax.dynamic_index_in_dim(planes, half, 1, keepdims=False)
    sent = lax.dynamic_index_in_dim(planes, 1 - half, 1, keepdims=False)
    other = lax.ppermute(sent, "gy", [(s, s ^ 1) for s in range(SLOTS)])
    pair = [jnp.where(half == 0, kept, other), jnp.where(half == 0, other, kept)]
    planes = jnp.stack(pair, axis=1).reshape(GY, PLANE_ROWS, LANES)
    tail = planes[:, 2 * PY : 2 * PY + PY // 2]
    tail = jnp.concatenate([tail[:, :, : LANES // 2], tail[:, :, LANES // 2 :]], axis=1)
    planes = jnp.concatenate([planes[:, :PY], planes[:, PY : 2 * PY], tail], axis=2)
    planes = planes.reshape(10, 32, 8, 40).transpose(1, 3, 0, 2).reshape(1280, 80)
    return pl.pallas_call(
        widen_kernel,
        out_shape=jax.ShapeDtypeStruct((1280, LANES), F32),
        compiler_params=LIMIT,
        cost_estimate=pl.CostEstimate(flops=100000000000, bytes_accessed=1000000, transcendentals=0),
        name="widen",
    )(planes)


def body(charges, mesh_start, mesh_frac, influence):
    table = {name: jnp.asarray(value) for name, value in tables().items()}
    sites = charges.shape[0]
    own, planes = pl.pallas_call(
        pack_kernel,
        out_shape=(
            jax.ShapeDtypeStruct((8, sites), F32),
            jax.ShapeDtypeStruct((GY * PLANE_ROWS, LANES), F32),
        ),
        in_specs=[pl.BlockSpec(memory_space=pl.ANY)] * 4,
        scratch_shapes=[
            pltpu.VMEM((1, sites), F32),
            pltpu.VMEM((3, sites), jnp.int32),
            pltpu.VMEM((3, sites), F32),
            pltpu.VMEM((SLOTS, PY, M), F32),
            pltpu.SemaphoreType.DMA((4,)),
        ],
        compiler_params=pltpu.CompilerParams(vmem_limit_bytes=60 * 1024 * 1024),
        name="pack",
    )(charges.reshape(1, sites), mesh_start, mesh_frac, influence)
    near = lax.ppermute(own, ("gx", "gz"), [(p, (p + 1) % PENCILS) for p in range(PENCILS)])
    planes = influence_along_x(planes)
    chunks = pl.pallas_call(
        spread_kernel,
        out_shape=jax.ShapeDtypeStruct((ROWS, LANES), F32),
        scratch_shapes=[pltpu.VMEM((2, M, 2 * sites), BF16), pltpu.VMEM((2, WIDE, 2 * sites), BF16)],
        compiler_params=LIMIT,
        cost_estimate=pl.CostEstimate(flops=40000000000, bytes_accessed=10000000, transcendentals=0),
        name="spread",
    )(own, near, table["front"])
    planes, chunks = lax.optimization_barrier((planes, chunks))
    planes = influence_layout(planes)
    chunks = exchange(chunks)
    chunks = pl.pallas_call(
        plane_kernel,
        out_shape=jax.ShapeDtypeStruct((ROWS, LANES), F32),
        scratch_shapes=PLANE_SCRATCH,
        compiler_params=LIMIT,
        name="plane",
    )(
        chunks,
        planes,
        table["mixes"],
        table["turns"],
    )
    chunks = exchange(chunks)
    mesh, edge = pl.pallas_call(
        near_kernel,
        out_shape=(jax.ShapeDtypeStruct((CELLS, DEEP), BF16), jax.ShapeDtypeStruct((4, sites), F32)),
        scratch_shapes=[pltpu.VMEM((2, DEEP, sites), BF16)],
        compiler_params=LIMIT,
        name="near",
    )(chunks, near, table["back"])
    edge = lax.ppermute(edge, ("gx", "gz"), [(p, (p - 1) % PENCILS) for p in range(PENCILS)])
    inner = pl.pallas_call(
        own_kernel,
        out_shape=jax.ShapeDtypeStruct((4, sites), F32),
        scratch_shapes=[pltpu.VMEM((2, DEEP, sites), BF16)],
        compiler_params=LIMIT,
        name="own",
    )(mesh, own)
    potential, forces = pl.pallas_call(
        finish_kernel,
        out_shape=(jax.ShapeDtypeStruct((1, sites), F32), jax.ShapeDtypeStruct((3, sites), F32)),
        compiler_params=LIMIT,
        name="finish",
    )(own, edge, inner)
    return potential.reshape(sites), forces


def solution(mesh):
    return jax.shard_map(
        body,
        mesh=mesh,
        in_specs=(
            P(("gx", "gy", "gz")),
            P(None, ("gx", "gy", "gz")),
            P(None, ("gx", "gy", "gz")),
            P(("gx", "gz"), "gy", None),
        ),
        out_specs=(P(("gx", "gy", "gz")), P(None, ("gx", "gy", "gz"))),
        check_vma=False,
    )
```

```python
import functools
import math

import jax
import jax.numpy as jnp
import ml_dtypes
import numpy as np
from jax import lax
from jax.experimental import pallas as pl
from jax.experimental.pallas import tpu as pltpu
from jax.sharding import PartitionSpec as P

M = 320
PX = 10
PY = 40
GX, GY, GZ = 4, 8, 8
PENCILS = GX * GZ
SLOTS = 6
CHUNK = 8
HALF = CHUNK // 2
ROWS = GX * GY * GZ * CHUNK
GROUPS_Y = 6
STEP_Y = 8
LANES = 128
WIDE = HALF * LANES
CELLS = GROUPS_Y * PX * STEP_Y
DEEP = 1024
STRIDE = 40
PLANE_ROWS = 104
SCALE_Y = 239.0
BF16 = jnp.bfloat16
F32 = jnp.float32
NT = (((1,), (1,)), ((), ()))


def halves(table):
    high = table.astype(ml_dtypes.bfloat16)
    low = (table - high.astype(np.float64)).astype(ml_dtypes.bfloat16)
    return high, low


def left_table(table):
    high, low = halves(table)
    return np.concatenate([high, high, low], axis=1)


def angles(rows, columns, period):
    phase = np.mod(np.outer(rows, columns), period)
    return phase * (2.0 * math.pi / period)


def complex_left(angle):
    c, s = np.cos(angle), np.sin(angle)
    return np.block([[c, s], [-s, c]])


def lanes_complex(angle, live):
    c, s = np.cos(angle) * live, np.sin(angle) * live
    return np.block([[c, -s], [s, c]])


def lanes_x_table():
    slot = np.arange(LANES) // STEP_Y
    y = np.arange(LANES) % STEP_Y
    live = (slot < PX)[:, None] & (y[:, None] == y[None, :]) & (slot < 10)[None, :]
    return lanes_complex(angles(slot, slot, 10), live)


def lanes_y_table():
    lane = np.arange(LANES)
    live = (lane[:, None] // 8 == lane[None, :] // 8) & (lane < 80)[:, None]
    return lanes_complex(angles(lane % 8, lane % 8, 8), live)


def wave_slots():
    waves = np.zeros((GX, SLOTS, GZ), np.int64)
    fold = np.zeros((GX, SLOTS, GZ))
    for gx in range(GX):
        for gz in range(GZ):
            p = gx * GZ + gz
            upper = p >= PENCILS // 2
            for j in range(SLOTS):
                wave = 10 * p + j
                if (j < 5 and not upper) or (j > 0 and upper) or wave == M // 2:
                    waves[gx, j, gz] = wave
                    fold[gx, j, gz] = 1.0 if wave in (0, M // 2) else 2.0
    return waves.reshape(-1), fold.reshape(-1)


@functools.lru_cache(maxsize=None)
def tables():
    waves, fold = wave_slots()
    angle = angles(waves, np.arange(M), M)
    live = (fold > 0)[:, None]
    front = np.concatenate([np.cos(angle) * live, -np.sin(angle) * live])
    scale = fold[:, None] / (float(M * M * M) * SCALE_Y**2)
    back = np.concatenate([np.cos(angle) * scale, -np.sin(angle) * scale]).T
    back = np.pad(back, [(0, 384 - M), (0, 0)])
    left_x = complex_left(angles(np.arange(32), np.arange(32), 32))
    order = np.concatenate([5 * np.arange(GY) + g for g in range(5)])
    left_y = complex_left(angles(np.arange(40), order, 40))
    lanes_x = lanes_x_table()
    lanes_y = lanes_y_table()
    lane = np.arange(LANES)
    turn_x = angles(np.arange(32), np.arange(WIDE) // STEP_Y % PX, M)
    turn_y = angles(np.arange(40), lane % 8, M)
    parts = [part for table in (lanes_x,) for part in halves(table)]
    parts.append(np.round(SCALE_Y * lanes_y).astype(ml_dtypes.bfloat16))
    for table in (left_x, left_x.T, left_y, left_y.T):
        left = left_table(table)
        parts.append(np.pad(left, [(0, 0), (0, 256 - left.shape[1])]))
    turns = [np.cos(turn_x), -np.sin(turn_x), np.cos(turn_y), -np.sin(turn_y)]
    turns = [part[:, i : i + LANES] for part in turns for i in range(0, part.shape[1], LANES)]
    return dict(
        front=left_table(front),
        back=left_table(back),
        mixes=np.concatenate(parts, axis=0),
        turns=np.concatenate(turns, axis=0).astype(np.float32),
    )


def split(value):
    high = value.astype(BF16)
    low = (value - high.astype(F32)).astype(BF16)
    return high, low


def split_rows(value):
    high, low = split(value)
    return jnp.concatenate([high, low, high], axis=0)


def split_lanes(value):
    high, low = split(value)
    return jnp.concatenate([high, low, high], axis=1)


def dot(left, right):
    return jnp.dot(left, right, preferred_element_type=F32)


def dot_nt(left, right):
    return lax.dot_general(left, right, NT, preferred_element_type=F32)


def dot_lanes(form, value, high_table, low_table):
    high, low = split(value)
    return form(high, high_table) + form(low, high_table) + form(high, low_table)


def dot_exact(form, value, table):
    high, low = split(value)
    return form(high, table) + form(low, table)


def spline_weights(fraction):
    values = [1.0 - fraction, fraction] + [jnp.zeros_like(fraction) for unused in range(4)]
    for order in range(3, 6):
        factor = 1.0 / (order - 1)
        values[order - 1] = factor * fraction * values[order - 2]
        for offset in range(1, order - 1):
            values[order - offset - 1] = factor * (
                (fraction + offset) * values[order - offset - 2]
                + (order - offset - fraction) * values[order - offset - 1]
            )
        values[0] = factor * (1.0 - fraction) * values[0]
    slopes = [-values[0]] + [values[offset - 1] - values[offset] for offset in range(1, 6)]
    factor = 1.0 / 5.0
    values[5] = factor * fraction * values[4]
    for offset in range(1, 5):
        values[5 - offset] = factor * (
            (fraction + offset) * values[4 - offset] + (6 - offset - fraction) * values[5 - offset]
        )
    values[0] = factor * (1.0 - fraction) * values[0]
    return values, slopes


def place(coefficients, dimension, offset):
    result = jnp.zeros(offset.shape, F32)
    for j in range(6):
        result = jnp.where(offset == j, coefficients[j][dimension : dimension + 1], result)
    return result


def rows_below(start, length):
    return lax.broadcasted_iota(jnp.int32, (length, start.shape[1]), 0) - start


def parameters(site_ref):
    whole = site_ref[4:7].astype(jnp.int32)
    return site_ref[0:1], site_ref[1:4], whole[0:1], whole[1:2], whole[2:3]


def z_offset_short(start, first, length):
    offset = lax.broadcasted_iota(jnp.int16, (length, start.shape[1]), 0) + jnp.int16(first) - start
    return jnp.where(offset < 0, offset + jnp.int16(M), offset)


def place_split(halved, offset):
    results = [jnp.zeros(offset.shape, BF16) for unused in range(2)]
    for j in range(6):
        here = offset == j
        results = [jnp.where(here, halved[j][i], results[i]) for i in range(2)]
    return results


def pack_kernel(
    charge_in, start_in, frac_in, influence_in, out_ref, planes_ref, charge_ref, start_ref, frac_ref, slab_ref, sems
):
    copies = [
        pltpu.make_async_copy(start_in, start_ref, sems.at[0]),
        pltpu.make_async_copy(frac_in, frac_ref, sems.at[1]),
        pltpu.make_async_copy(charge_in, charge_ref, sems.at[2]),
        pltpu.make_async_copy(influence_in.at[0:SLOTS], slab_ref, sems.at[3]),
    ]
    for copy in copies:
        copy.start()
    for copy in copies[:3]:
        copy.wait()
    out_ref[0:1] = charge_ref[...]
    out_ref[1:4] = frac_ref[...]
    out_ref[4:5] = lax.rem(start_ref[0:1], PX).astype(F32)
    out_ref[5:6] = lax.rem(start_ref[1:2], PY).astype(F32)
    out_ref[6:7] = start_ref[2:3].astype(F32)
    out_ref[7:8] = jnp.zeros(charge_ref.shape, F32)
    copies[3].wait()
    half = PY // 2
    for j in range(SLOTS):
        first = j * PLANE_ROWS
        tail = slab_ref[j, :, 2 * LANES : M]
        planes_ref[first : first + PY] = slab_ref[j, :, :LANES]
        planes_ref[first + PY : first + 2 * PY] = slab_ref[j, :, LANES : 2 * LANES]
        planes_ref[first + 2 * PY : first + 2 * PY + half] = jnp.concatenate([tail[:half], tail[half:]], axis=1)
        planes_ref[first + 2 * PY + half : first + PLANE_ROWS] = jnp.zeros((PLANE_ROWS - 2 * PY - half, LANES), F32)
    planes_ref[SLOTS * PLANE_ROWS :] = jnp.zeros(((GY - SLOTS) * PLANE_ROWS, LANES), F32)


def finish_kernel(own_ref, edge_ref, inner_ref, potential_ref, forces_ref):
    total = inner_ref[...] + edge_ref[...]
    potential_ref[...] = total[0:1]
    forces_ref[...] = -own_ref[0:1] * total[1:4]


def spread_kernel(own_ref, near_ref, front_ref, out_ref, wz_ref, plane_ref):
    sites = own_ref.shape[1]
    mesh = None
    for source in range(2):
        charge, fraction, start_x, start_y, start_z = parameters((own_ref, near_ref)[source])
        values, unused = spline_weights(fraction)
        weight_x = place(values, 0, rows_below(start_x - source * PX, 16)) * charge
        weight_y = place(values, 1, rows_below(start_y, GROUPS_Y * STEP_Y))
        for part in range(0, sites, 256):
            picked = slice(part, part + 256)
            lanes = slice(source * sites + part, source * sites + part + 256)
            halved = [split(value[2:3, picked]) for value in values]
            short_z = start_z[:, picked].astype(jnp.int16)
            for block in range(0, M, 16):
                high, low = place_split(halved, z_offset_short(short_z, block, 16))
                wz_ref[0, block : block + 16, lanes] = high
                wz_ref[1, block : block + 16, lanes] = low
            for cell in range(0, WIDE, 16):
                pair = []
                for first in (cell, cell + STEP_Y):
                    if first < CELLS:
                        g, x = first // (PX * STEP_Y), first // STEP_Y % PX
                        near = weight_y[g * STEP_Y : (g + 1) * STEP_Y, picked]
                        pair.append(near * jnp.broadcast_to(weight_x[x : x + 1, picked], near.shape))
                    else:
                        pair.append(jnp.zeros((STEP_Y, 256), F32))
                high, low = split(jnp.concatenate(pair, axis=0))
                plane_ref[0, cell : cell + 16, lanes] = high
                plane_ref[1, cell : cell + 16, lanes] = low
            for i, j in ((0, 0), (0, 1), (1, 0)):
                term = dot_nt(wz_ref[i, :, lanes], plane_ref[j, :, lanes])
                mesh = term if mesh is None else mesh + term
    waves = dot(front_ref[...], split_rows(mesh))
    span = SLOTS * GZ
    for gx in range(GX):
        first = gx * GY * GZ * CHUNK
        for part in range(2):
            rows = waves[(part * GX + gx) * span : (part * GX + gx + 1) * span]
            for r in range(HALF):
                out_ref[pl.ds(first + part * HALF + r, span, stride=CHUNK), :] = rows[:, r * LANES : (r + 1) * LANES]
        out_ref[first + span * CHUNK : first + GY * GZ * CHUNK] = jnp.zeros(((GY * GZ - span) * CHUNK, LANES), F32)


def turn(real, imag, cos, sin):
    return real * cos - imag * sin, real * sin + imag * cos


def plane_kernel(in_ref, influence_ref, mixes_ref, turns_ref, out_ref, real_ref, imag_ref, real_back_ref, imag_back_ref):
    def lanes_x_table(group):
        shift = group * PX * STEP_Y % LANES
        pieces = []
        for first in range(0, 512, LANES):
            if shift:
                pieces.append(mixes_ref[first + LANES - shift : first + LANES])
            pieces.append(mixes_ref[first : first + LANES - shift])
        table = jnp.concatenate(pieces, axis=0)
        return table[:256], table[256:]

    lanes_y_table = mixes_ref[512:768]
    first = 768
    left_x, left_xh = mixes_ref[first : first + 64, :192], mixes_ref[first + 64 : first + 128, :192]
    left_y, left_yh = mixes_ref[first + 128 : first + 208, :240], mixes_ref[first + 208 : first + 288, :240]
    cos_x, sin_x = [
        jnp.concatenate([turns_ref[(i * HALF + r) * 32 : (i * HALF + r + 1) * 32] for r in range(HALF)], axis=1)
        for i in range(2)
    ]
    cos_y, sin_y = turns_ref[256:296], turns_ref[296:336]

    def lane(value, k):
        return value[:, k * LANES : (k + 1) * LANES]

    def chunk_rows(gx, q, part, r):
        return pl.ds((gx * GY + q) * GZ * CHUNK + part * HALF + r, GZ, stride=CHUNK)

    turned = []
    for q in range(GY):
        rows = [
            jnp.concatenate([in_ref[chunk_rows(gx, q, part, r), :] for r in range(HALF)], axis=1)
            for part in range(2)
            for gx in range(GX)
        ]
        mixed = dot(left_x, split_rows(jnp.concatenate(rows, axis=0)))
        turned.append(turn(mixed[:32], mixed[32:], cos_x, sin_x))
    lanes = lax.broadcasted_iota(jnp.int32, (1, 2 * LANES), 1) % LANES

    def placed(group, rows):
        first = group * PX * STEP_Y
        row = first // LANES
        if first % LANES + PX * STEP_Y <= LANES:
            return rows[row]
        return jnp.where(lanes >= first % LANES, rows[row], rows[row + 1])

    rows = [
        jnp.concatenate([jnp.concatenate([lane(re, r), lane(im, r)], axis=1) for re, im in turned], axis=0)
        for r in range(HALF)
    ]
    groups = [
        dot_lanes(dot, placed(g, rows), *lanes_x_table(g)) for g in range(GROUPS_Y)
    ]
    spill = groups[5]
    groups[0] = groups[0] + jnp.concatenate([spill[7 * 32 :], spill[: 7 * 32]], axis=0)
    for g in range(5):
        for q in range(GY):
            first = (g * GY + q) * STRIDE
            real_ref[first : first + 32] = lane(groups[g][q * 32 : (q + 1) * 32], 0)
            imag_ref[first : first + 32] = lane(groups[g][q * 32 : (q + 1) * 32], 1)

    batch = 32
    for k in range(0, 32, batch):
        picks = [pl.ds(k + i, 40, stride=STRIDE) for i in range(batch)]
        real = jnp.concatenate([real_ref[pick, :] for pick in picks], axis=1)
        imag = jnp.concatenate([imag_ref[pick, :] for pick in picks], axis=1)
        mixed = dot(left_y, split_rows(jnp.concatenate([real, imag], axis=0)))
        turned = [
            jnp.concatenate(turn(lane(mixed[:40], i), lane(mixed[40:], i), cos_y, sin_y), axis=1)
            for i in range(batch)
        ]
        spectrum = dot_exact(dot, jnp.concatenate(turned, axis=0), lanes_y_table)
        influence = influence_ref[k * 40 : (k + batch) * 40]
        spectrum = spectrum * jnp.concatenate([influence, influence], axis=1)
        back = dot_exact(dot_nt, spectrum, lanes_y_table)
        pieces = [
            turn(lane(back[i * 40 : (i + 1) * 40], 0), lane(back[i * 40 : (i + 1) * 40], 1), cos_y, -sin_y)
            for i in range(batch)
        ]
        stacked = jnp.concatenate(
            [jnp.concatenate([piece[part] for piece in pieces], axis=1) for part in range(2)], axis=0
        )
        inverse = dot(left_yh, split_rows(stacked))
        for i in range(batch):
            real_back_ref[picks[i], :] = lane(inverse[:40], i)
            imag_back_ref[picks[i], :] = lane(inverse[40:], i)

    groups = [
        jnp.concatenate(
            [
                jnp.concatenate(
                    [ref[(g * GY + q) * STRIDE : (g * GY + q) * STRIDE + 32] for q in range(GY)], axis=0
                )
                for ref in (real_back_ref, imag_back_ref)
            ],
            axis=1,
        )
        for g in range(5)
    ]
    groups.append(jnp.concatenate([groups[0][32:], groups[0][:32]], axis=0))
    pieces = [None] * HALF
    for g in range(GROUPS_Y):
        back = dot_lanes(dot_nt, groups[g], *lanes_x_table(g))
        first = g * PX * STEP_Y
        row = first // LANES
        pieces[row] = back if pieces[row] is None else jnp.where(lanes >= first % LANES, back, pieces[row])
        if first % LANES + PX * STEP_Y > LANES:
            pieces[row + 1] = back
    for q in range(GY):
        picked = [back[q * 32 : (q + 1) * 32] for back in pieces]
        real = jnp.concatenate([lane(back, 0) for back in picked], axis=1)
        imag = jnp.concatenate([lane(back, 1) for back in picked], axis=1)
        stacked = jnp.concatenate(turn(real, imag, cos_x, -sin_x), axis=0)
        inverse = dot(left_xh, split_rows(stacked))
        for part in range(2):
            for gx in range(GX):
                tile = inverse[(part * GX + gx) * GZ : (part * GX + gx + 1) * GZ]
                for r in range(HALF):
                    out_ref[chunk_rows(gx, q, part, r), :] = lane(tile, r)


def gather_sites(site_ref, shift, columns, mesh, wz_ref, finish):
    sites = site_ref.shape[1]
    unused, fraction, start_x, start_y, start_z = parameters(site_ref)
    values, slopes = spline_weights(fraction)
    offset_x = rows_below(start_x - shift, 16)
    offset_y = rows_below(start_y, GROUPS_Y * STEP_Y)
    weight_x, slope_x = place(values, 0, offset_x), place(slopes, 0, offset_x)
    weight_y, slope_y = place(values, 1, offset_y), place(slopes, 1, offset_y)
    short_z = start_z.astype(jnp.int16)
    halved = [[split(value[2:3]) for value in coefficients] for coefficients in (values, slopes)]
    for block in range(0, M, 16):
        offset = z_offset_short(short_z, block, 16)
        for kind in range(2):
            high, low = place_split(halved[kind], offset)
            for term, part in enumerate((high, high, low)):
                row = term * 256 + block if block < 256 else 768 + term * 64 + block - 256
                wz_ref[kind, row : row + 16] = part
    for kind in range(2):
        wz_ref[kind, 960:DEEP] = jnp.zeros((64, sites), BF16)
    width = 256
    for first in range(0, sites, width):
        lanes = slice(first, first + width)
        near = dot(mesh, wz_ref[0, :, lanes])
        near_slope = dot(mesh, wz_ref[1, :, lanes])
        sums = [jnp.zeros((STEP_Y, width), F32) for unused in range(4)]
        for g in range(GROUPS_Y):
            wy = weight_y[g * STEP_Y : (g + 1) * STEP_Y, lanes]
            sy = slope_y[g * STEP_Y : (g + 1) * STEP_Y, lanes]
            for x in range(columns):
                row = (g * columns + x) * STEP_Y
                value = near[row : row + STEP_Y]
                weighted = wy * value
                wx = weight_x[x : x + 1, lanes]
                sums[0] = sums[0] + wx * weighted
                sums[1] = sums[1] + slope_x[x : x + 1, lanes] * weighted
                sums[2] = sums[2] + wx * (sy * value)
                sums[3] = sums[3] + wx * (wy * near_slope[row : row + STEP_Y])
        finish(lanes, [jnp.sum(part, axis=0, keepdims=True) for part in sums])


def deep_lanes(mesh):
    high, low = split(mesh)
    tail = jnp.concatenate([high[:, 256:M], low[:, 256:M], high[:, 256:M], jnp.zeros((mesh.shape[0], 64), BF16)], axis=1)
    return jnp.concatenate([high[:, :256], low[:, :256], high[:, :256], tail], axis=1)


def near_kernel(in_ref, near_ref, back_ref, mesh_ref, part_ref, wz_ref):
    span = SLOTS * GZ
    rows = [
        jnp.concatenate(
            [in_ref[pl.ds(gx * GY * GZ * CHUNK + part * HALF + r, span, stride=CHUNK), :] for r in range(HALF)],
            axis=1,
        )
        for part in range(2)
        for gx in range(GX)
    ]
    mesh = dot(back_ref[...], split_rows(jnp.concatenate(rows, axis=0)))
    mesh = jnp.transpose(mesh)[:CELLS]
    mesh_ref[...] = deep_lanes(mesh)
    edge = [mesh[g * PX * STEP_Y : g * PX * STEP_Y + 5 * STEP_Y] for g in range(GROUPS_Y)]
    edge = deep_lanes(jnp.concatenate(edge, axis=0))

    def finish(lanes, totals):
        for i in range(4):
            part_ref[i : i + 1, lanes] = totals[i]

    gather_sites(near_ref, PX, 5, edge, wz_ref, finish)


def own_kernel(mesh_ref, own_ref, part_ref, wz_ref):
    def finish(lanes, totals):
        for i in range(4):
            part_ref[i : i + 1, lanes] = totals[i]

    gather_sites(own_ref, 0, PX, mesh_ref[...], wz_ref, finish)


PLANE_SCRATCH = [pltpu.VMEM((40 * STRIDE, LANES), F32) for unused in range(4)]
LIMIT = pltpu.CompilerParams(vmem_limit_bytes=24 * 1024 * 1024)


def exchange(chunks):
    flat = chunks.reshape(GX * GY * GZ, 1, CHUNK * LANES)
    return lax.all_to_all(flat, ("gx", "gy", "gz"), 0, 0, tiled=True).reshape(ROWS, LANES)


def influence_along_x(planes):
    groups = [[2 * x + half for x in range(4)] for half in range(2)]
    flat = planes.reshape(GY // 2, 1, 2 * PLANE_ROWS * LANES)
    planes = lax.all_to_all(flat, "gy", 0, 0, tiled=True, axis_index_groups=groups)
    return planes.reshape(GY // 2, 2, PLANE_ROWS, LANES)


def widen_kernel(in_ref, out_ref):
    out_ref[:, :80] = in_ref[...]
    out_ref[:, 80:] = jnp.zeros((1280, LANES - 80), F32)


def influence_layout(planes):
    half = lax.axis_index("gy") % 2
    kept = lax.dynamic_index_in_dim(planes, half, 1, keepdims=False)
    sent = lax.dynamic_index_in_dim(planes, 1 - half, 1, keepdims=False)
    other = lax.ppermute(sent, "gy", [(s, s ^ 1) for s in range(SLOTS)])
    pair = [jnp.where(half == 0, kept, other), jnp.where(half == 0, other, kept)]
    planes = jnp.stack(pair, axis=1).reshape(GY, PLANE_ROWS, LANES)
    tail = planes[:, 2 * PY : 2 * PY + PY // 2]
    tail = jnp.concatenate([tail[:, :, : LANES // 2], tail[:, :, LANES // 2 :]], axis=1)
    planes = jnp.concatenate([planes[:, :PY], planes[:, PY : 2 * PY], tail], axis=2)
    planes = planes.reshape(10, 32, 8, 40).transpose(1, 3, 0, 2).reshape(1280, 80)
    return pl.pallas_call(
        widen_kernel,
        out_shape=jax.ShapeDtypeStruct((1280, LANES), F32),
        compiler_params=LIMIT,
        cost_estimate=pl.CostEstimate(flops=100000000000, bytes_accessed=1000000, transcendentals=0),
        name="widen",
    )(planes)


def body(charges, mesh_start, mesh_frac, influence):
    table = {name: jnp.asarray(value) for name, value in tables().items()}
    sites = charges.shape[0]
    own, planes = pl.pallas_call(
        pack_kernel,
        out_shape=(
            jax.ShapeDtypeStruct((8, sites), F32),
            jax.ShapeDtypeStruct((GY * PLANE_ROWS, LANES), F32),
        ),
        in_specs=[pl.BlockSpec(memory_space=pl.ANY)] * 4,
        scratch_shapes=[
            pltpu.VMEM((1, sites), F32),
            pltpu.VMEM((3, sites), jnp.int32),
            pltpu.VMEM((3, sites), F32),
            pltpu.VMEM((SLOTS, PY, M), F32),
            pltpu.SemaphoreType.DMA((4,)),
        ],
        compiler_params=pltpu.CompilerParams(vmem_limit_bytes=60 * 1024 * 1024),
        name="pack",
    )(charges.reshape(1, sites), mesh_start, mesh_frac, influence)
    near = lax.ppermute(own, ("gx", "gz"), [(p, (p + 1) % PENCILS) for p in range(PENCILS)])
    planes = influence_along_x(planes)
    chunks = pl.pallas_call(
        spread_kernel,
        out_shape=jax.ShapeDtypeStruct((ROWS, LANES), F32),
        scratch_shapes=[pltpu.VMEM((2, M, 2 * sites), BF16), pltpu.VMEM((2, WIDE, 2 * sites), BF16)],
        compiler_params=LIMIT,
        cost_estimate=pl.CostEstimate(flops=40000000000, bytes_accessed=10000000, transcendentals=0),
        name="spread",
    )(own, near, table["front"])
    planes, chunks = lax.optimization_barrier((planes, chunks))
    planes = influence_layout(planes)
    chunks = exchange(chunks)
    chunks = pl.pallas_call(
        plane_kernel,
        out_shape=jax.ShapeDtypeStruct((ROWS, LANES), F32),
        scratch_shapes=PLANE_SCRATCH,
        compiler_params=LIMIT,
        name="plane",
    )(
        chunks,
        planes,
        table["mixes"],
        table["turns"],
    )
    chunks = exchange(chunks)
    mesh, edge = pl.pallas_call(
        near_kernel,
        out_shape=(jax.ShapeDtypeStruct((CELLS, DEEP), BF16), jax.ShapeDtypeStruct((4, sites), F32)),
        scratch_shapes=[pltpu.VMEM((2, DEEP, sites), BF16)],
        compiler_params=LIMIT,
        name="near",
    )(chunks, near, table["back"])
    edge = lax.ppermute(edge, ("gx", "gz"), [(p, (p - 1) % PENCILS) for p in range(PENCILS)])
    inner = pl.pallas_call(
        own_kernel,
        out_shape=jax.ShapeDtypeStruct((4, sites), F32),
        scratch_shapes=[pltpu.VMEM((2, DEEP, sites), BF16)],
        compiler_params=LIMIT,
        name="own",
    )(mesh, own)
    potential, forces = pl.pallas_call(
        finish_kernel,
        out_shape=(jax.ShapeDtypeStruct((1, sites), F32), jax.ShapeDtypeStruct((3, sites), F32)),
        compiler_params=LIMIT,
        name="finish",
    )(own, edge, inner)
    return potential.reshape(sites), forces


def solution(mesh):
    return jax.shard_map(
        body,
        mesh=mesh,
        in_specs=(
            P(("gx", "gy", "gz")),
            P(None, ("gx", "gy", "gz")),
            P(None, ("gx", "gy", "gz")),
            P(("gx", "gz"), "gy", None),
        ),
        out_specs=(P(("gx", "gy", "gz")), P(None, ("gx", "gy", "gz"))),
        check_vma=False,
    )
```

```python
import functools
import math

import jax
import jax.numpy as jnp
import ml_dtypes
import numpy as np
from jax import lax
from jax.experimental import pallas as pl
from jax.experimental.pallas import tpu as pltpu
from jax.sharding import PartitionSpec as P

M = 320
PX = 10
PY = 40
GX, GY, GZ = 4, 8, 8
PENCILS = GX * GZ
SLOTS = 6
CHUNK = 8
HALF = CHUNK // 2
ROWS = GX * GY * GZ * CHUNK
GROUPS_Y = 6
STEP_Y = 8
LANES = 128
WIDE = HALF * LANES
CELLS = GROUPS_Y * PX * STEP_Y
DEEP = 1024
STRIDE = 40
PLANE_ROWS = 104
SCALE_Y = 239.0
BF16 = jnp.bfloat16
F32 = jnp.float32
NT = (((1,), (1,)), ((), ()))


def halves(table):
    high = table.astype(ml_dtypes.bfloat16)
    low = (table - high.astype(np.float64)).astype(ml_dtypes.bfloat16)
    return high, low


def left_table(table):
    high, low = halves(table)
    return np.concatenate([high, high, low], axis=1)


def angles(rows, columns, period):
    phase = np.mod(np.outer(rows, columns), period)
    return phase * (2.0 * math.pi / period)


def complex_left(angle):
    c, s = np.cos(angle), np.sin(angle)
    return np.block([[c, s], [-s, c]])


def lanes_complex(angle, live):
    c, s = np.cos(angle) * live, np.sin(angle) * live
    return np.block([[c, -s], [s, c]])


def lanes_x_table():
    slot = np.arange(LANES) // STEP_Y
    y = np.arange(LANES) % STEP_Y
    live = (slot < PX)[:, None] & (y[:, None] == y[None, :]) & (slot < 10)[None, :]
    return lanes_complex(angles(slot, slot, 10), live)


def lanes_y_table():
    lane = np.arange(LANES)
    live = (lane[:, None] // 8 == lane[None, :] // 8) & (lane < 80)[:, None]
    return lanes_complex(angles(lane % 8, lane % 8, 8), live)


def wave_slots():
    waves = np.zeros((GX, SLOTS, GZ), np.int64)
    fold = np.zeros((GX, SLOTS, GZ))
    for gx in range(GX):
        for gz in range(GZ):
            p = gx * GZ + gz
            upper = p >= PENCILS // 2
            for j in range(SLOTS):
                wave = 10 * p + j
                if (j < 5 and not upper) or (j > 0 and upper) or wave == M // 2:
                    waves[gx, j, gz] = wave
                    fold[gx, j, gz] = 1.0 if wave in (0, M // 2) else 2.0
    return waves.reshape(-1), fold.reshape(-1)


@functools.lru_cache(maxsize=None)
def tables():
    waves, fold = wave_slots()
    angle = angles(waves, np.arange(M), M)
    live = (fold > 0)[:, None]
    front = np.concatenate([np.cos(angle) * live, -np.sin(angle) * live])
    scale = fold[:, None] / (float(M * M * M) * SCALE_Y**2)
    back = np.concatenate([np.cos(angle) * scale, -np.sin(angle) * scale]).T
    back = np.pad(back, [(0, 384 - M), (0, 0)])
    left_x = complex_left(angles(np.arange(32), np.arange(32), 32))
    order = np.concatenate([5 * np.arange(GY) + g for g in range(5)])
    left_y = complex_left(angles(np.arange(40), order, 40))
    lanes_x = lanes_x_table()
    lanes_y = lanes_y_table()
    lane = np.arange(LANES)
    turn_x = angles(np.arange(32), np.arange(WIDE) // STEP_Y % PX, M)
    turn_y = angles(np.arange(40), lane % 8, M)
    parts = [part for table in (lanes_x,) for part in halves(table)]
    parts.append(np.round(SCALE_Y * lanes_y).astype(ml_dtypes.bfloat16))
    for table in (left_x, left_x.T, left_y, left_y.T):
        left = left_table(table)
        parts.append(np.pad(left, [(0, 0), (0, 256 - left.shape[1])]))
    turns = [np.cos(turn_x), -np.sin(turn_x), np.cos(turn_y), -np.sin(turn_y)]
    turns = [part[:, i : i + LANES] for part in turns for i in range(0, part.shape[1], LANES)]
    return dict(
        front=left_table(front),
        back=left_table(back),
        mixes=np.concatenate(parts, axis=0),
        turns=np.concatenate(turns, axis=0).astype(np.float32),
    )


def split(value):
    high = value.astype(BF16)
    low = (value - high.astype(F32)).astype(BF16)
    return high, low


def split_rows(value):
    high, low = split(value)
    return jnp.concatenate([high, low, high], axis=0)


def split_lanes(value):
    high, low = split(value)
    return jnp.concatenate([high, low, high], axis=1)


def dot(left, right):
    return jnp.dot(left, right, preferred_element_type=F32)


def dot_nt(left, right):
    return lax.dot_general(left, right, NT, preferred_element_type=F32)


def dot_lanes(form, value, high_table, low_table):
    high, low = split(value)
    return form(high, high_table) + form(low, high_table) + form(high, low_table)


def dot_exact(form, value, table):
    high, low = split(value)
    return form(high, table) + form(low, table)


def spline_weights(fraction):
    values = [1.0 - fraction, fraction] + [jnp.zeros_like(fraction) for unused in range(4)]
    for order in range(3, 6):
        factor = 1.0 / (order - 1)
        values[order - 1] = factor * fraction * values[order - 2]
        for offset in range(1, order - 1):
            values[order - offset - 1] = factor * (
                (fraction + offset) * values[order - offset - 2]
                + (order - offset - fraction) * values[order - offset - 1]
            )
        values[0] = factor * (1.0 - fraction) * values[0]
    slopes = [-values[0]] + [values[offset - 1] - values[offset] for offset in range(1, 6)]
    factor = 1.0 / 5.0
    values[5] = factor * fraction * values[4]
    for offset in range(1, 5):
        values[5 - offset] = factor * (
            (fraction + offset) * values[4 - offset] + (6 - offset - fraction) * values[5 - offset]
        )
    values[0] = factor * (1.0 - fraction) * values[0]
    return values, slopes


def place(coefficients, dimension, offset):
    result = jnp.zeros(offset.shape, F32)
    for j in range(6):
        result = jnp.where(offset == j, coefficients[j][dimension : dimension + 1], result)
    return result


def rows_below(start, length):
    return lax.broadcasted_iota(jnp.int32, (length, start.shape[1]), 0) - start


def parameters(site_ref):
    whole = site_ref[4:7].astype(jnp.int32)
    return site_ref[0:1], site_ref[1:4], whole[0:1], whole[1:2], whole[2:3]


def z_offset_short(start, first, length):
    offset = lax.broadcasted_iota(jnp.int16, (length, start.shape[1]), 0) + jnp.int16(first) - start
    return jnp.where(offset < 0, offset + jnp.int16(M), offset)


def place_split(halved, offset):
    results = [jnp.zeros(offset.shape, BF16) for unused in range(2)]
    for j in range(6):
        here = offset == j
        results = [jnp.where(here, halved[j][i], results[i]) for i in range(2)]
    return results


def pack_kernel(
    charge_in, start_in, frac_in, influence_in, out_ref, planes_ref, charge_ref, start_ref, frac_ref, slab_ref, sems
):
    copies = [
        pltpu.make_async_copy(start_in, start_ref, sems.at[0]),
        pltpu.make_async_copy(frac_in, frac_ref, sems.at[1]),
        pltpu.make_async_copy(charge_in, charge_ref, sems.at[2]),
        pltpu.make_async_copy(influence_in.at[0:SLOTS], slab_ref, sems.at[3]),
    ]
    for copy in copies:
        copy.start()
    for copy in copies[:3]:
        copy.wait()
    out_ref[0:1] = charge_ref[...]
    out_ref[1:4] = frac_ref[...]
    out_ref[4:5] = lax.rem(start_ref[0:1], PX).astype(F32)
    out_ref[5:6] = lax.rem(start_ref[1:2], PY).astype(F32)
    out_ref[6:7] = start_ref[2:3].astype(F32)
    out_ref[7:8] = jnp.zeros(charge_ref.shape, F32)
    copies[3].wait()
    half = PY // 2
    for j in range(SLOTS):
        first = j * PLANE_ROWS
        tail = slab_ref[j, :, 2 * LANES : M]
        planes_ref[first : first + PY] = slab_ref[j, :, :LANES]
        planes_ref[first + PY : first + 2 * PY] = slab_ref[j, :, LANES : 2 * LANES]
        planes_ref[first + 2 * PY : first + 2 * PY + half] = jnp.concatenate([tail[:half], tail[half:]], axis=1)
        planes_ref[first + 2 * PY + half : first + PLANE_ROWS] = jnp.zeros((PLANE_ROWS - 2 * PY - half, LANES), F32)
    planes_ref[SLOTS * PLANE_ROWS :] = jnp.zeros(((GY - SLOTS) * PLANE_ROWS, LANES), F32)


def finish_kernel(own_ref, edge_ref, inner_ref, potential_ref, forces_ref):
    total = inner_ref[...] + edge_ref[...]
    potential_ref[...] = total[0:1]
    forces_ref[...] = -own_ref[0:1] * total[1:4]


def spread_kernel(own_ref, near_ref, front_ref, out_ref, wz_ref, plane_ref):
    sites = own_ref.shape[1]
    mesh = None
    for source in range(2):
        charge, fraction, start_x, start_y, start_z = parameters((own_ref, near_ref)[source])
        values, unused = spline_weights(fraction)
        weight_x = place(values, 0, rows_below(start_x - source * PX, 16)) * charge
        weight_y = place(values, 1, rows_below(start_y, GROUPS_Y * STEP_Y))
        for part in range(0, sites, 256):
            picked = slice(part, part + 256)
            lanes = slice(source * sites + part, source * sites + part + 256)
            halved = [split(value[2:3, picked]) for value in values]
            short_z = start_z[:, picked].astype(jnp.int16)
            for block in range(0, M, 16):
                high, low = place_split(halved, z_offset_short(short_z, block, 16))
                wz_ref[0, block : block + 16, lanes] = high
                wz_ref[1, block : block + 16, lanes] = low
            for cell in range(0, WIDE, 16):
                pair = []
                for first in (cell, cell + STEP_Y):
                    if first < CELLS:
                        g, x = first // (PX * STEP_Y), first // STEP_Y % PX
                        near = weight_y[g * STEP_Y : (g + 1) * STEP_Y, picked]
                        pair.append(near * jnp.broadcast_to(weight_x[x : x + 1, picked], near.shape))
                    else:
                        pair.append(jnp.zeros((STEP_Y, 256), F32))
                high, low = split(jnp.concatenate(pair, axis=0))
                plane_ref[0, cell : cell + 16, lanes] = high
                plane_ref[1, cell : cell + 16, lanes] = low
            for i, j in ((0, 0), (0, 1), (1, 0)):
                term = dot_nt(wz_ref[i, :, lanes], plane_ref[j, :, lanes])
                mesh = term if mesh is None else mesh + term
    waves = dot(front_ref[...], split_rows(mesh))
    span = SLOTS * GZ
    for gx in range(GX):
        first = gx * GY * GZ * CHUNK
        for part in range(2):
            rows = waves[(part * GX + gx) * span : (part * GX + gx + 1) * span]
            for r in range(HALF):
                out_ref[pl.ds(first + part * HALF + r, span, stride=CHUNK), :] = rows[:, r * LANES : (r + 1) * LANES]
        out_ref[first + span * CHUNK : first + GY * GZ * CHUNK] = jnp.zeros(((GY * GZ - span) * CHUNK, LANES), F32)


def turn(real, imag, cos, sin):
    return real * cos - imag * sin, real * sin + imag * cos


def plane_kernel(in_ref, influence_ref, mixes_ref, turns_ref, out_ref, real_ref, imag_ref, real_back_ref, imag_back_ref):
    def lanes_x_table(group):
        shift = group * PX * STEP_Y % LANES
        pieces = []
        for first in range(0, 512, LANES):
            if shift:
                pieces.append(mixes_ref[first + LANES - shift : first + LANES])
            pieces.append(mixes_ref[first : first + LANES - shift])
        table = jnp.concatenate(pieces, axis=0)
        return table[:256], table[256:]

    lanes_y_table = mixes_ref[512:768]
    first = 768
    left_x, left_xh = mixes_ref[first : first + 64, :192], mixes_ref[first + 64 : first + 128, :192]
    left_y, left_yh = mixes_ref[first + 128 : first + 208, :240], mixes_ref[first + 208 : first + 288, :240]
    cos_x, sin_x = [
        jnp.concatenate([turns_ref[(i * HALF + r) * 32 : (i * HALF + r + 1) * 32] for r in range(HALF)], axis=1)
        for i in range(2)
    ]
    cos_y, sin_y = turns_ref[256:296], turns_ref[296:336]

    def lane(value, k):
        return value[:, k * LANES : (k + 1) * LANES]

    def chunk_rows(gx, q, part, r):
        return pl.ds((gx * GY + q) * GZ * CHUNK + part * HALF + r, GZ, stride=CHUNK)

    turned = []
    for q in range(GY):
        rows = [
            jnp.concatenate([in_ref[chunk_rows(gx, q, part, r), :] for r in range(HALF)], axis=1)
            for part in range(2)
            for gx in range(GX)
        ]
        mixed = dot(left_x, split_rows(jnp.concatenate(rows, axis=0)))
        turned.append(turn(mixed[:32], mixed[32:], cos_x, sin_x))
    lanes = lax.broadcasted_iota(jnp.int32, (1, 2 * LANES), 1) % LANES

    def placed(group, rows):
        first = group * PX * STEP_Y
        row = first // LANES
        if first % LANES + PX * STEP_Y <= LANES:
            return rows[row]
        return jnp.where(lanes >= first % LANES, rows[row], rows[row + 1])

    rows = [
        jnp.concatenate([jnp.concatenate([lane(re, r), lane(im, r)], axis=1) for re, im in turned], axis=0)
        for r in range(HALF)
    ]
    groups = [
        dot_lanes(dot, placed(g, rows), *lanes_x_table(g)) for g in range(GROUPS_Y)
    ]
    spill = groups[5]
    groups[0] = groups[0] + jnp.concatenate([spill[7 * 32 :], spill[: 7 * 32]], axis=0)
    for g in range(5):
        for q in range(GY):
            first = (g * GY + q) * STRIDE
            real_ref[first : first + 32] = lane(groups[g][q * 32 : (q + 1) * 32], 0)
            imag_ref[first : first + 32] = lane(groups[g][q * 32 : (q + 1) * 32], 1)

    batch = 32
    for k in range(0, 32, batch):
        picks = [pl.ds(k + i, 40, stride=STRIDE) for i in range(batch)]
        real = jnp.concatenate([real_ref[pick, :] for pick in picks], axis=1)
        imag = jnp.concatenate([imag_ref[pick, :] for pick in picks], axis=1)
        mixed = dot(left_y, split_rows(jnp.concatenate([real, imag], axis=0)))
        turned = [
            jnp.concatenate(turn(lane(mixed[:40], i), lane(mixed[40:], i), cos_y, sin_y), axis=1)
            for i in range(batch)
        ]
        spectrum = dot_exact(dot, jnp.concatenate(turned, axis=0), lanes_y_table)
        influence = influence_ref[k * 40 : (k + batch) * 40]
        spectrum = spectrum * jnp.concatenate([influence, influence], axis=1)
        back = dot_exact(dot_nt, spectrum, lanes_y_table)
        pieces = [
            turn(lane(back[i * 40 : (i + 1) * 40], 0), lane(back[i * 40 : (i + 1) * 40], 1), cos_y, -sin_y)
            for i in range(batch)
        ]
        stacked = jnp.concatenate(
            [jnp.concatenate([piece[part] for piece in pieces], axis=1) for part in range(2)], axis=0
        )
        inverse = dot(left_yh, split_rows(stacked))
        for i in range(batch):
            real_back_ref[picks[i], :] = lane(inverse[:40], i)
            imag_back_ref[picks[i], :] = lane(inverse[40:], i)

    groups = [
        jnp.concatenate(
            [
                jnp.concatenate(
                    [ref[(g * GY + q) * STRIDE : (g * GY + q) * STRIDE + 32] for q in range(GY)], axis=0
                )
                for ref in (real_back_ref, imag_back_ref)
            ],
            axis=1,
        )
        for g in range(5)
    ]
    groups.append(jnp.concatenate([groups[0][32:], groups[0][:32]], axis=0))
    pieces = [None] * HALF
    for g in range(GROUPS_Y):
        back = dot_lanes(dot_nt, groups[g], *lanes_x_table(g))
        first = g * PX * STEP_Y
        row = first // LANES
        pieces[row] = back if pieces[row] is None else jnp.where(lanes >= first % LANES, back, pieces[row])
        if first % LANES + PX * STEP_Y > LANES:
            pieces[row + 1] = back
    for q in range(GY):
        picked = [back[q * 32 : (q + 1) * 32] for back in pieces]
        real = jnp.concatenate([lane(back, 0) for back in picked], axis=1)
        imag = jnp.concatenate([lane(back, 1) for back in picked], axis=1)
        stacked = jnp.concatenate(turn(real, imag, cos_x, -sin_x), axis=0)
        inverse = dot(left_xh, split_rows(stacked))
        for part in range(2):
            for gx in range(GX):
                tile = inverse[(part * GX + gx) * GZ : (part * GX + gx + 1) * GZ]
                for r in range(HALF):
                    out_ref[chunk_rows(gx, q, part, r), :] = lane(tile, r)


def gather_sites(site_ref, shift, columns, mesh, wz_ref, finish):
    sites = site_ref.shape[1]
    unused, fraction, start_x, start_y, start_z = parameters(site_ref)
    values, slopes = spline_weights(fraction)
    offset_x = rows_below(start_x - shift, 16)
    offset_y = rows_below(start_y, GROUPS_Y * STEP_Y)
    weight_x, slope_x = place(values, 0, offset_x), place(slopes, 0, offset_x)
    weight_y, slope_y = place(values, 1, offset_y), place(slopes, 1, offset_y)
    short_z = start_z.astype(jnp.int16)
    halved = [[split(value[2:3]) for value in coefficients] for coefficients in (values, slopes)]
    for block in range(0, M, 16):
        offset = z_offset_short(short_z, block, 16)
        for kind in range(2):
            high, low = place_split(halved[kind], offset)
            for term, part in enumerate((high, high, low)):
                row = term * 256 + block if block < 256 else 768 + term * 64 + block - 256
                wz_ref[kind, row : row + 16] = part
    for kind in range(2):
        wz_ref[kind, 960:DEEP] = jnp.zeros((64, sites), BF16)
    width = 256
    for first in range(0, sites, width):
        lanes = slice(first, first + width)
        near = dot(mesh, wz_ref[0, :, lanes])
        near_slope = dot(mesh, wz_ref[1, :, lanes])
        sums = [jnp.zeros((STEP_Y, width), F32) for unused in range(4)]
        for g in range(GROUPS_Y):
            wy = weight_y[g * STEP_Y : (g + 1) * STEP_Y, lanes]
            sy = slope_y[g * STEP_Y : (g + 1) * STEP_Y, lanes]
            for x in range(columns):
                row = (g * columns + x) * STEP_Y
                value = near[row : row + STEP_Y]
                weight, slope = weight_x[x : x + 1, lanes], slope_x[x : x + 1, lanes]
                terms = [weight * value, slope * value, weight * near_slope[row : row + STEP_Y]]
                along = terms if x == 0 else [total + term for total, term in zip(along, terms)]
            sums[0] = sums[0] + wy * along[0]
            sums[1] = sums[1] + wy * along[1]
            sums[2] = sums[2] + sy * along[0]
            sums[3] = sums[3] + wy * along[2]
        finish(lanes, [jnp.sum(part, axis=0, keepdims=True) for part in sums])


def deep_lanes(mesh):
    high, low = split(mesh)
    tail = jnp.concatenate([high[:, 256:M], low[:, 256:M], high[:, 256:M], jnp.zeros((mesh.shape[0], 64), BF16)], axis=1)
    return jnp.concatenate([high[:, :256], low[:, :256], high[:, :256], tail], axis=1)


def near_kernel(in_ref, near_ref, back_ref, mesh_ref, part_ref, wz_ref):
    span = SLOTS * GZ
    rows = [
        jnp.concatenate(
            [in_ref[pl.ds(gx * GY * GZ * CHUNK + part * HALF + r, span, stride=CHUNK), :] for r in range(HALF)],
            axis=1,
        )
        for part in range(2)
        for gx in range(GX)
    ]
    mesh = dot(back_ref[...], split_rows(jnp.concatenate(rows, axis=0)))
    mesh = jnp.transpose(mesh)[:CELLS]
    mesh_ref[...] = deep_lanes(mesh)
    edge = [mesh[g * PX * STEP_Y : g * PX * STEP_Y + 5 * STEP_Y] for g in range(GROUPS_Y)]
    edge = deep_lanes(jnp.concatenate(edge, axis=0))

    def finish(lanes, totals):
        for i in range(4):
            part_ref[i : i + 1, lanes] = totals[i]

    gather_sites(near_ref, PX, 5, edge, wz_ref, finish)


def own_kernel(mesh_ref, own_ref, part_ref, wz_ref):
    def finish(lanes, totals):
        for i in range(4):
            part_ref[i : i + 1, lanes] = totals[i]

    gather_sites(own_ref, 0, PX, mesh_ref[...], wz_ref, finish)


PLANE_SCRATCH = [pltpu.VMEM((40 * STRIDE, LANES), F32) for unused in range(4)]
LIMIT = pltpu.CompilerParams(vmem_limit_bytes=24 * 1024 * 1024)


def exchange(chunks):
    flat = chunks.reshape(GX * GY * GZ, 1, CHUNK * LANES)
    return lax.all_to_all(flat, ("gx", "gy", "gz"), 0, 0, tiled=True).reshape(ROWS, LANES)


def influence_along_x(planes):
    groups = [[2 * x + half for x in range(4)] for half in range(2)]
    flat = planes.reshape(GY // 2, 1, 2 * PLANE_ROWS * LANES)
    planes = lax.all_to_all(flat, "gy", 0, 0, tiled=True, axis_index_groups=groups)
    return planes.reshape(GY // 2, 2, PLANE_ROWS, LANES)


def widen_kernel(in_ref, out_ref):
    out_ref[:, :80] = in_ref[...]
    out_ref[:, 80:] = jnp.zeros((1280, LANES - 80), F32)


def influence_layout(planes):
    half = lax.axis_index("gy") % 2
    kept = lax.dynamic_index_in_dim(planes, half, 1, keepdims=False)
    sent = lax.dynamic_index_in_dim(planes, 1 - half, 1, keepdims=False)
    other = lax.ppermute(sent, "gy", [(s, s ^ 1) for s in range(SLOTS)])
    pair = [jnp.where(half == 0, kept, other), jnp.where(half == 0, other, kept)]
    planes = jnp.stack(pair, axis=1).reshape(GY, PLANE_ROWS, LANES)
    tail = planes[:, 2 * PY : 2 * PY + PY // 2]
    tail = jnp.concatenate([tail[:, :, : LANES // 2], tail[:, :, LANES // 2 :]], axis=1)
    planes = jnp.concatenate([planes[:, :PY], planes[:, PY : 2 * PY], tail], axis=2)
    planes = planes.reshape(10, 32, 8, 40).transpose(1, 3, 0, 2).reshape(1280, 80)
    return pl.pallas_call(
        widen_kernel,
        out_shape=jax.ShapeDtypeStruct((1280, LANES), F32),
        compiler_params=LIMIT,
        cost_estimate=pl.CostEstimate(flops=100000000000, bytes_accessed=1000000, transcendentals=0),
        name="widen",
    )(planes)


def body(charges, mesh_start, mesh_frac, influence):
    table = {name: jnp.asarray(value) for name, value in tables().items()}
    sites = charges.shape[0]
    own, planes = pl.pallas_call(
        pack_kernel,
        out_shape=(
            jax.ShapeDtypeStruct((8, sites), F32),
            jax.ShapeDtypeStruct((GY * PLANE_ROWS, LANES), F32),
        ),
        in_specs=[pl.BlockSpec(memory_space=pl.ANY)] * 4,
        scratch_shapes=[
            pltpu.VMEM((1, sites), F32),
            pltpu.VMEM((3, sites), jnp.int32),
            pltpu.VMEM((3, sites), F32),
            pltpu.VMEM((SLOTS, PY, M), F32),
            pltpu.SemaphoreType.DMA((4,)),
        ],
        compiler_params=pltpu.CompilerParams(vmem_limit_bytes=60 * 1024 * 1024),
        name="pack",
    )(charges.reshape(1, sites), mesh_start, mesh_frac, influence)
    near = lax.ppermute(own, ("gx", "gz"), [(p, (p + 1) % PENCILS) for p in range(PENCILS)])
    planes = influence_along_x(planes)
    chunks = pl.pallas_call(
        spread_kernel,
        out_shape=jax.ShapeDtypeStruct((ROWS, LANES), F32),
        scratch_shapes=[pltpu.VMEM((2, M, 2 * sites), BF16), pltpu.VMEM((2, WIDE, 2 * sites), BF16)],
        compiler_params=LIMIT,
        cost_estimate=pl.CostEstimate(flops=40000000000, bytes_accessed=10000000, transcendentals=0),
        name="spread",
    )(own, near, table["front"])
    planes, chunks = lax.optimization_barrier((planes, chunks))
    planes = influence_layout(planes)
    chunks = exchange(chunks)
    chunks = pl.pallas_call(
        plane_kernel,
        out_shape=jax.ShapeDtypeStruct((ROWS, LANES), F32),
        scratch_shapes=PLANE_SCRATCH,
        compiler_params=LIMIT,
        name="plane",
    )(
        chunks,
        planes,
        table["mixes"],
        table["turns"],
    )
    chunks = exchange(chunks)
    mesh, edge = pl.pallas_call(
        near_kernel,
        out_shape=(jax.ShapeDtypeStruct((CELLS, DEEP), BF16), jax.ShapeDtypeStruct((4, sites), F32)),
        scratch_shapes=[pltpu.VMEM((2, DEEP, sites), BF16)],
        compiler_params=LIMIT,
        name="near",
    )(chunks, near, table["back"])
    edge = lax.ppermute(edge, ("gx", "gz"), [(p, (p - 1) % PENCILS) for p in range(PENCILS)])
    inner = pl.pallas_call(
        own_kernel,
        out_shape=jax.ShapeDtypeStruct((4, sites), F32),
        scratch_shapes=[pltpu.VMEM((2, DEEP, sites), BF16)],
        compiler_params=LIMIT,
        name="own",
    )(mesh, own)
    potential, forces = pl.pallas_call(
        finish_kernel,
        out_shape=(jax.ShapeDtypeStruct((1, sites), F32), jax.ShapeDtypeStruct((3, sites), F32)),
        compiler_params=LIMIT,
        name="finish",
    )(own, edge, inner)
    return potential.reshape(sites), forces


def solution(mesh):
    return jax.shard_map(
        body,
        mesh=mesh,
        in_specs=(
            P(("gx", "gy", "gz")),
            P(None, ("gx", "gy", "gz")),
            P(None, ("gx", "gy", "gz")),
            P(("gx", "gz"), "gy", None),
        ),
        out_specs=(P(("gx", "gy", "gz")), P(None, ("gx", "gy", "gz"))),
        check_vma=False,
    )
```
